32 devices in a mesh: clip: 8 (over z, y), row: 4 (over x, core).
Axes of the slice: x: 2, y: 2, z: 4, core: 2. Of those that a mesh axis runs over, the one named last changes fastest.
Arguments:
- frames: bfloat16 [8, 12, 3, 256, 256], P('clip', None, None, 'row'), may hold values from -6 to 6
- frame_start: int32 [8, 8], P('clip'), may hold values from 0 to 7
- boundary_mask: int32 [8, 8], P('clip'), may hold values from 0 to 1, as said below
- stem_weight: bfloat16 [64, 735], P('clip'), may hold values from -0.21875 to 0.21875
- stem_gain: float32 [64], replicated, may hold values from 0.5 to 1.5
- stem_bias: float32 [64], replicated, may hold values from -3 to 3
- block_input: bfloat16 [64, 8, 8, 2048], P('clip', 'row'), may hold values from -6 to 6
- w_one: bfloat16 [2048, 512], P('clip'), may hold values from -0.125 to 0.125
- w_reduce: bfloat16 [512, 128], P('clip'), may hold values from -0.25 to 0.25
- k_fine: bfloat16 [1152, 128], P('clip'), may hold values from -0.1875 to 0.1875
- k_half: bfloat16 [1152, 128], P('clip'), may hold values from -0.1875 to 0.1875
- k_quarter: bfloat16 [1152, 128], P('clip'), may hold values from -0.1875 to 0.1875
- w_expand: bfloat16 [128, 512], P('clip'), may hold values from -0.5 to 0.5
- w_two: bfloat16 [4608, 512], P('clip'), may hold values from -0.09375 to 0.09375
- w_three: bfloat16 [512, 2048], P('clip'), may hold values from -0.25 to 0.25
- gain_one: float32 [512], replicated, may hold values from 0.5 to 1.5
- bias_one: float32 [512], replicated, may hold values from -3 to 3
- gain_two: float32 [512], replicated, may hold values from 0.5 to 1.5
- bias_two: float32 [512], replicated, may hold values from -3 to 3
- gain_three: float32 [2048], replicated, may hold values from 0.5 to 1.5
- bias_three: float32 [2048], replicated, may hold values from -3 to 3
- stem_cot: bfloat16 [64, 64, 128, 128], P('clip', None, 'row'), may hold values from -6 to 6
- block_cot: bfloat16 [64, 8, 8, 2048], P('clip', 'row'), may hold values from -6 to 6
Outputs:
- block_out: bfloat16 [64, 8, 8, 2048], P('clip', 'row')
- input_grad: float32 [64, 8, 8, 2048], P('clip', 'row')
- stem_weight_grad: float32 [64, 735], P('clip')
- stem_gain_grad: float32 [64], replicated
- stem_bias_grad: float32 [64], replicated
- w_one_grad: float32 [2048, 512], P('clip')
- w_reduce_grad: float32 [512, 128], P('clip')
- k_fine_grad: float32 [1152, 128], P('clip')
- k_half_grad: float32 [1152, 128], P('clip')
- k_quarter_grad: float32 [1152, 128], P('clip')
- w_expand_grad: float32 [128, 512], P('clip')
- w_two_grad: float32 [4608, 512], P('clip')
- w_three_grad: float32 [512, 2048], P('clip')
- gain_one_grad: float32 [512], replicated
- bias_one_grad: float32 [512], replicated
- gain_two_grad: float32 [512], replicated
- bias_two_grad: float32 [512], replicated
- gain_three_grad: float32 [2048], replicated
- bias_three_grad: float32 [2048], replicated
The draws below stay inside these ranges and needn't reach their ends.
Inputs may be any that keep to these rules, and one draw needn't show every extreme that they name: `frame_start`: the 5 frames from this one form the segment's window. `boundary_mask`: each clip slot holds one or two videos; exactly one segment of a slot is 0, the last segment of its first video (7 where the slot holds one video).
All inputs are finite; a program needn't handle non-finite values.
Results may differ from the reference program's by a relative error of at most 0.02.
Values may be sent and summed in bfloat16 or wider, within the bound.
No kernel may reach another device: no remote copies, remote signals or barrier semaphores. Data moves between devices by JAX's collectives and lax.ppermute only.
A program may use at most 192 MiB of HBM per device.

```python
import jax
import jax.numpy as jnp
from jax import lax

C_IN = 2048
MID = 512
STEM = 64
RED = 128
SEG = 8
WIN = 5
FRAMES = 12
WB = 8
CLIPS = 8
NB = 64
HB = 8
HI = 256
WI = 256
HS = 128
WS = 128
PATCH = 735


def draw_boundary_mask(key, part):
    key = jax.random.fold_in(key, 7)
    first_ends = jax.random.randint(key, (CLIPS,), 1, SEG + 1)
    segment_ids = jnp.arange(SEG)
    return (segment_ids[None, :] != first_ends[:, None] - 1).astype(jnp.int32)


def plant(entries, stream_key, least, top_value):
    longest = entries.shape.index(max(entries.shape))
    spots = []
    for shift in (0, 1):
        where = [jax.random.randint(jax.random.fold_in(stream_key, axis), (), 0, length) for axis, length in enumerate(entries.shape)]
        where[longest] = (where[longest] + shift) % entries.shape[longest]
        spots.append(tuple(where))
    return entries.at[spots[0]].set(least).at[spots[1]].set(top_value)


def levels(key, dims, cuts, least, top_value):
    factor_of, own = 1.0, jax.random.fold_in(key, 6)
    for dim, shards_of in cuts:
        draws = jnp.exp(jax.random.uniform(jax.random.fold_in(own, dim), (shards_of,), jnp.float32, least / len(cuts), top_value / len(cuts)))
        factor_of = factor_of * jnp.repeat(draws, dims[dim] // shards_of).reshape([-1 if axis == dim else 1 for axis in range(len(dims))])
    return factor_of


def bell_draw(rng, dims, scale, reach, cuts=(), held_as=jnp.bfloat16):
    values = scale * jax.random.normal(rng, dims, jnp.float32)
    if cuts:
        values = values * levels(rng, dims, cuts, -0.22, 0.18)
    return jnp.clip(values, -reach, reach).astype(held_as)


def setup_inputs(seed: int = 0) -> dict:
    streams_of = jax.random.split(jax.random.key(seed), 24)
    return {
        "frames": bell_draw(streams_of[0], (CLIPS, FRAMES, 3, HI, WI), 1.0, 6.0, ((0, 8), (3, 4))),
        "frame_start": plant(jax.random.randint(streams_of[1], (CLIPS, SEG), 0, FRAMES - WIN + 1), jax.random.fold_in(streams_of[1], 1), 0, FRAMES - WIN).astype(jnp.int32),
        "boundary_mask": draw_boundary_mask(jax.random.fold_in(streams_of[23], 71), 0),
        "stem_weight": bell_draw(streams_of[3], (STEM, PATCH), PATCH ** -0.5, 0.21875, ((0, 8),)),
        "stem_gain": jnp.clip(jax.random.uniform(streams_of[4], (STEM,), jnp.float32, 0.5, 1.5), 0.5, 1.5),
        "stem_bias": bell_draw(streams_of[5], (STEM,), 0.5, 3.0, (), jnp.float32),
        "block_input": bell_draw(streams_of[6], (NB, HB, WB, C_IN), 1.0, 6.0, ((0, 8), (1, 4))),
        "w_one": bell_draw(streams_of[7], (C_IN, MID), C_IN ** -0.5, 0.125, ((0, 8),)),
        "w_reduce": bell_draw(streams_of[8], (MID, RED), MID ** -0.5, 0.25, ((0, 8),)),
        "k_fine": bell_draw(streams_of[9], (9 * RED, RED), (9 * RED) ** -0.5, 0.1875, ((0, 8),)),
        "k_half": bell_draw(streams_of[10], (9 * RED, RED), (9 * RED) ** -0.5, 0.1875, ((0, 8),)),
        "k_quarter": bell_draw(streams_of[11], (9 * RED, RED), (9 * RED) ** -0.5, 0.1875, ((0, 8),)),
        "w_expand": bell_draw(streams_of[12], (RED, MID), RED ** -0.5, 0.5, ((0, 8),)),
        "w_two": bell_draw(streams_of[13], (9 * MID, MID), (9 * MID) ** -0.5, 0.09375, ((0, 8),)),
        "w_three": bell_draw(streams_of[14], (MID, C_IN), MID ** -0.5, 0.25, ((0, 8),)),
        "gain_one": jnp.clip(jax.random.uniform(streams_of[15], (MID,), jnp.float32, 0.5, 1.5), 0.5, 1.5),
        "bias_one": bell_draw(streams_of[16], (MID,), 0.5, 3.0, (), jnp.float32),
        "gain_two": jnp.clip(jax.random.uniform(streams_of[17], (MID,), jnp.float32, 0.5, 1.5), 0.5, 1.5),
        "bias_two": bell_draw(streams_of[18], (MID,), 0.5, 3.0, (), jnp.float32),
        "gain_three": jnp.clip(jax.random.uniform(streams_of[19], (C_IN,), jnp.float32, 0.5, 1.5), 0.5, 1.5),
        "bias_three": bell_draw(streams_of[20], (C_IN,), 0.5, 3.0, (), jnp.float32),
        "stem_cot": bell_draw(streams_of[21], (NB, STEM, HS, WS), 1.0, 6.0, ((0, 8), (2, 4))),
        "block_cot": bell_draw(streams_of[22], (NB, HB, WB, C_IN), 1.0, 6.0, ((0, 8), (1, 4))),
    }


@jax.custom_vjp
def low(v):
    return lax.optimization_barrier(v.astype(jnp.bfloat16)).astype(jnp.float32)

@jax.custom_vjp
def low_back(v):
    return v

def low_keep(v):
    return (low(v), None)

def low_pass(kept, grad):
    return (grad,)

def back_keep(v):
    return (v, None)

def back_low(kept, grad):
    return (low(grad),)
low.defvjp(low_keep, low_pass)
low_back.defvjp(back_keep, back_low)
epsilon = 1e-05
highest = lax.Precision.HIGHEST

def stack_clip(clip_frames, starts):
    frame_picks = starts[:, None] + jnp.arange(WIN, dtype=jnp.int32)
    window = clip_frames[frame_picks].astype(jnp.float32)
    center = window[:, (WIN - 1) // 2]
    differences = window[:, 1:] - window[:, :-1]
    stacked = jnp.concatenate([center[:, None], differences], axis=1)
    return stacked.reshape(SEG, 3 * WIN, HI, WI)

def stem_conv(stacked, kernel):
    return lax.conv_general_dilated(stacked, kernel, (2, 2), ((3, 3), (3, 3)), dimension_numbers=('NCHW', 'OIHW', 'NCHW'), precision=highest)

def stem_total(frames, frame_start, cot_clips, weight, norm_gain, norm_bias):
    kernel = weight.reshape(STEM, 3 * WIN, 7, 7)

    def pre_of(clip_frames, starts):
        return low_back(stem_conv(low(stack_clip(clip_frames, starts)), kernel))

    def clip_sums(inputs):
        pre_act = pre_of(inputs[0], inputs[1])
        return (lax.optimization_barrier(jnp.sum(pre_act, axis=(0, 2, 3))), lax.optimization_barrier(jnp.sum(pre_act * pre_act, axis=(0, 2, 3))))
    sums_all, squares_all = lax.map(jax.checkpoint(clip_sums), (frames, frame_start))
    count_all = NB * HS * WS
    mean_vec = lax.optimization_barrier(jnp.sum(sums_all, axis=0)) / count_all
    variance = lax.optimization_barrier(jnp.sum(squares_all, axis=0)) / count_all - mean_vec * mean_vec
    inverse = lax.rsqrt(variance + epsilon)

    def clip_total(inputs):
        pre_act = pre_of(inputs[0], inputs[1])
        normed = (pre_act - mean_vec[:, None, None]) * inverse[:, None, None]
        activated = jax.nn.silu(normed * norm_gain[:, None, None] + norm_bias[:, None, None])
        return jnp.sum(activated * inputs[2].astype(jnp.float32))
    return jnp.sum(lax.map(jax.checkpoint(clip_total), (frames, frame_start, cot_clips)))

def conv_same(tensor, kernel, channels):
    kernel_taps = kernel.reshape(3, 3, channels, -1)
    return lax.conv_general_dilated(tensor, kernel_taps, (1, 1), ((1, 1), (1, 1)), dimension_numbers=('NHWC', 'HWIO', 'NHWC'), precision=highest)

def pool_two(tensor):
    images, height, breadth, channels = tensor.shape
    return tensor.reshape(images, height // 2, 2, breadth // 2, 2, channels).mean(axis=(2, 4))

def spread(tensor, factor):
    return jnp.repeat(jnp.repeat(tensor, factor, axis=1), factor, axis=2)

def project(tensor, weight):
    return jnp.einsum('nhwc,cd->nhwd', tensor, weight, precision=highest)

def normalize(pre_act, norm_gain, norm_bias):
    mean_vec = lax.optimization_barrier(jnp.mean(pre_act, axis=(0, 1, 2)))
    variance = lax.optimization_barrier(jnp.mean(pre_act * pre_act, axis=(0, 1, 2))) - mean_vec * mean_vec
    inverse = lax.rsqrt(variance + epsilon)
    return (pre_act - mean_vec) * inverse * norm_gain + norm_bias

def block(mask_float, inputs, w_one, w_reduce, k_fine, k_half, k_quarter, w_expand, w_two, w_three, gain_one, bias_one, gain_two, bias_two, gain_three, bias_three):
    first_pre = low_back(project(inputs, w_one))
    hidden_one = low(jax.nn.silu(normalize(first_pre, gain_one, bias_one)))
    reduced = low_back(project(hidden_one, w_reduce))
    shaped = reduced.reshape(CLIPS, SEG, HB, WB, RED)
    following = jnp.concatenate([shaped[:, 1:], shaped[:, -1:]], axis=1)
    change = low((mask_float[:, :, None, None, None] * (following - shaped)).reshape(NB, HB, WB, RED))
    fine_out = low_back(conv_same(change, k_fine, RED))
    half_map = low(pool_two(change))
    coarse = low_back(conv_same(half_map, k_half, RED))
    quarter = pool_two(half_map)
    coarsest = conv_same(quarter, k_quarter, RED)
    merged = low(fine_out + spread(coarse, 2) + spread(coarsest, 4))
    gate_pre = low_back(project(merged, w_expand))
    gated_map = low(hidden_one * (1.0 + jax.nn.sigmoid(gate_pre)))
    second = low_back(conv_same(gated_map, w_two, MID))
    hidden_two = low(jax.nn.silu(normalize(second, gain_two, bias_two)))
    third_pre = low_back(project(hidden_two, w_three))
    return jax.nn.silu(normalize(third_pre, gain_three, bias_three) + inputs)

def reference(frames, frame_start, boundary_mask, stem_weight, stem_gain, stem_bias, block_input, w_one, w_reduce, k_fine, k_half, k_quarter, w_expand, w_two, w_three, gain_one, bias_one, gain_two, bias_two, gain_three, bias_three, stem_cot, block_cot):
    cot_clips = stem_cot.reshape(CLIPS, SEG, STEM, HS, WS)

    def stem_part(weight, norm_gain, norm_bias):
        return stem_total(frames, frame_start, cot_clips, weight, norm_gain, norm_bias)
    stem_value, stem_backward = jax.vjp(stem_part, stem_weight.astype(jnp.float32), stem_gain, stem_bias)
    stem_grads = stem_backward(jnp.ones((), jnp.float32))
    mask_float = boundary_mask.astype(jnp.float32)

    def block_part(*primals):
        return block(mask_float, *primals)
    primals = (block_input.astype(jnp.float32), w_one.astype(jnp.float32), w_reduce.astype(jnp.float32), k_fine.astype(jnp.float32), k_half.astype(jnp.float32), k_quarter.astype(jnp.float32), w_expand.astype(jnp.float32), w_two.astype(jnp.float32), w_three.astype(jnp.float32), gain_one, bias_one, gain_two, bias_two, gain_three, bias_three)
    output, block_backward = jax.vjp(block_part, *primals)
    grads = block_backward(block_cot.astype(jnp.float32))
    return (output.astype(jnp.bfloat16), grads[0], stem_grads[0], stem_grads[1], stem_grads[2], grads[1], grads[2], grads[3], grads[4], grads[5], grads[6], grads[7], grads[8], grads[9], grads[10], grads[11], grads[12], grads[13], grads[14])
```

```python
import jax
import jax.numpy as jnp
from jax import lax
from jax.sharding import PartitionSpec as P

STEM = 64
SEG = 8
WIN = 5


epsilon = 1e-05
highest = lax.Precision.HIGHEST


def with_halo(x, sides, width):
    for axis, dim in sides:
        size, length = (lax.axis_size(axis), x.shape[dim])
        up = [(i, (i + 1) % size) for i in range(size - 1)]
        down = [(j, i) for i, j in up]
        last = lax.slice_in_dim(x, length - width, length, axis=dim)
        leading = lax.slice_in_dim(x, 0, width, axis=dim)
        before = lax.ppermute(last, axis, up)
        after = lax.ppermute(leading, axis, down)
        x = jnp.concatenate([before, x, after], axis=dim)
    return x


def silu_slope(values):
    sigmoid_val = jax.nn.sigmoid(values)
    return sigmoid_val * (1.0 + values * (1.0 - sigmoid_val))


def project(tensor, weight):
    flat_rows = tensor.reshape(-1, tensor.shape[-1])
    return jnp.dot(flat_rows, weight, preferred_element_type=jnp.float32).reshape(
        tensor.shape[:-1] + (weight.shape[1],)
    )


def project_back(cotangent, weight):
    flat_rows = cotangent.reshape(-1, cotangent.shape[-1])
    result = lax.dot_general(
        flat_rows, weight, (((1,), (1,)), ((), ())), preferred_element_type=jnp.float32
    )
    return result.reshape(cotangent.shape[:-1] + (weight.shape[0],))


def outer_sum(tensor, cotangent):
    return lax.dot_general(
        tensor.reshape(-1, tensor.shape[-1]),
        cotangent.reshape(-1, cotangent.shape[-1]),
        (((0,), (0,)), ((), ())),
        preferred_element_type=jnp.float32,
    )


def conv_same(padded, kernel, precision=None):
    channels = padded.shape[-1]
    kernel_taps = kernel.reshape(3, 3, channels, -1)
    return lax.conv_general_dilated(
        padded,
        kernel_taps,
        (1, 1),
        ((1, 1), (1, 1)),
        dimension_numbers=("NHWC", "HWIO", "NHWC"),
        preferred_element_type=jnp.float32,
        precision=precision,
    )


def flipped(kernel, channels):
    kernel_taps = kernel.reshape(3, 3, channels, -1)
    return jnp.flip(kernel_taps, (0, 1)).transpose(0, 1, 3, 2).reshape(-1, channels)


def kernel_grad(padded, cotangent, precision=None):
    widened = jnp.pad(padded, ((0, 0), (1, 1), (1, 1), (0, 0)))
    result = lax.conv_general_dilated(
        widened,
        cotangent,
        (1, 1),
        "VALID",
        dimension_numbers=("CHWN", "IHWO", "HWNC"),
        preferred_element_type=jnp.float32,
        precision=precision,
    )
    return result.reshape(-1, cotangent.shape[-1])


def pool_sum(tensor):
    images, height, breadth, channels = tensor.shape
    return tensor.reshape(images, height // 2, 2, breadth // 2, 2, channels).sum(axis=(2, 4))


def spread(tensor, factor):
    return jnp.repeat(jnp.repeat(tensor, factor, axis=1), factor, axis=2)


def exchange(blocks, axis):
    return lax.all_to_all(blocks, axis, 0, 0)


def to_all(part, axis):
    size = lax.axis_size(axis)
    return exchange(jnp.broadcast_to(part[None], (size,) + part.shape), axis)


def total(sums, axis):
    flat = jnp.concatenate([entry.reshape(-1) for entry in sums])
    rows = jnp.pad(flat, (0, -flat.size % 1024)).reshape(-1, 128)
    flat = jnp.sum(to_all(rows, axis), 0).reshape(-1)
    results, start = [], 0
    for entry in sums:
        results.append(flat[start : start + entry.size].reshape(entry.shape))
        start += entry.size
    return results


def moments(values, axes):
    return (jnp.sum(values, axes), jnp.sum(values * values, axes))


def statistics(totals, count):
    mean = totals[0] / count
    return mean, lax.rsqrt(totals[1] / count - mean * mean + epsilon)


def gather_pair(shard):
    side = lax.rem(lax.axis_index("row"), 2)
    half = shard.shape[0] // 2
    mine = to_all(lax.dynamic_slice_in_dim(shard, side * half, half, 0), "clip")
    size = lax.axis_size("row")
    other = lax.ppermute(mine, "row", [(i, i ^ 1) for i in range(size)])
    lower = jnp.where(side == 0, mine, other)
    upper = jnp.where(side == 0, other, mine)
    return jnp.stack([lower, upper], 1).reshape((mine.shape[0], 2 * half) + mine.shape[2:])


def strided(vector, clips, rows, place):
    return lax.dynamic_index_in_dim(
        vector.reshape(clips, rows, -1), place, 1, keepdims=False
    ).reshape(-1)


def per_device(
    frames,
    frame_start,
    boundary_mask,
    stem_weight,
    stem_gain,
    stem_bias,
    block_input,
    w_one,
    w_reduce,
    k_fine,
    k_half,
    k_quarter,
    w_expand,
    w_two,
    w_three,
    gain_one,
    bias_one,
    gain_two,
    bias_two,
    gain_three,
    bias_three,
    stem_cot,
    block_cot,
):
    bf16, f32 = jnp.bfloat16, jnp.float32
    nc, nr = lax.axis_size("clip"), lax.axis_size("row")
    place = lax.axis_index("row")
    both = ("clip", "row")
    clip_count = frames.shape[0]
    images, block_rows, cols, c_in = block_input.shape
    mid = gain_one.shape[0]
    red = w_reduce.shape[1]
    height = block_rows * nr
    mid_r, in_r = mid // nr, c_in // nr
    step = c_in // (nc * nr)
    pixels = images * height * cols
    own = images * block_rows * cols
    map_count = pixels * nc

    full_stem = to_all(stem_weight, "clip").reshape(STEM, -1)
    full_one = gather_pair(w_one).reshape(c_in, mid)
    parts = (w_reduce, k_fine, k_half, k_quarter, w_expand.reshape(-1, red))
    packed = gather_pair(jnp.concatenate(parts, 0))
    full_small, start = [], 0
    for part in parts:
        full_small.append(packed[:, start : start + part.shape[0]].reshape(-1, red))
        start += part.shape[0]
    full_reduce, full_fine, full_half, full_quarter, full_expand = full_small
    full_expand = full_expand.reshape(red, mid)
    two_r = to_all(
        lax.dynamic_slice_in_dim(w_two, place * mid_r, mid_r, 1), "clip"
    ).reshape(-1, mid_r)
    three_r = to_all(
        lax.dynamic_index_in_dim(
            w_three.reshape(-1, nc, nr, step), place, 2, keepdims=False
        ).reshape(-1, in_r),
        "clip",
    ).reshape(mid, in_r)

    def to_channels(tensor):
        return tensor.reshape(images, block_rows, cols, nc, nr, step).transpose(4, 0, 1, 2, 3, 5)

    def from_pixels(blocks):
        return blocks.swapaxes(0, 1).reshape(images, height, cols, -1)

    swapped = exchange(
        jnp.stack([to_channels(block_input), to_channels(block_cot)], 1), "row"
    ).reshape(nr, 2, images, block_rows, cols, in_r)
    input_r = from_pixels(swapped[:, 0])
    cot_r = from_pixels(swapped[:, 1])

    frame_rows = frames.shape[3]
    columns = frames.shape[4]
    offsets = frame_start[:, :, None] + jnp.arange(WIN, dtype=jnp.int32)
    window = jax.vmap(lambda clip_frames, frame_picks: clip_frames[frame_picks])(frames, offsets)
    window_float = window.astype(f32)
    center = window_float[:, :, (WIN - 1) // 2]
    differences = window_float[:, :, 1:] - window_float[:, :, :-1]
    stacked = jnp.concatenate([center[:, :, None], differences], axis=2)
    stacked = stacked.reshape(clip_count * SEG, 3 * WIN, frame_rows, columns).astype(bf16)
    padded_stem = with_halo(stacked, (("row", 2),), 3)
    padded_stem = jnp.pad(padded_stem, ((0, 0), (0, 0), (0, 0), (3, 3)))
    stem_kernel = full_stem.reshape(STEM, 3 * WIN, 7, 7)
    stem_pre = lax.conv_general_dilated(
        padded_stem,
        stem_kernel,
        (2, 2),
        "VALID",
        dimension_numbers=("NCHW", "OIHW", "NCHW"),
        preferred_element_type=f32,
    )
    column = (1, -1, 1, 1)
    stem_count = stem_pre.size // STEM * nc * nr
    stem_mean, stem_inverse = statistics(total(moments(stem_pre, (0, 2, 3)), both), stem_count)
    stem_normed = (stem_pre - stem_mean.reshape(column)) * stem_inverse.reshape(column)
    stem_level = stem_normed * stem_gain.reshape(column) + stem_bias.reshape(column)
    stem_outer = stem_cot.astype(f32) * silu_slope(stem_level)
    stem_bias_grad, stem_gain_grad = total(
        (jnp.sum(stem_outer, (0, 2, 3)), jnp.sum(stem_outer * stem_normed, (0, 2, 3))), both
    )
    stem_grad = (stem_gain * stem_inverse).reshape(column) * (
        stem_outer
        - (stem_bias_grad / stem_count).reshape(column)
        - stem_normed * (stem_gain_grad / stem_count).reshape(column)
    )
    stem_kernel_grad = lax.conv_general_dilated(
        padded_stem,
        stem_grad.astype(bf16),
        (1, 1),
        "VALID",
        rhs_dilation=(2, 2),
        dimension_numbers=("CNHW", "IOHW", "CNHW"),
        preferred_element_type=f32,
    )[:, :, :7, :7]

    first_pre = project(block_input, full_one)
    mean_one, inverse_one = statistics(total(moments(first_pre, (0, 1, 2)), both), map_count)
    normed_one = (first_pre - mean_one) * inverse_one
    level_one = normed_one * gain_one + bias_one
    hidden_one = jax.nn.silu(level_one).astype(bf16)
    shaped = project(hidden_one, full_reduce).reshape(clip_count, SEG, block_rows, cols, red)
    following = jnp.concatenate([shaped[:, 1:], shaped[:, -1:]], axis=1)
    mask_float = boundary_mask.astype(f32)[:, :, None, None, None]
    change = (mask_float * (following - shaped)).reshape(images, block_rows, cols, red)
    change = from_pixels(lax.all_gather(change.astype(bf16), "row"))
    row_start = place * block_rows

    def own_rows(tensor):
        return lax.dynamic_slice_in_dim(tensor, row_start, block_rows, 1)

    half_map = (pool_sum(change.astype(f32)) * 0.25).astype(bf16)
    quarter = pool_sum(half_map.astype(f32)) * 0.25
    quarter_kernel = full_quarter.astype(f32)
    fine_out = conv_same(change, full_fine)
    coarse = conv_same(half_map, full_half)
    coarsest = conv_same(quarter, quarter_kernel, highest)
    merged = own_rows(fine_out + spread(coarse, 2) + spread(coarsest, 4)).astype(bf16)
    sigmoid_gate = jax.nn.sigmoid(project(merged, full_expand))
    hidden_float = hidden_one.astype(f32)
    gated = (hidden_float * (1.0 + sigmoid_gate)).astype(bf16)
    gated = from_pixels(lax.all_gather(gated, "row"))
    second = conv_same(gated, two_r)

    def mid_slice(vector):
        return lax.dynamic_slice_in_dim(vector, place * mid_r, mid_r, 0)

    gain_two_r = mid_slice(gain_two)
    mean_two, inverse_two = statistics(total(moments(second, (0, 1, 2)), "clip"), map_count)
    normed_two = (second - mean_two) * inverse_two
    level_two = normed_two * gain_two_r + mid_slice(bias_two)
    hidden_two = jax.nn.silu(level_two).astype(bf16).reshape(pixels, mid_r)
    hidden_two = lax.all_gather(hidden_two, "row").swapaxes(0, 1).reshape(pixels, mid)
    third = jnp.dot(hidden_two, three_r, preferred_element_type=f32)
    gain_three_r = strided(gain_three, nc, nr, place)
    bias_three_r = strided(bias_three, nc, nr, place)
    mean_three, inverse_three = statistics(total(moments(third, 0), "clip"), map_count)
    normed_three = (third - mean_three) * inverse_three
    summed = normed_three * gain_three_r + bias_three_r + input_r.reshape(pixels, in_r).astype(f32)
    block_out_r = jax.nn.silu(summed).astype(bf16)
    grad_summed = cot_r.reshape(pixels, in_r).astype(f32) * silu_slope(summed)
    bias_three_grad, gain_three_grad = total(
        (jnp.sum(grad_summed, 0), jnp.sum(grad_summed * normed_three, 0)), "clip"
    )

    def to_pixels(tensor):
        return tensor.reshape(images, nr, block_rows, cols, in_r).swapaxes(0, 1)

    returned = exchange(
        jnp.stack([to_pixels(block_out_r), to_pixels(grad_summed.astype(bf16))], 1), "row"
    )
    returned = returned.reshape(nr, 2, images, block_rows, cols, nc, step)
    returned = returned.transpose(1, 2, 3, 4, 5, 0, 6).reshape(2, images, block_rows, cols, c_in)
    block_out = returned[0]

    grad_third = (
        gain_three_r
        * inverse_three
        * (
            grad_summed
            - bias_three_grad / map_count
            - normed_three * (gain_three_grad / map_count)
        )
    ).astype(bf16)
    three_grad = jnp.sum(
        exchange(outer_sum(hidden_two, grad_third).astype(bf16).reshape(nc, -1, in_r), "clip"),
        0,
        dtype=f32,
    )
    back_two = project_back(grad_third, three_r).astype(bf16)
    back_two = jnp.sum(
        exchange(back_two.reshape(pixels, nr, mid_r).swapaxes(0, 1), "row"), 0, dtype=f32
    ).reshape(level_two.shape)
    grad_two = back_two * silu_slope(level_two)
    bias_two_grad, gain_two_grad = total(
        (jnp.sum(grad_two, (0, 1, 2)), jnp.sum(grad_two * normed_two, (0, 1, 2))), "clip"
    )
    grad_second = (
        gain_two_r
        * inverse_two
        * (grad_two - bias_two_grad / map_count - normed_two * (gain_two_grad / map_count))
    ).astype(bf16)
    two_grad = jnp.sum(
        exchange(kernel_grad(gated, grad_second).astype(bf16).reshape(nc, -1, mid_r), "clip"),
        0,
        dtype=f32,
    )
    grad_gated = conv_same(grad_second, flipped(two_r, mid)).astype(bf16)
    grad_gated = grad_gated.reshape(images, nr, block_rows, cols, mid).swapaxes(0, 1)
    grad_gated = jnp.sum(exchange(grad_gated, "row"), 0, dtype=f32)
    grad_gate = (grad_gated * hidden_float * sigmoid_gate * (1.0 - sigmoid_gate)).astype(bf16)
    expand_grad = outer_sum(merged, grad_gate)
    grad_fine = project_back(grad_gate, full_expand).astype(bf16)
    grad_fine = from_pixels(lax.all_gather(grad_fine, "row"))
    grad_coarse = pool_sum(grad_fine.astype(f32))
    grad_coarsest = pool_sum(grad_coarse)
    grad_coarse = grad_coarse.astype(bf16)
    grad_half = conv_same(grad_coarse, flipped(full_half, red)) + 0.25 * spread(
        conv_same(grad_coarsest, flipped(quarter_kernel, red), highest), 2
    )
    grad_change = own_rows(
        conv_same(grad_fine, flipped(full_fine, red)) + 0.25 * spread(grad_half, 2)
    )
    keep_mask = mask_float * (jnp.arange(SEG) < SEG - 1).astype(f32)[None, :, None, None, None]
    carried = keep_mask * grad_change.reshape(shaped.shape)
    grad_reduced = (
        jnp.concatenate([jnp.zeros_like(carried[:, :1]), carried[:, :-1]], axis=1) - carried
    )
    grad_reduced = grad_reduced.reshape(images, block_rows, cols, red).astype(bf16)
    reduce_grad = outer_sum(hidden_one, grad_reduced)
    grad_hidden = grad_gated * (1.0 + sigmoid_gate) + project_back(grad_reduced, full_reduce)
    grad_one = grad_hidden * silu_slope(level_one)
    bias_one_grad, gain_one_grad = total(
        (jnp.sum(grad_one, (0, 1, 2)), jnp.sum(grad_one * normed_one, (0, 1, 2))), both
    )
    grad_first = (
        gain_one
        * inverse_one
        * (grad_one - bias_one_grad / map_count - normed_one * (gain_one_grad / map_count))
    ).astype(bf16)
    input_grad = returned[1].astype(f32) + project_back(grad_first, full_one)
    grad_first = from_pixels(lax.all_gather(grad_first, "row"))
    one_grad = outer_sum(input_r, grad_first).astype(bf16).reshape(nc, -1, mid)

    def padded_parts(gradient):
        shares = gradient.reshape(nc, -1)
        shares = jnp.pad(shares, ((0, 0), (0, -shares.shape[1] % (nr * 8 * red))))
        return shares.reshape(nc, nr, -1, red)

    def quarter_of(gradient):
        return lax.dynamic_index_in_dim(padded_parts(gradient), place, 1, keepdims=False)

    def share_of(blocks, like):
        return blocks.reshape(-1)[: like.size].reshape(like.shape)

    clip_parts = [
        one_grad.reshape(nc, -1, red),
        quarter_of(kernel_grad(change, grad_fine)).astype(bf16),
        quarter_of(kernel_grad(half_map, grad_coarse)).astype(bf16),
        quarter_of(kernel_grad(quarter, grad_coarsest, highest)).astype(bf16),
    ]
    clip_sizes = [part.shape[1] for part in clip_parts]
    clip_sum = jnp.sum(exchange(jnp.concatenate(clip_parts, 1), "clip"), 0, dtype=f32)
    both_parts = [
        padded_parts(part).reshape(nc * nr, -1, red)
        for part in (reduce_grad, expand_grad, stem_kernel_grad)
    ]
    both_sizes = [part.shape[1] for part in both_parts]
    both_sum = jnp.sum(
        exchange(jnp.concatenate(both_parts, 1).astype(bf16), both), 0, dtype=f32
    )
    shares_a = lax.all_gather(
        jnp.concatenate([two_grad.reshape(-1, red), three_grad.reshape(-1, red)], 0).astype(bf16),
        "row",
    ).astype(f32)
    two_rows = two_grad.size // red
    two_share = shares_a[:, :two_rows].reshape(nr, -1, mid_r).swapaxes(0, 1).reshape(-1, mid)
    three_share = shares_a[:, two_rows:].reshape(nr, -1, nc, step)
    three_share = three_share.transpose(1, 2, 0, 3).reshape(-1, c_in)
    shares_b = lax.all_gather(
        jnp.concatenate([clip_sum, both_sum], 0).astype(bf16), "row"
    ).astype(f32)
    cut = []
    start = 0
    for size in clip_sizes + both_sizes:
        cut.append(shares_b[:, start : start + size])
        start += size
    one_share = cut[0].reshape(-1, mid)
    fine_share, half_share, quarter_share, reduce_share, expand_share, stem_share = (
        share_of(blocks, like)
        for blocks, like in zip(
            cut[1:], (k_fine, k_half, k_quarter, w_reduce, w_expand, stem_weight)
        )
    )
    vectors = jnp.concatenate([gain_two_grad, bias_two_grad, gain_three_grad, bias_three_grad])
    vectors = lax.all_gather(vectors.reshape(-1, red), "row").reshape(nr, -1)
    gain_two_full = vectors[:, :mid_r].reshape(-1)
    bias_two_full = vectors[:, mid_r : 2 * mid_r].reshape(-1)
    gain_three_full = vectors[:, 2 * mid_r : 2 * mid_r + in_r].reshape(nr, nc, step)
    bias_three_full = vectors[:, 2 * mid_r + in_r :].reshape(nr, nc, step)
    return (
        block_out,
        input_grad,
        stem_share,
        stem_gain_grad,
        stem_bias_grad,
        one_share,
        reduce_share,
        fine_share,
        half_share,
        quarter_share,
        expand_share,
        two_share,
        three_share,
        gain_one_grad,
        bias_one_grad,
        gain_two_full,
        bias_two_full,
        gain_three_full.swapaxes(0, 1).reshape(-1),
        bias_three_full.swapaxes(0, 1).reshape(-1),
    )


def solution(mesh):
    in_specs = (
        P("clip", None, None, "row", None),
        P("clip", None),
        P("clip", None),
        P("clip", None),
        P(),
        P(),
        P("clip", "row", None, None),
        P("clip", None),
        P("clip", None),
        P("clip", None),
        P("clip", None),
        P("clip", None),
        P("clip", None),
        P("clip", None),
        P("clip", None),
        P(),
        P(),
        P(),
        P(),
        P(),
        P(),
        P("clip", None, "row", None),
        P("clip", "row", None, None),
    )
    out_specs = (
        P("clip", "row", None, None),
        P("clip", "row", None, None),
        P("clip", None),
        P(),
        P(),
        P("clip", None),
        P("clip", None),
        P("clip", None),
        P("clip", None),
        P("clip", None),
        P("clip", None),
        P("clip", None),
        P("clip", None),
        P(),
        P(),
        P(),
        P(),
        P(),
        P(),
    )
    return jax.shard_map(
        per_device, mesh=mesh, in_specs=in_specs, out_specs=out_specs, check_vma=False
    )
```

```python
import functools

import jax
import jax.numpy as jnp
from jax import lax
from jax.experimental import pallas as pl
from jax.experimental.pallas import tpu as pltpu
from jax.sharding import PartitionSpec as P

STEM = 64
SEG = 8
WIN = 5


epsilon = 1e-05


def silu_slope(values):
    sigmoid_val = jax.nn.sigmoid(values)
    return sigmoid_val * (1.0 + values * (1.0 - sigmoid_val))


def statistics(totals, count):
    mean = totals[0] / count
    return mean, lax.rsqrt(totals[1] / count - mean * mean + epsilon)


def stack_index(shape, dim):
    return lax.broadcasted_iota(jnp.int32, shape, dim)


def stem_planes_kernel(
    start_ref, local_ref, above_ref, below_ref, planes_ref, pick_ref, shift_ref
):
    pair = pl.program_id(0)

    @pl.when(pair == 0)
    def _():
        dims = (256, 240)
        out, inner = stack_index(dims, 0), stack_index(dims, 1)
        channel, plane = out % 16, inner // 16
        plus = plane == jnp.where(channel < 3, channel + 6, channel)
        minus = (channel >= 3) & (plane == channel - 3)
        value = jnp.where(plus, 1.0, 0.0) - jnp.where(minus, 1.0, 0.0)
        keep = (out // 16 == inner % 16) & (channel < 15)
        pick_ref[...] = jnp.where(keep, value, 0.0).astype(jnp.bfloat16)
        dims = (256, 896)
        source, target = stack_index(dims, 0), stack_index(dims, 1)
        wanted = 2 * (target % 128) + target // 128 - 3
        shift_ref[...] = jnp.where(source == wanted, 1.0, 0.0).astype(jnp.bfloat16)

    for side in range(2):
        first = start_ref[2 * pair + side]
        lanes = slice(128 * side, 128 * side + 128)
        for block in range(6):
            if block == 0:
                window = above_ref[pl.ds(first, WIN)]
            elif block == 5:
                window = below_ref[pl.ds(first, WIN)]
            else:
                window = local_ref[pl.ds(first, WIN), :, 16 * block - 16 : 16 * block, :]
            window = window.reshape(240, 256)
            stacked = jnp.dot(pick_ref[...], window, preferred_element_type=jnp.float32)
            shifted = jnp.dot(
                stacked.astype(jnp.bfloat16), shift_ref[...], preferred_element_type=jnp.float32
            ).astype(jnp.bfloat16)
            low, high = (8 if block == 0 else 0), (8 if block == 5 else 16)
            for kx in range(7):
                piece = shifted[:, 128 * kx : 128 * kx + 128].reshape(16, 16, 128)
                planes_ref[
                    0, 16 * block - 8 + low : 16 * block - 8 + high, 16 * kx : 16 * kx + 16, lanes
                ] = piece[low:high]


def stem_conv_kernel(planes_ref, weight_ref, pre_ref, sums_ref):
    @pl.when(pl.program_id(0) == 0)
    def _():
        sums_ref[...] = jnp.zeros_like(sums_ref)

    @pl.loop(0, 8)
    def _(group):
        patches = planes_ref[0, pl.ds(5 + 8 * group, 13)].reshape(13 * 112, 256)
        out = jnp.dot(weight_ref[...], patches, preferred_element_type=jnp.float32)
        out = out.reshape(4, 64, 256)
        for side in range(2):
            half = out[:, :, 128 * side : 128 * side + 128]
            pre_ref[side, pl.ds(4 * group, 4)] = half
            sums_ref[0] += jnp.sum(half, 0)
            sums_ref[1] += jnp.sum(half * half, 0)


def stem_slope_kernel(pre_ref, cot_ref, vectors_ref, outer_ref, sums_ref, swap_ref):
    @pl.when(pl.program_id(0) == 0)
    def _():
        out, inner = stack_index((256, 256), 0), stack_index((256, 256), 1)
        hit = (out // 16 == inner % 16) & (out % 16 == inner // 16)
        swap_ref[...] = jnp.where(hit, 1.0, 0.0).astype(jnp.bfloat16)
        sums_ref[...] = jnp.zeros_like(sums_ref)

    for part in range(4):
        channels = slice(16 * part, 16 * part + 16)
        mean, inverse = vectors_ref[0, channels], vectors_ref[1, channels]
        gain, bias = vectors_ref[2, channels], vectors_ref[3, channels]
        block = jnp.concatenate(
            [cot_ref[0, channels, 16 * k : 16 * k + 16, :].reshape(256, 128) for k in range(2)], 1
        )
        turned = jnp.dot(swap_ref[...], block, preferred_element_type=jnp.float32)
        total_bias, total_gain = jnp.zeros((16, 128)), jnp.zeros((16, 128))
        for k in range(2):
            rows = slice(16 * k, 16 * k + 16)
            cot = turned[:, 128 * k : 128 * k + 128].reshape(16, 16, 128)
            normed = (pre_ref[0, rows, channels, :] - mean) * inverse
            outer = cot * silu_slope(normed * gain + bias)
            outer_ref[0, rows, channels, :] = outer.astype(jnp.bfloat16)
            total_bias += jnp.sum(outer, 0)
            total_gain += jnp.sum(outer * normed, 0)
        sums_ref[0, channels] += total_bias
        sums_ref[1, channels] += total_gain


def stem_grad_kernel(planes_ref, pre_ref, outer_ref, vectors_ref, out_ref, acc_ref):
    pair, last = pl.program_id(0), pl.num_programs(0) - 1

    @pl.when(pair == 0)
    def _():
        acc_ref[...] = jnp.zeros_like(acc_ref)

    @pl.loop(0, 8)
    def _(group):
        rows = pl.ds(4 * group, 4)
        sides = []
        for side in range(2):
            normed = (pre_ref[side, rows] - vectors_ref[0]) * vectors_ref[1]
            outer = outer_ref[side, rows].astype(jnp.float32)
            grad = vectors_ref[2] * (outer - vectors_ref[3] - normed * vectors_ref[4])
            sides.append(grad.astype(jnp.bfloat16).reshape(256, 128))
        patches = planes_ref[0, pl.ds(5 + 8 * group, 13)].reshape(13 * 112, 256)
        acc_ref[...] += lax.dot_general(
            jnp.concatenate(sides, 1),
            patches,
            (((1,), (1,)), ((), ())),
            preferred_element_type=jnp.float32,
        )

    @pl.when(pair == last)
    def _():
        total = acc_ref[0:64, 0:784]
        for y in range(1, 4):
            total += acc_ref[64 * y : 64 * y + 64, 224 * y : 224 * y + 784]
        total = jnp.concatenate([total, jnp.zeros((64, 240), jnp.float32)], 1)
        for part in range(8):
            out_ref[part] = total[:, 128 * part : 128 * part + 128]


stem_limit = 24 * 1024 * 1024
block_limit = 40 * 1024 * 1024
planes_shape, map_shape = (80, 112, 256), (32, 64, 128)


def whole(shape):
    return pl.BlockSpec(shape, lambda *_: (0,) * len(shape))


def by_step(shape):
    return pl.BlockSpec(shape, lambda i: (i,) + (0,) * (len(shape) - 1))


def in_hbm(array):
    return pltpu.with_memory_space_constraint(array, pltpu.HBM)


def stem_call(kernel, steps, in_specs, out_specs, outs, scratch, flops, moved, args, waits=()):
    used = len(args)

    def body(*refs):
        kernel(*refs[:used], *refs[used + len(waits) :])

    return pl.pallas_call(
        body,
        grid=(steps,),
        in_specs=in_specs + [pl.BlockSpec(memory_space=pl.ANY)] * len(waits),
        out_specs=out_specs,
        out_shape=[
            (pltpu.HBM if len(shape) == 4 else jax.ShapeDtypeStruct)(shape, dtype)
            for shape, dtype in outs
        ],
        scratch_shapes=[pltpu.VMEM(shape, dtype) for shape, dtype in scratch],
        compiler_params=pltpu.CompilerParams(vmem_limit_bytes=stem_limit),
        cost_estimate=pl.CostEstimate(flops=flops, bytes_accessed=moved, transcendentals=0),
    )(*(in_hbm(entry) if entry.ndim > 1 else entry for entry in args), *waits)


def stem_planes(starts, local, above, below):
    pairs = starts.shape[0] // 2
    return stem_call(
        stem_planes_kernel,
        pairs,
        [pl.BlockSpec(memory_space=pltpu.SMEM)]
        + [whole(entry.shape) for entry in (local, above, below)],
        [by_step((1,) + planes_shape)],
        [((pairs,) + planes_shape, jnp.bfloat16)],
        [((256, 240), jnp.bfloat16), ((256, 896), jnp.bfloat16)],
        4 * 10**9 * pairs,
        5 * 10**6 * pairs,
        (starts, local, above, below),
    )[0]


def stem_conv(planes, weight, *waits):
    pairs = planes.shape[0]
    return stem_call(
        stem_conv_kernel,
        pairs,
        [
            by_step((1,) + planes_shape),
            whole(weight.shape),
        ],
        [by_step((2,) + map_shape), whole((2, 64, 128))],
        [((2 * pairs,) + map_shape, jnp.float32), ((2, 64, 128), jnp.float32)],
        [],
        4 * 10**9 * pairs,
        7 * 10**6 * pairs,
        (planes, weight),
        waits,
    )


def stem_slope(pre, cot, first, vectors, *waits):
    images = pre.shape[0] // 2
    return stem_call(
        stem_slope_kernel,
        images,
        [
            pl.BlockSpec((1,) + map_shape, lambda i: (i + first, 0, 0, 0)),
            pl.BlockSpec((1, 64, 32, 128), lambda i: (i + first, 0, 0, 0)),
            whole(vectors.shape),
        ],
        [by_step((1,) + map_shape), whole((2, 64, 128))],
        [((images,) + map_shape, jnp.bfloat16), ((2, 64, 128), jnp.float32)],
        [((256, 256), jnp.bfloat16)],
        10**9 * images,
        2 * 10**6 * images,
        (pre, cot, vectors),
        waits,
    )


def stem_grad(planes, pre, outer, first, vectors, *waits):
    pairs = planes.shape[0] // 2

    def later(shape):
        return pl.BlockSpec(shape, lambda i: (i + first, 0, 0, 0))

    return stem_call(
        stem_grad_kernel,
        pairs,
        [
            later((1,) + planes_shape), later((2,) + map_shape), by_step((2,) + map_shape),
            whole(vectors.shape),
        ],
        [whole((8, 64, 128))],
        [((8, 64, 128), jnp.float32)],
        [((256, 13 * 112), jnp.float32)],
        4 * 10**9 * pairs,
        8 * 10**6 * pairs,
        (planes, pre, outer, vectors),
        waits,
    )[0]


def filters_inside(weight):
    taps = weight.reshape(-1, 3 * WIN, 49).swapaxes(1, 2)
    return jnp.pad(taps, ((0, 0), (0, 0), (0, 1))).reshape(weight.shape[0], -1)


def filters_outside(weight):
    return weight.reshape(-1, 49, 16)[:, :, : 3 * WIN].swapaxes(1, 2).reshape(weight.shape[0], -1)


def lanes(*entries):
    return jnp.broadcast_to(jnp.stack(entries)[:, :, None], (len(entries), entries[0].size, 128))


taps = [(ky, kx) for ky in range(3) for kx in range(3)]
f32, bf16 = jnp.float32, jnp.bfloat16


def dot(left, right, sides="NN", precision=None):
    contract = ((0 if sides[0] == "T" else 1,), (1 if sides[1] == "T" else 0,))
    return lax.dot_general(
        left, right, (contract, ((), ())), preferred_element_type=f32, precision=precision
    )


def split_dot(matrix, values):
    upper = values.astype(bf16)
    lower = (values - upper.astype(f32)).astype(bf16)
    return dot(matrix, upper) + dot(matrix, lower)


def shift_columns(pad_ref, values, width):
    rows = values.shape[0]
    band = (pad_ref.shape[1] - rows) // 2
    column = stack_index(values.shape, 0) % width
    wide = values.astype(f32)
    for kx in range(3):
        moved = wide
        if kx == 0:
            moved = jnp.where(column == 0, 0.0, pltpu.roll(wide, 1, 0))
        if kx == 2:
            moved = jnp.where(column == width - 1, 0.0, pltpu.roll(wide, rows - 1, 0))
        zeros = jnp.zeros((band, values.shape[1]), pad_ref.dtype)
        pad_ref[kx, 0:band] = zeros
        pad_ref[kx, band : band + rows] = moved.astype(pad_ref.dtype)
        pad_ref[kx, band + rows :] = zeros
    return band


def conv_taps(pad_ref, band, first, rows, weight_ref, back=False, precision=None):
    channels = weight_ref.shape[0] // 9
    result = None
    for ky, kx in taps:
        part = pad_ref[kx, pl.ds(first + ky * band, rows)]
        tap = 8 - (3 * ky + kx) if back else 3 * ky + kx
        weight = weight_ref[tap * channels : (tap + 1) * channels, :].astype(pad_ref.dtype)
        term = dot(part, weight, "NT" if back else "NN", precision)
        result = term if result is None else result + term
    return result


def pool_matrix(out_rows, rows, factor, width, value, dtype=bf16):
    out, inner = stack_index((out_rows, rows), 0), stack_index((out_rows, rows), 1)
    band, small = SEG * width, width // factor
    out_band = SEG * small
    hit = (
        (out // out_band == inner // band // factor)
        & (out % out_band // small == inner % band // width)
        & (out % small == inner % width // factor)
    )
    return jnp.where(hit, value, 0.0).astype(dtype)


def spread_matrix(rows, factor, width):
    small = width // factor
    dims = (rows, SEG * small)
    out, inner = stack_index(dims, 0), stack_index(dims, 1)
    image, column = out % (SEG * width) // width, out % width
    hit = (inner // small == image) & (inner % small == column // factor)
    return jnp.where(hit, 1.0, 0.0).astype(bf16)


def as_row(block):
    return jnp.concatenate([block[j : j + 1] for j in range(block.shape[0])], 1)


def as_block(row):
    lanes_of = row.shape[1] // 128
    return jnp.concatenate([row[:, 128 * j : 128 * j + 128] for j in range(lanes_of)], 0)


def put_sums(out_ref, first, second, extra=None):
    block = jnp.concatenate([as_block(first), as_block(second)], 0)
    rows = out_ref.shape[1]
    if extra is not None:
        block = jnp.concatenate([block, extra], 0)
    if block.shape[0] < rows:
        block = jnp.concatenate([block, jnp.zeros((rows - block.shape[0], 128), f32)], 0)
    out_ref[...] = jnp.broadcast_to(block[None], out_ref.shape)


def get_sums(sums_ref, rows):
    block = jnp.sum(sums_ref[...], 0)
    return as_row(block[:rows]), as_row(block[rows : 2 * rows])


def norm_of(sums_ref, rows, count):
    first, second = get_sums(sums_ref, rows)
    mean = first / count
    return mean, lax.rsqrt(second / count - mean * mean + epsilon)


def silu(values):
    return values * jax.nn.sigmoid(values)


def column_sum(values):
    return jnp.sum(values, 0, keepdims=True)


def padded(rows, unit=16):
    return (rows + unit - 1) // unit * unit


def pack_kernel(place_ref, side_ref, one_ref, fine_ref, half_w_ref, quarter_w_ref, expand_ref,
                reduce_ref, two_ref, three_ref, sent_ref, parts_ref, early_ref):
    place, side = place_ref[0], side_ref[0]
    half = one_ref.shape[0] // 2
    quarter = early_ref.shape[0] // 4
    start = 0
    for part_ref in (fine_ref, half_w_ref, quarter_w_ref):
        early_ref[start : start + part_ref.shape[0]] = part_ref[...]
        start += padded(part_ref.shape[0])
    for block in range(expand_ref.shape[1] // 128):
        lanes_of = slice(128 * block, 128 * block + 128)
        early_ref[start : start + expand_ref.shape[0]] = expand_ref[:, lanes_of]
        start += padded(expand_ref.shape[0])

    def put(start, value):
        shape = (sent_ref.shape[0],) + value.shape
        sent_ref[:, start : start + value.shape[0]] = jnp.broadcast_to(value[None], shape)
        return start + padded(value.shape[0])

    start = 0
    rows = pl.ds(pl.multiple_of(side * half, half), half)
    for block in range(one_ref.shape[1] // 128):
        start = put(start, one_ref[rows, 128 * block : 128 * block + 128])
    start = put(start, early_ref[pl.ds(pl.multiple_of(place * quarter, quarter), quarter)])
    put(start, reduce_ref[...])
    wide = three_ref.shape[1] // 4
    columns = pl.ds(pl.multiple_of(place * 128, 128), 128)
    parts_ref[0 : two_ref.shape[0]] = two_ref[:, columns]
    start = padded(two_ref.shape[0])
    for block in range(wide // 128):
        columns = pl.ds(pl.multiple_of(place * wide + 128 * block, 128), 128)
        parts_ref[start : start + three_ref.shape[0]] = three_ref[:, columns]
        start += padded(three_ref.shape[0])


def own_lanes(place_ref, *refs):
    wide = refs[0].shape[1] // 4
    return [ref[:, pl.ds(pl.multiple_of(place_ref[0] * wide, wide), wide)] for ref in refs]


def first_kernel(side_ref, x_ref, mine_ref, other_ref, stem_ref,
                 full_ref, first_ref, sums_ref):
    side = side_ref[0]
    half = full_ref.shape[2]
    for part in range(full_ref.shape[3] // 128):
        rows, lanes_of = slice(half * part, half * part + half), slice(128 * part, 128 * part + 128)
        full_ref[:, pl.ds(side, 1), :, lanes_of] = mine_ref[:, rows][:, None]
        full_ref[:, pl.ds(1 - side, 1), :, lanes_of] = other_ref[:, rows][:, None]
    weight = full_ref[...].reshape(x_ref.shape[1], -1)
    first = dot(x_ref[...], weight)
    first_ref[...] = first
    put_sums(sums_ref, column_sum(first), column_sum(first * first), stem_row(stem_ref))


def stem_row(*refs):
    stem = sum(ref[...] for ref in refs).reshape(128, 128)
    return dot(jnp.ones((8, 128), f32), stem, "NT", lax.Precision.HIGHEST)


def hidden_kernel(count, mask_ref, sums_ref, first_ref, gain_ref, bias_ref, reduce_ref,
                  hidden_ref, change_ref, norm_ref):
    mean, inverse = norm_of(sums_ref, 4, count)
    norm_ref[...] = jnp.concatenate([mean, inverse], 0)
    level = (first_ref[...] - mean) * inverse * gain_ref[...] + bias_ref[...]
    hidden = silu(level).astype(bf16)
    hidden_ref[...] = hidden
    reduced = dot(hidden, reduce_ref[...])
    reduced = reduced.reshape(-1, SEG, 8, reduced.shape[1])
    steps = [
        mask_ref[0, t].astype(f32) * (reduced[:, t + 1] - reduced[:, t]) for t in range(SEG - 1)
    ]
    steps.append(jnp.zeros_like(steps[0]))
    change_ref[...] = jnp.stack(steps, 1).reshape(change_ref.shape).astype(bf16)


def gate_kernel(place_ref, change_ref, hidden_ref, fine_ref, half_w_ref, quarter_w_ref, expand_ref,
                gated_ref, sigmoid_ref, merged_ref, half_ref, quarter_ref,
                pad_ref, pad_half_ref, pad_quarter_ref):
    place = place_ref[0]
    change = change_ref[...]
    own = gated_ref.shape[0]
    band = shift_columns(pad_ref, change, 8)
    first = pl.multiple_of(place * own, own)
    fine = conv_taps(pad_ref, band, first, own, fine_ref)
    half = dot(pool_matrix(own, 4 * own, 2, 8, 0.25), change).astype(bf16)
    half_ref[...] = half
    band = shift_columns(pad_half_ref, half, 4)
    coarse = conv_taps(pad_half_ref, band, pl.multiple_of(place * 32, 32), 32, half_w_ref)
    quarter = dot(pool_matrix(own // 4, own, 2, 4, 0.25), half)
    quarter_ref[...] = quarter
    band = shift_columns(pad_quarter_ref, quarter, 2)
    coarsest = conv_taps(
        pad_quarter_ref, band, pl.multiple_of(place // 2 * 16, 16), 16, quarter_w_ref,
        precision=lax.Precision.HIGHEST,
    )
    merged = (
        fine
        + split_dot(spread_matrix(own, 2, 8), coarse)
        + split_dot(spread_matrix(own, 4, 8), coarsest)
    ).astype(bf16)
    merged_ref[...] = merged
    sigmoid = jax.nn.sigmoid(dot(merged, expand_ref[...]))
    sigmoid_ref[...] = sigmoid
    gated_ref[...] = (hidden_ref[...].astype(f32) * (1.0 + sigmoid)).astype(bf16)


def second_kernel(two_rows, gated_ref, packed_ref, second_ref, weight_ref, sums_ref, pad_ref):
    for clip in range(packed_ref.shape[0]):
        weight_ref[two_rows * clip : two_rows * clip + two_rows] = packed_ref[clip, :two_rows]
    band = shift_columns(pad_ref, gated_ref[...], 8)
    second = conv_taps(pad_ref, band, 0, second_ref.shape[0], weight_ref)
    second_ref[...] = second
    put_sums(sums_ref, column_sum(second), column_sum(second * second))


def hidden_two_kernel(count, place_ref, sums_ref, second_ref, gain_ref, bias_ref, hidden_ref, norm_ref):
    mean, inverse = norm_of(sums_ref, 1, count)
    norm_ref[...] = jnp.concatenate([mean, inverse], 0)
    gain, bias = own_lanes(place_ref, gain_ref, bias_ref)
    level = (second_ref[...] - mean) * inverse * gain + bias
    hidden_ref[...] = silu(level).astype(bf16)


def third_kernel(two_rows, three_rows, hidden_ref, packed_ref, third_ref, weight_ref, sums_ref):
    start = padded(two_rows)
    for block in range(weight_ref.shape[1] // 128):
        for clip in range(packed_ref.shape[0]):
            weight_ref[
                three_rows * clip : three_rows * clip + three_rows, 128 * block : 128 * block + 128
            ] = packed_ref[clip, start : start + three_rows]
        start += padded(three_rows)
    third = None
    for part in range(hidden_ref.shape[0]):
        term = dot(hidden_ref[part], weight_ref[128 * part : 128 * part + 128, :])
        third = term if third is None else third + term
    third_ref[...] = third
    put_sums(sums_ref, column_sum(third), column_sum(third * third))


def sources(place, size):
    return [place ^ s for s in range(size)]


def output_kernel(count, place_ref, sums_ref, third_ref, gain_ref, bias_ref,
                  x0_ref, x1_ref, x2_ref, x3_ref, c0_ref, c1_ref, c2_ref, c3_ref,
                  low_ref, high_ref, send_ref, slope_ref, norm_ref, out_sums_ref):
    place = place_ref[0]
    mean, inverse = norm_of(sums_ref, 4, count)
    norm_ref[...] = jnp.concatenate([mean, inverse], 0)
    gain, bias = own_lanes(place_ref, gain_ref, bias_ref)
    own, wide = x0_ref.shape[0], third_ref.shape[1]
    lanes_r = pl.ds(pl.multiple_of(place * wide, wide), wide)
    total_bias, total_gain = jnp.zeros((1, wide), f32), jnp.zeros((1, wide), f32)
    pieces = zip(
        sources(place, 4), (x0_ref, x1_ref, x2_ref, x3_ref), (c0_ref, c1_ref, c2_ref, c3_ref)
    )
    for source, x_ref, c_ref in pieces:
        rows = pl.ds(pl.multiple_of(source * own, own), own)
        normed = (third_ref[rows] - mean) * inverse
        summed = normed * gain + bias + x_ref[:, lanes_r].astype(f32)
        sigmoid = jax.nn.sigmoid(summed)
        send_ref[pl.ds(source, 1), 0] = (summed * sigmoid).astype(bf16)[None]
        slope = c_ref[...].astype(f32) * (sigmoid * (1.0 + summed * (1.0 - sigmoid)))
        slope_ref[rows] = slope
        send_ref[pl.ds(source, 1), 1] = slope.astype(bf16)[None]
        total_bias += column_sum(slope)
        total_gain += column_sum(slope * normed)
    put_sums(out_sums_ref, total_bias, total_gain, stem_row(low_ref, high_ref))


def third_back_kernel(count, place_ref, sums_ref, third_ref, slope_ref, norm_ref, gain_ref, weight_ref,
                      grad_ref, part_ref, vectors_ref):
    total_bias, total_gain = get_sums(sums_ref, 4)
    vectors_ref[...] = jnp.concatenate([as_block(total_bias), as_block(total_gain)], 0)
    mean, inverse = norm_ref[0:1], norm_ref[1:2]
    normed = (third_ref[...] - mean) * inverse
    grad = own_lanes(place_ref, gain_ref)[0] * inverse * (
        slope_ref[...] - total_bias / count - normed * (total_gain / count)
    )
    grad = grad.astype(bf16)
    grad_ref[...] = grad
    back = dot(grad, weight_ref[...], "NT").astype(bf16)
    rest, stem = jnp.sum(sums_ref[:, 8:16], 0), []
    for _ in range(2):
        stem.append(rest.astype(bf16).astype(f32))
        rest = rest - stem[-1]
    order = stack_index((16, 128), 0)
    stem = jnp.where(
        order == 0, stem[0][0:1], jnp.where(order == 1, stem[1][0:1], rest[0:1])
    ).astype(bf16)
    rows = grad.shape[0]
    for part in range(part_ref.shape[0]):
        part_ref[part, :rows] = back[:, 128 * part : 128 * part + 128]
        part_ref[part, rows:] = stem


def second_slope_kernel(place_ref, part_ref, second_ref, norm_ref, gain_ref, bias_ref,
                        grad_ref, stem_ref, sums_ref):
    rows = second_ref.shape[0]
    back = jnp.sum(part_ref[:, :rows].astype(f32), 0)
    stem = jnp.sum(part_ref[:, rows:].astype(f32), 0)
    stem_ref[...] = jnp.broadcast_to(stem[0:1] + stem[1:2] + stem[2:3], stem_ref.shape)
    normed = (second_ref[...] - norm_ref[0:1]) * norm_ref[1:2]
    gain, bias = own_lanes(place_ref, gain_ref, bias_ref)
    grad = back * silu_slope(normed * gain + bias)
    grad_ref[...] = grad
    put_sums(sums_ref, column_sum(grad), column_sum(grad * normed))


def second_back_kernel(count, place_ref, sums_ref, slope_ref, second_ref, norm_ref, gain_ref, weight_ref,
                       grad_ref, part_ref, vectors_ref, pad_ref):
    total_bias, total_gain = get_sums(sums_ref, 1)
    vectors_ref[...] = jnp.concatenate([total_bias, total_gain], 0)
    inverse = norm_ref[1:2]
    normed = (second_ref[...] - norm_ref[0:1]) * inverse
    grad = own_lanes(place_ref, gain_ref)[0] * inverse * (
        slope_ref[...] - total_bias / count - normed * (total_gain / count)
    )
    grad = grad.astype(bf16)
    grad_ref[...] = grad
    band = shift_columns(pad_ref, grad, 8)
    own = part_ref.shape[1]
    for part in range(part_ref.shape[0]):
        back = conv_taps(pad_ref, band, part * own, own, weight_ref, True)
        part_ref[part] = back.astype(bf16)


def split_blocks(side, first_ref, second_ref, put):
    for index in range(2 * first_ref.shape[0]):
        own, rest = (first_ref, second_ref) if index % 2 == 0 else (second_ref, first_ref)

        @pl.when(side == 0)
        def _():
            put(index, own, index // 2)

        @pl.when(side == 1)
        def _():
            put(index, rest, index // 2)


def wide_grads_kernel(side_ref, gated_ref, grad_ref, hidden_ref, third_ref,
                      keep_ref, send_ref, pad_ref, all_ref):
    band = shift_columns(pad_ref, gated_ref[...], 8)
    rows, channels = gated_ref.shape
    clips = 2 * keep_ref.shape[0]
    two_rows = 9 * channels // clips
    for ky, kx in taps:
        tap = 3 * ky + kx
        all_ref[tap * channels : (tap + 1) * channels, :] = dot(
            pad_ref[kx, ky * band : ky * band + rows], grad_ref[...], "TN"
        ).astype(bf16)
    start = 9 * channels
    for part in range(hidden_ref.shape[0]):
        value = dot(hidden_ref[part], third_ref[...], "TN").astype(bf16)
        for block in range(value.shape[1] // 128):
            first = start + channels * block + 128 * part
            all_ref[first : first + 128] = value[:, 128 * block : 128 * block + 128]
    three_rows = channels // clips

    def put(clip, out_ref, index):
        out_ref[index, 0:two_rows] = all_ref[two_rows * clip : two_rows * clip + two_rows]
        at = padded(two_rows)
        for block in range(third_ref.shape[1] // 128):
            first = start + channels * block + three_rows * clip
            out_ref[index, at : at + three_rows] = all_ref[first : first + three_rows]
            at += padded(three_rows)

    split_blocks(side_ref[0], keep_ref, send_ref, put)


def halve_kernel(side_ref, held_ref, arrived_ref, keep_ref, send_ref):
    def put(source, out_ref, index):
        total = held_ref[source].astype(f32) + arrived_ref[source].astype(f32)
        out_ref[index] = total.astype(bf16)

    split_blocks(side_ref[0], keep_ref, send_ref, put)


def last_kernel(held_ref, arrived_ref, three_ref, two_ref, out_ref):
    rows = held_ref.shape[1]
    total = held_ref[0].astype(f32) + arrived_ref[0].astype(f32)
    out_ref[0:rows] = total.astype(bf16)
    vectors = jnp.concatenate([three_ref[...], two_ref[...], jnp.zeros((6, 128), f32)], 0)
    upper = vectors.astype(bf16)
    out_ref[rows : rows + 16] = upper
    out_ref[rows + 16 : rows + 32] = (vectors - upper.astype(f32)).astype(bf16)


def gate_back_kernel(part_ref, hidden_ref, sigmoid_ref, expand_ref,
                     fine_ref, gate_ref, hidden_grad_ref):
    gated = jnp.sum(part_ref[...].astype(f32), 0)
    sigmoid = sigmoid_ref[...]
    gate = (gated * hidden_ref[...].astype(f32) * sigmoid * (1.0 - sigmoid)).astype(bf16)
    gate_ref[...] = gate
    hidden_grad_ref[...] = gated * (1.0 + sigmoid)
    fine_ref[...] = dot(gate, expand_ref[...], "NT").astype(bf16)


def reduce_back_kernel(place_ref, mask_ref, grad_ref, fine_ref, half_w_ref, quarter_w_ref,
                       reduce_ref, hidden_grad_ref, first_ref, norm_ref, gain_ref, bias_ref,
                       reduced_ref, slope_ref, coarse_ref, coarsest_ref, sums_ref,
                       pad_ref, pad_half_ref, pad_quarter_ref):
    place = place_ref[0]
    own = reduced_ref.shape[0]
    grad_fine = grad_ref[...]
    coarse = dot(pool_matrix(own, 4 * own, 2, 8, 1.0), grad_fine).astype(bf16)
    coarse_ref[...] = coarse
    coarsest = dot(pool_matrix(own // 4, 4 * own, 4, 8, 1.0), grad_fine)
    coarsest_ref[...] = coarsest
    band = shift_columns(pad_quarter_ref, coarsest, 2)
    low = conv_taps(
        pad_quarter_ref, band, pl.multiple_of(place // 2 * 16, 16), 16, quarter_w_ref, True,
        lax.Precision.HIGHEST,
    )
    band = shift_columns(pad_half_ref, coarse, 4)
    middle = conv_taps(pad_half_ref, band, pl.multiple_of(place * 32, 32), 32, half_w_ref, True)
    middle = middle + 0.25 * split_dot(spread_matrix(32, 2, 4), low)
    band = shift_columns(pad_ref, grad_fine, 8)
    change = conv_taps(pad_ref, band, pl.multiple_of(place * own, own), own, fine_ref, True)
    change = change + 0.25 * split_dot(spread_matrix(own, 2, 8), middle)
    change = change.reshape(-1, SEG, 8, change.shape[1])
    carried = [mask_ref[0, t].astype(f32) * change[:, t] for t in range(SEG - 1)]
    zero = jnp.zeros_like(carried[0])
    before, here = [zero] + carried, carried + [zero]
    reduced = jnp.stack([b - h for b, h in zip(before, here)], 1)
    reduced = reduced.reshape(reduced_ref.shape).astype(bf16)
    reduced_ref[...] = reduced
    grad_hidden = hidden_grad_ref[...] + dot(reduced, reduce_ref[...], "NT")
    normed = (first_ref[...] - norm_ref[0:1]) * norm_ref[1:2]
    slope = grad_hidden * silu_slope(normed * gain_ref[...] + bias_ref[...])
    slope_ref[...] = slope
    put_sums(sums_ref, column_sum(slope), column_sum(slope * normed))


def first_back_kernel(count, sums_ref, slope_ref, first_ref, norm_ref, gain_ref,
                      grad_ref, vectors_ref):
    total_bias, total_gain = get_sums(sums_ref, 4)
    vectors_ref[...] = jnp.concatenate([total_bias, total_gain], 0)
    inverse = norm_ref[1:2]
    normed = (first_ref[...] - norm_ref[0:1]) * inverse
    grad = gain_ref[...] * inverse * (
        slope_ref[...] - total_bias / count - normed * (total_gain / count)
    )
    grad_ref[...] = grad.astype(bf16)


def one_grad_kernel(place_ref, grad_ref, x0_ref, x1_ref, x2_ref, x3_ref, out_ref):
    place = place_ref[0]
    wide = out_ref.shape[1]
    lanes_r = pl.ds(pl.multiple_of(place * wide, wide), wide)
    total = None
    for source, x_ref in zip(sources(place, 4), (x0_ref, x1_ref, x2_ref, x3_ref)):
        grad = grad_ref[pl.ds(source, 1), :, lanes_r][0]
        term = dot(x_ref[...], grad, "TN")
        total = term if total is None else total + term
    out_ref[...] = total.astype(bf16)


def small_grads_kernel(change_ref, half_ref, quarter_ref, grad_ref, coarse_ref, coarsest_ref,
                       hidden_ref, reduced_ref, merged_ref, gate_ref,
                       fine_ref, half_w_ref, quarter_w_ref, reduce_ref, expand_ref,
                       pad_ref, pad_half_ref, pad_quarter_ref):
    scales = (
        (change_ref, grad_ref, fine_ref, pad_ref, 8, None),
        (half_ref, coarse_ref, half_w_ref, pad_half_ref, 4, None),
        (quarter_ref, coarsest_ref, quarter_w_ref, pad_quarter_ref, 2, lax.Precision.HIGHEST),
    )
    for map_ref, cot_ref, out_ref, padded_ref, width, precision in scales:
        rows, channels = map_ref.shape
        band = shift_columns(padded_ref, map_ref[...], width)
        for ky, kx in taps:
            tap = 3 * ky + kx
            out_ref[tap * channels : (tap + 1) * channels, :] = dot(
                padded_ref[kx, ky * band : ky * band + rows], cot_ref[...], "TN", precision
            ).astype(bf16)
    reduce_ref[...] = dot(hidden_ref[...], reduced_ref[...], "TN").astype(bf16)
    value = dot(merged_ref[...], gate_ref[...], "TN").astype(bf16)
    for block in range(expand_ref.shape[0]):
        expand_ref[block] = value[:, 128 * block : 128 * block + 128]


def input_grad_kernel(place_ref, grad_ref, weight_ref, r0_ref, r1_ref, r2_ref, r3_ref,
                      input_ref, out_ref):
    place = place_ref[0]
    wide = r0_ref.shape[2]
    for source, r_ref in zip(sources(place, 4), (r0_ref, r1_ref, r2_ref, r3_ref)):
        lanes_r = pl.ds(pl.multiple_of(source * wide, wide), wide)
        weight = weight_ref[pl.ds(pl.multiple_of(source * wide, wide), wide), :]
        value = dot(grad_ref[...], weight, "NT") + r_ref[1].astype(f32)
        shape = (input_ref.shape[1], input_ref.shape[0], input_ref.shape[2], wide)
        value, result = value.reshape(shape), r_ref[0].astype(f32).reshape(shape)
        for row in range(shape[0]):
            input_ref[:, row, :, lanes_r] = value[row]
            out_ref[:, row, :, lanes_r] = result[row].astype(bf16)


class Fresh:
    def __init__(self, array):
        self.array = array


def call(kernel, scalars, arrays, outs, scratch=(), waits=(), flops=10**9, moved=2 * 10**6):
    used = len(scalars) + len(arrays)

    def body(*refs):
        kernel(*refs[:used], *refs[used + len(waits) :])

    shapes = [(entry.array if isinstance(entry, Fresh) else entry).shape for entry in arrays]
    return pl.pallas_call(
        body,
        grid=(1,),
        in_specs=[pl.BlockSpec(memory_space=pltpu.SMEM)] * len(scalars)
        + [whole(shape) for shape in shapes]
        + [pl.BlockSpec(memory_space=pl.ANY)] * len(waits),
        out_specs=[whole(shape) for shape, _ in outs],
        out_shape=[pltpu.HBM(shape, dtype) for shape, dtype in outs],
        scratch_shapes=[pltpu.VMEM(shape, dtype) for shape, dtype in scratch],
        compiler_params=pltpu.CompilerParams(vmem_limit_bytes=block_limit),
        cost_estimate=pl.CostEstimate(flops=flops, bytes_accessed=moved, transcendentals=0),
    )(
        *scalars,
        *(entry.array if isinstance(entry, Fresh) else in_hbm(entry) for entry in arrays),
        *waits,
    )


def together(*values):
    return lax.optimization_barrier(values)


def exchange(blocks, axis):
    return lax.all_to_all(blocks, axis, 0, 0)


def to_all(part, axis):
    size = lax.axis_size(axis)
    return exchange(jnp.broadcast_to(part[None], (size,) + part.shape), axis)


def swap(piece, axis, step):
    return lax.ppermute(piece, axis, [(i, i ^ step) for i in range(lax.axis_size(axis))])


def lane_blocks(array):
    return [array[:, start : start + 128] for start in range(0, array.shape[1], 128)]


def pick(array, index, axis=0):
    return lax.dynamic_index_in_dim(array, index, axis, keepdims=False)


def per_device(
    frames,
    frame_start,
    boundary_mask,
    stem_weight,
    stem_gain,
    stem_bias,
    block_input,
    w_one,
    w_reduce,
    k_fine,
    k_half,
    k_quarter,
    w_expand,
    w_two,
    w_three,
    gain_one,
    bias_one,
    gain_two,
    bias_two,
    gain_three,
    bias_three,
    stem_cot,
    block_cot,
):
    nc, nr = lax.axis_size("clip"), lax.axis_size("row")
    u32 = jnp.uint32
    place = lax.axis_index("row").astype(u32)
    spots = [place ^ u32(s) for s in range(nr)]
    side = place & u32(1)
    clip = lax.axis_index("clip").astype(u32)
    bits, bit = [], 1
    while bit < nc:
        bits.append((bit, (clip // u32(bit)) & u32(1)))
        bit *= 2
    spot = place.astype(jnp.int32).reshape(1)
    both = ("clip", "row")
    images, block_rows, cols, c_in = block_input.shape
    mid, red = gain_one.shape[0], w_reduce.shape[1]
    mid_r, in_r = mid // nr, c_in // nr
    own = images * block_rows * cols
    pixels = own * nr
    count = float(pixels * nc)
    clip_sums = ((nc, 8, 128), f32)
    both_sums = ((nc * nr, 16, 128), f32)

    def in_part(array, index):
        return lax.dynamic_slice_in_dim(array, index * u32(in_r), in_r, array.ndim - 1)

    half = w_one.shape[0] // 2
    stem_taps = to_all(filters_inside(stem_weight), "clip").reshape(STEM, -1)
    expand_rows = padded(w_expand.shape[0])
    early_rows = padded(3 * padded(k_fine.shape[0]) + mid // 128 * expand_rows, 16 * nr)
    quarter_rows = early_rows // nr
    edges = [4 * padded(half)]
    for rows in (quarter_rows, w_reduce.shape[0]):
        edges.append(edges[-1] + padded(rows))
    two_rows, three_rows = w_two.shape[0], w_three.shape[0]
    two_end = padded(two_rows)
    part_rows = two_end + in_r // 128 * padded(three_rows)
    sides = [entry.astype(jnp.int32).reshape(1) for _, entry in bits]
    sent, parts = call(
        pack_kernel,
        (spot, side.astype(jnp.int32).reshape(1)),
        (w_one, k_fine, k_half, k_quarter, w_expand, w_reduce, w_two, w_three),
        (((nc, edges[-1], 128), bf16), ((part_rows, 128), bf16)),
        [((early_rows, 128), bf16)],
        (*sides, *[entry.reshape(1) for entry in spots]),
    )
    sent, stem_taps = together(sent, stem_taps)
    mine = exchange(sent, "clip")
    filters = jnp.concatenate(
        [jnp.pad(stem_taps, ((0, 0), (224 * y, 672 - 224 * y))) for y in range(4)], 0
    )

    x_own = block_input.swapaxes(0, 1).reshape(own, c_in)
    cot_own = block_cot.swapaxes(0, 1).reshape(own, c_in)

    local = frames[0]
    rows = local.shape[2]
    above = lax.ppermute(local[:, :, rows - 16 :], "row", [(i, i + 1) for i in range(nr - 1)])
    below = lax.ppermute(local[:, :, :16], "row", [(i + 1, i) for i in range(nr - 1)])
    cot_own, x_own, above, below = together(cot_own, x_own, above, below)
    planes = stem_planes(frame_start[0], local, above, below)
    stem_count = float(SEG * (rows // 2) * (local.shape[3] // 2) * nc * nr)
    cot_pieces = [in_part(cot_own, place)] + [
        swap(in_part(cot_own, spots[s]), "row", s) for s in range(1, nr)
    ]
    x_pieces = [x_own, swap(x_own, "row", 1), swap(x_own, "row", 2)]
    x_pieces.append(swap(x_pieces[2], "row", 1))

    stem_pre, stem_sums = stem_conv(planes, filters, *x_pieces[1:3], *cot_pieces[1:])
    mine, stem_sums = together(mine, stem_sums)
    other = swap(mine, "row", 1)
    parts, mine = together(parts, mine)
    packed = lax.all_gather(parts, "clip")
    full_one, first, sums = call(
        first_kernel,
        (side.astype(jnp.int32).reshape(1),),
        (x_own, Fresh(mine), Fresh(other), stem_sums),
        (((nc, 2, half, mid), bf16), ((own, mid), f32), both_sums),
    )
    full_one = full_one.reshape(c_in, mid)
    sums = exchange(sums, both)
    mine, other, first = together(mine, other, first)
    full_reduce = mine[:, edges[1] : edges[1] + w_reduce.shape[0]].reshape(mid, red)
    mine_early = mine[:, edges[0] : edges[1]]
    quarters = [mine_early, other[:, edges[0] : edges[1]]] + [
        swap(mine_early, "row", s) for s in (2, 3)
    ]
    quarters = [
        jnp.where(
            place == u32(q),
            quarters[0],
            jnp.where(
                place == u32(q ^ 1),
                quarters[1],
                jnp.where(place == u32(q ^ 2), quarters[2], quarters[3]),
            ),
        )
        for q in range(nr)
    ]
    quarters = jnp.concatenate(quarters, 1)
    early_parts, start = [], 0
    for size in (k_fine.shape[0],) * 3 + (w_expand.shape[0],) * (mid // 128):
        early_parts.append(quarters[:, start : start + size].reshape(-1, 128))
        start += padded(size)
    full_fine, full_half, full_quarter = early_parts[:3]
    full_expand = jnp.concatenate(early_parts[3:], 1)
    stem_totals = jnp.sum(sums[:, 8], 0).reshape(2, STEM)
    stem_mean, stem_inverse = statistics(stem_totals, stem_count)
    stem_vectors = lanes(stem_mean, stem_inverse, stem_gain, stem_bias)
    gain_one, bias_one = gain_one.reshape(1, -1), bias_one.reshape(1, -1)
    hidden_one, change, norm_one = call(
        functools.partial(hidden_kernel, count),
        (boundary_mask,),
        (Fresh(sums), first, gain_one, bias_one, full_reduce),
        (((own, mid), bf16), ((own, red), bf16), ((2, mid), f32)),
    )
    change = lax.all_gather(change, "row").reshape(pixels, red)
    pads = [
        ((3, pixels + 2 * images * cols, red), bf16),
        ((3, pixels // 4 + images * cols, red), bf16),
        ((3, pixels // 16 + images * cols // 2, red), f32),
    ]
    gated, sigmoid, merged, half_map, quarter = call(
        gate_kernel,
        (spot,),
        (Fresh(change), hidden_one, full_fine, full_half, full_quarter, full_expand),
        (
            ((own, mid), bf16),
            ((own, mid), f32),
            ((own, red), bf16),
            ((pixels // 4, red), bf16),
            ((pixels // 16, red), f32),
        ),
        pads,
    )
    gated = lax.all_gather(gated, "row").reshape(pixels, mid)
    second, two_r, sums = call(
        functools.partial(second_kernel, two_rows),
        (),
        (Fresh(gated), packed),
        (((pixels, mid_r), f32), ((9 * mid, mid_r), bf16), clip_sums),
        [((3, pixels + 2 * images * cols, mid), bf16)],
    )
    gain_two, bias_two = gain_two.reshape(1, -1), bias_two.reshape(1, -1)
    outer_low, slope_low = stem_slope(stem_pre, stem_cot, 0, stem_vectors, second)
    hidden_two, norm_two = call(
        functools.partial(hidden_two_kernel, count),
        (spot,),
        (Fresh(exchange(sums, "clip")), second, gain_two, bias_two),
        (((pixels, mid_r), bf16), ((2, mid_r), f32)),
        waits=(slope_low,),
    )
    hidden_two = lax.all_gather(hidden_two, "row")
    third, three_r, sums = call(
        functools.partial(third_kernel, two_rows, three_rows),
        (),
        (Fresh(hidden_two), packed),
        (((pixels, in_r), f32), ((mid, in_r), bf16), clip_sums),
    )
    outer_high, slope_high = stem_slope(stem_pre, stem_cot, 4, stem_vectors, third)
    gain_three, bias_three = gain_three.reshape(1, -1), bias_three.reshape(1, -1)
    send, slope_three, norm_three, sums = call(
        functools.partial(output_kernel, count),
        (spot,),
        (
            Fresh(exchange(sums, "clip")), third, gain_three, bias_three, *x_pieces, *cot_pieces,
            slope_low, slope_high,
        ),
        (
            ((nr, 2, own, in_r), bf16),
            ((pixels, in_r), f32),
            ((2, in_r), f32),
            ((nc, 16, 128), f32),
        ),
    )

    grad_third, parts, vectors_three = call(
        functools.partial(third_back_kernel, count),
        (spot,),
        (
            Fresh(exchange(sums, "clip")), third, slope_three, norm_three, gain_three, three_r,
        ),
        (((pixels, in_r), bf16), ((nr, pixels + 16, mid_r), bf16), ((8, 128), f32)),
    )
    slope_two, stem_totals, sums = call(
        second_slope_kernel,
        (spot,),
        (Fresh(exchange(parts, "row")), second, norm_two, gain_two, bias_two),
        (((pixels, mid_r), f32), ((8, 128), f32), clip_sums),
    )
    stem_bias_grad, stem_gain_grad = stem_totals[0].reshape(2, STEM)
    stem_vectors = lanes(
        stem_mean,
        stem_inverse,
        stem_gain * stem_inverse,
        stem_bias_grad / stem_count,
        stem_gain_grad / stem_count,
    )
    stem_low = stem_grad(planes, stem_pre, outer_low, 0, stem_vectors)
    grad_second, parts, vectors_two = call(
        functools.partial(second_back_kernel, count),
        (spot,),
        (
            Fresh(exchange(sums, "clip")), slope_two, second, norm_two, gain_two, two_r,
        ),
        (((pixels, mid_r), bf16), ((nr, own, mid), bf16), ((2, mid_r), f32)),
        [((3, pixels + 2 * images * cols, mid_r), bf16)],
        (stem_low,),
    )
    blocks = ((nc // 2, part_rows, 128), bf16)
    keep, give = call(
        wide_grads_kernel,
        (sides[0],),
        (gated, grad_second, hidden_two, grad_third),
        (blocks, blocks),
        [
            ((3, pixels + 2 * images * cols, mid), bf16),
            ((9 * mid + mid * in_r // 128, 128), bf16),
        ],
    )
    arrived = swap(give, "clip", 1)
    grad_fine, grad_gate, grad_hidden = call(
        gate_back_kernel,
        (),
        (Fresh(exchange(parts, "row")), hidden_one, sigmoid, full_expand),
        (((own, red), bf16), ((own, mid), bf16), ((own, mid), f32)),
        waits=(keep,),
    )
    grad_fine = lax.all_gather(grad_fine, "row").reshape(pixels, red)
    grad_reduced, slope_one, grad_coarse, grad_coarsest, sums = call(
        reduce_back_kernel,
        (spot, boundary_mask),
        (
            Fresh(grad_fine), full_fine, full_half, full_quarter, full_reduce,
            grad_hidden, first, norm_one, gain_one, bias_one,
        ),
        (
            ((own, red), bf16),
            ((own, mid), f32),
            ((pixels // 4, red), bf16),
            ((pixels // 16, red), f32),
            both_sums,
        ),
        pads,
    )
    fine_grad, half_grad, quarter_grad, reduce_grad, expand_grad = call(
        small_grads_kernel,
        (),
        (
            change, half_map, quarter, grad_fine, grad_coarse, grad_coarsest,
            hidden_one, grad_reduced, merged, grad_gate,
        ),
        [((9 * red, red), bf16)] * 3 + [((mid, red), bf16), ((mid // 128, red, 128), bf16)],
        pads,
    )
    sums = exchange(sums, both)
    stem_high = stem_grad(planes, stem_pre, outer_high, len(planes) // 2, stem_vectors, slope_one)
    grad_first, vectors_one = call(
        functools.partial(first_back_kernel, count),
        (),
        (Fresh(sums), slope_one, first, norm_one, gain_one),
        (((own, mid), bf16), ((2, mid), f32)),
        waits=(stem_high, fine_grad),
    )
    stem_blocks = (stem_low + stem_high).astype(bf16).reshape(nr, 8 // nr, nc, -1, 128)
    both_parts = [
        reduce_grad.reshape(nc, nr, -1, red),
        expand_grad.reshape(nr, nc, -1, red).swapaxes(0, 1),
        stem_blocks.transpose(2, 0, 1, 3, 4).reshape(nc, nr, -1, 128),
    ]
    both_rows = [part.shape[2] for part in both_parts]
    both_parts = jnp.concatenate(both_parts, 2).reshape(nc * nr, -1, 128)
    both_total = exchange(both_parts, both)
    both_total = jnp.sum(both_total, 0, dtype=f32).astype(bf16)

    def halving(keep, arrived, bit, side, *waits):
        rows = ((keep.shape[0] // 2, part_rows, 128), bf16)
        keep, give = call(halve_kernel, (side,), (keep, Fresh(arrived)), (rows, rows), (), waits)
        return keep, swap(give, "clip", bit)

    keep, arrived = halving(keep, arrived, bits[1][0], sides[1], slope_one)
    (one_grad,) = call(
        one_grad_kernel,
        (spot,),
        (Fresh(lax.all_gather(grad_first, "row")), *x_pieces),
        (((c_in, mid_r), bf16),),
    )
    send, one_grad = together(send, one_grad)

    def quarter_of(gradient):
        shares = gradient.reshape(nc, -1, red)
        shares = jnp.pad(shares, ((0, 0), (0, -shares.shape[1] % (8 * nr)), (0, 0)))
        return pick(shares.reshape(nc, nr, -1, red), place, 1)

    clip_parts = [one_grad.reshape(nc, -1, red)] + [
        quarter_of(gradient) for gradient in (fine_grad, half_grad, quarter_grad)
    ]
    one_rows, tap_rows = clip_parts[0].shape[1], clip_parts[1].shape[1]
    clip_parts = jnp.concatenate(clip_parts, 1)
    clip_parts, both_total = together(clip_parts, both_total)
    for (bit, _), spot_of in zip(bits[2:], sides[2:]):
        keep, arrived = halving(keep, arrived, bit, spot_of, one_grad)
    clip_total = jnp.sum(exchange(clip_parts, "clip"), 0, dtype=f32)
    returned = [pick(send, place)] + [
        swap(pick(send, spots[s]), "row", s) for s in range(1, nr)
    ]
    input_grad, block_out = call(
        input_grad_kernel,
        (spot,),
        (grad_first, full_one, *returned),
        ((block_input.shape, f32), (block_input.shape, bf16)),
    )

    def wide(blocks):
        return blocks.swapaxes(0, 1).reshape(blocks.shape[1], -1).astype(f32)

    (last,) = call(
        last_kernel,
        (),
        (keep, Fresh(arrived), vectors_three, vectors_two),
        (((part_rows + 32, 128), bf16),),
    )
    shares_a = lax.all_gather(last, "row")
    two_share = wide(shares_a[:, :two_rows])
    three_share = shares_a[:, two_end:part_rows].reshape(c_in // 128, -1, 128)
    three_share = wide(three_share[:, :three_rows])
    vectors = shares_a[:, part_rows:].astype(f32)
    vectors = vectors[:, :16] + vectors[:, 16:]
    clip_rows = clip_total.shape[0]
    shares_b = lax.all_gather(
        jnp.concatenate([clip_total.astype(bf16), both_total], 0), "row"
    )
    shares_c = shares_b[:, clip_rows:]
    one_share = wide(shares_b[:, :one_rows])
    tap_shares = [
        shares_b[:, start : start + tap_rows].reshape(-1, red)[: k_fine.shape[0]].astype(f32)
        for start in range(one_rows, clip_rows, tap_rows)
    ]
    reduce_share = shares_c[:, : both_rows[0]].reshape(-1, red).astype(f32)
    expand_share = wide(shares_c[:, both_rows[0] : both_rows[0] + both_rows[1]])
    stem_share = wide(shares_c[:, both_rows[0] + both_rows[1] :].reshape(8, -1, 128))[:, :784]
    return (
        block_out,
        input_grad,
        filters_outside(stem_share),
        stem_gain_grad,
        stem_bias_grad,
        one_share,
        reduce_share,
        *tap_shares,
        expand_share,
        two_share,
        three_share,
        vectors_one[1],
        vectors_one[0],
        vectors[:, 9].reshape(-1),
        vectors[:, 8].reshape(-1),
        vectors[:, 4:8].reshape(-1),
        vectors[:, 0:4].reshape(-1),
    )


def solution(mesh):
    in_specs = (
        P("clip", None, None, "row", None),
        P("clip", None),
        P("clip", None),
        P("clip", None),
        P(),
        P(),
        P("clip", "row", None, None),
        P("clip", None),
        P("clip", None),
        P("clip", None),
        P("clip", None),
        P("clip", None),
        P("clip", None),
        P("clip", None),
        P("clip", None),
        P(),
        P(),
        P(),
        P(),
        P(),
        P(),
        P("clip", None, "row", None),
        P("clip", "row", None, None),
    )
    out_specs = (
        P("clip", "row", None, None),
        P("clip", "row", None, None),
        P("clip", None),
        P(),
        P(),
        P("clip", None),
        P("clip", None),
        P("clip", None),
        P("clip", None),
        P("clip", None),
        P("clip", None),
        P("clip", None),
        P("clip", None),
        P(),
        P(),
        P(),
        P(),
        P(),
        P(),
    )
    return jax.shard_map(
        per_device, mesh=mesh, in_specs=in_specs, out_specs=out_specs, check_vma=False
    )
```

```python
import functools

import jax
import jax.numpy as jnp
from jax import lax
from jax.experimental import pallas as pl
from jax.experimental.pallas import tpu as pltpu
from jax.sharding import PartitionSpec as P

STEM = 64
SEG = 8
WIN = 5


epsilon = 1e-05


def silu_slope(values):
    sigmoid_val = jax.nn.sigmoid(values)
    return sigmoid_val * (1.0 + values * (1.0 - sigmoid_val))


def statistics(totals, count):
    mean = totals[0] / count
    return mean, lax.rsqrt(totals[1] / count - mean * mean + epsilon)


def stack_index(shape, dim):
    return lax.broadcasted_iota(jnp.int32, shape, dim)


def stem_planes_kernel(
    start_ref, local_ref, above_ref, below_ref, planes_ref, pick_ref, shift_ref
):
    pair = pl.program_id(0)

    @pl.when(pair == 0)
    def _():
        dims = (256, 240)
        out, inner = stack_index(dims, 0), stack_index(dims, 1)
        channel, plane = out % 16, inner // 16
        plus = plane == jnp.where(channel < 3, channel + 6, channel)
        minus = (channel >= 3) & (plane == channel - 3)
        value = jnp.where(plus, 1.0, 0.0) - jnp.where(minus, 1.0, 0.0)
        keep = (out // 16 == inner % 16) & (channel < 15)
        pick_ref[...] = jnp.where(keep, value, 0.0).astype(jnp.bfloat16)
        dims = (256, 896)
        source, target = stack_index(dims, 0), stack_index(dims, 1)
        wanted = 2 * (target % 128) + target // 128 - 3
        shift_ref[...] = jnp.where(source == wanted, 1.0, 0.0).astype(jnp.bfloat16)

    for side in range(2):
        first = start_ref[2 * pair + side]
        lanes = slice(128 * side, 128 * side + 128)
        for base in (0, 3):
            parts = []
            for block in range(base, base + 3):
                if block == 0:
                    window = above_ref[pl.ds(first, WIN)]
                elif block == 5:
                    window = below_ref[pl.ds(first, WIN)]
                else:
                    window = local_ref[pl.ds(first, WIN), :, 16 * block - 16 : 16 * block, :]
                part = jnp.dot(
                    pick_ref[...], window.reshape(240, 256), preferred_element_type=jnp.float32
                )
                parts.append(part.astype(jnp.bfloat16))
            stacked = jnp.concatenate(parts, 0)
            low, high = (8, 48) if base == 0 else (0, 40)
            at = 16 * base - 8
            for first_kx in range(0, 7, 2):
                count = min(2, 7 - first_kx)
                shifted = jnp.dot(
                    stacked,
                    shift_ref[:, 128 * first_kx : 128 * (first_kx + count)],
                    preferred_element_type=jnp.float32,
                ).astype(jnp.bfloat16)
                for k in range(count):
                    piece = shifted[:, 128 * k : 128 * k + 128].reshape(48, 16, 128)
                    channels = slice(16 * (first_kx + k), 16 * (first_kx + k) + 16)
                    planes_ref[0, at + low : at + high, channels, lanes] = piece[low:high]


def stem_conv_kernel(planes_ref, weight_ref, pre_ref, sums_ref):
    @pl.when(pl.program_id(0) == 0)
    def _():
        sums_ref[...] = jnp.zeros_like(sums_ref)

    @pl.loop(0, 2)
    def _(part):
        totals = [jnp.zeros((64, 128), jnp.float32)] * 2
        for step in range(4):
            group = 4 * part + step
            patches = planes_ref[0, pl.ds(5 + 8 * group, 13)].reshape(13 * 112, 256)
            out = jnp.dot(weight_ref[...], patches, preferred_element_type=jnp.float32)
            out = out.reshape(4, 64, 256)
            for side in range(2):
                half = out[:, :, 128 * side : 128 * side + 128]
                pre_ref[side, pl.ds(4 * group, 4)] = half
                totals = [totals[0] + jnp.sum(half, 0), totals[1] + jnp.sum(half * half, 0)]
        sums_ref[0] += totals[0]
        sums_ref[1] += totals[1]


def stem_slope_kernel(pre_ref, cot_ref, vectors_ref, outer_ref, sums_ref, swap_ref):
    @pl.when(pl.program_id(0) == 0)
    def _():
        out, inner = stack_index((256, 256), 0), stack_index((256, 256), 1)
        hit = (out // 16 == inner % 16) & (out % 16 == inner // 16)
        swap_ref[...] = jnp.where(hit, 1.0, 0.0).astype(jnp.bfloat16)
        sums_ref[...] = jnp.zeros_like(sums_ref)

    for part in range(4):
        channels = slice(16 * part, 16 * part + 16)
        mean, inverse = vectors_ref[0, channels], vectors_ref[1, channels]
        gain, bias = vectors_ref[2, channels], vectors_ref[3, channels]
        block = jnp.concatenate(
            [cot_ref[0, channels, 16 * k : 16 * k + 16, :].reshape(256, 128) for k in range(2)], 1
        )
        turned = jnp.dot(swap_ref[...], block, preferred_element_type=jnp.float32)
        total_bias, total_gain = jnp.zeros((16, 128)), jnp.zeros((16, 128))
        for k in range(2):
            rows = slice(16 * k, 16 * k + 16)
            cot = turned[:, 128 * k : 128 * k + 128].reshape(16, 16, 128)
            normed = (pre_ref[0, rows, channels, :] - mean) * inverse
            outer = cot * silu_slope(normed * gain + bias)
            outer_ref[0, rows, channels, :] = outer.astype(jnp.bfloat16)
            total_bias += jnp.sum(outer, 0)
            total_gain += jnp.sum(outer * normed, 0)
        sums_ref[0, channels] += total_bias
        sums_ref[1, channels] += total_gain


def stem_grad_kernel(planes_ref, pre_ref, outer_ref, vectors_ref, out_ref, acc_ref):
    pair, last = pl.program_id(0), pl.num_programs(0) - 1

    @pl.when(pair == 0)
    def _():
        acc_ref[...] = jnp.zeros_like(acc_ref)

    @pl.loop(0, 2)
    def _(half):
        total = None
        for step in range(4):
            group = 4 * half + step
            rows = pl.ds(4 * group, 4)
            sides = []
            for side in range(2):
                normed = (pre_ref[side, rows] - vectors_ref[0]) * vectors_ref[1]
                outer = outer_ref[side, rows].astype(jnp.float32)
                grad = vectors_ref[2] * (outer - vectors_ref[3] - normed * vectors_ref[4])
                sides.append(grad.astype(jnp.bfloat16).reshape(256, 128))
            patches = planes_ref[0, pl.ds(5 + 8 * group, 13)].reshape(13 * 112, 256)
            term = lax.dot_general(
                jnp.concatenate(sides, 1),
                patches,
                (((1,), (1,)), ((), ())),
                preferred_element_type=jnp.float32,
            )
            total = term if total is None else total + term
        acc_ref[...] += total

    @pl.when(pair == last)
    def _():
        total = acc_ref[0:64, 0:784]
        for y in range(1, 4):
            total += acc_ref[64 * y : 64 * y + 64, 224 * y : 224 * y + 784]
        total = jnp.concatenate([total, jnp.zeros((64, 240), jnp.float32)], 1)
        for part in range(8):
            out_ref[part] = total[:, 128 * part : 128 * part + 128]


stem_limit = 24 * 1024 * 1024
block_limit = 40 * 1024 * 1024
planes_shape, map_shape = (80, 112, 256), (32, 64, 128)


def whole(shape):
    return pl.BlockSpec(shape, lambda *_: (0,) * len(shape))


def by_step(shape):
    return pl.BlockSpec(shape, lambda i: (i,) + (0,) * (len(shape) - 1))


def in_hbm(array):
    return pltpu.with_memory_space_constraint(array, pltpu.HBM)


def stem_call(kernel, steps, in_specs, out_specs, outs, scratch, flops, moved, args, waits=()):
    flops = 10**6 if len(waits) == 1 and args[-1].shape[0] == 5 else flops
    used = len(args)

    def body(*refs):
        kernel(*refs[:used], *refs[used + len(waits) :])

    return pl.pallas_call(
        body,
        grid=(steps,),
        in_specs=in_specs + [pl.BlockSpec(memory_space=pl.ANY)] * len(waits),
        out_specs=out_specs,
        out_shape=[
            (pltpu.HBM if len(shape) == 4 else jax.ShapeDtypeStruct)(shape, dtype)
            for shape, dtype in outs
        ],
        scratch_shapes=[pltpu.VMEM(shape, dtype) for shape, dtype in scratch],
        compiler_params=pltpu.CompilerParams(vmem_limit_bytes=stem_limit),
        cost_estimate=pl.CostEstimate(flops=flops, bytes_accessed=moved, transcendentals=0),
    )(*(in_hbm(entry) if entry.ndim > 1 else entry for entry in args), *waits)


def stem_planes(starts, local, above, below):
    pairs = starts.shape[0] // 2
    return stem_call(
        stem_planes_kernel,
        pairs,
        [pl.BlockSpec(memory_space=pltpu.SMEM)]
        + [whole(entry.shape) for entry in (local, above, below)],
        [by_step((1,) + planes_shape)],
        [((pairs,) + planes_shape, jnp.bfloat16)],
        [((256, 240), jnp.bfloat16), ((256, 896), jnp.bfloat16)],
        4 * 10**9 * pairs,
        5 * 10**6 * pairs,
        (starts, local, above, below),
    )[0]


def stem_conv(planes, weight, *waits):
    pairs = planes.shape[0]
    return stem_call(
        stem_conv_kernel,
        pairs,
        [
            by_step((1,) + planes_shape),
            whole(weight.shape),
        ],
        [by_step((2,) + map_shape), whole((2, 64, 128))],
        [((2 * pairs,) + map_shape, jnp.float32), ((2, 64, 128), jnp.float32)],
        [],
        4 * 10**9 * pairs,
        7 * 10**6 * pairs,
        (planes, weight),
        waits,
    )


def stem_slope(pre, cot, first, vectors, *waits):
    images = pre.shape[0] // 2
    return stem_call(
        stem_slope_kernel,
        images,
        [
            pl.BlockSpec((1,) + map_shape, lambda i: (i + first, 0, 0, 0)),
            pl.BlockSpec((1, 64, 32, 128), lambda i: (i + first, 0, 0, 0)),
            whole(vectors.shape),
        ],
        [by_step((1,) + map_shape), whole((2, 64, 128))],
        [((images,) + map_shape, jnp.bfloat16), ((2, 64, 128), jnp.float32)],
        [((256, 256), jnp.bfloat16)],
        10**9 * images,
        2 * 10**6 * images,
        (pre, cot, vectors),
        waits,
    )


def stem_grad(planes, pre, outer, first, vectors, *waits):
    pairs = planes.shape[0] // 2

    def later(shape):
        return pl.BlockSpec(shape, lambda i: (i + first, 0, 0, 0))

    return stem_call(
        stem_grad_kernel,
        pairs,
        [
            later((1,) + planes_shape), later((2,) + map_shape), by_step((2,) + map_shape),
            whole(vectors.shape),
        ],
        [whole((8, 64, 128))],
        [((8, 64, 128), jnp.float32)],
        [((256, 13 * 112), jnp.float32)],
        4 * 10**9 * pairs,
        8 * 10**6 * pairs,
        (planes, pre, outer, vectors),
        waits,
    )[0]


def filters_inside(weight):
    taps = weight.reshape(-1, 3 * WIN, 49).swapaxes(1, 2)
    return jnp.pad(taps, ((0, 0), (0, 0), (0, 1))).reshape(weight.shape[0], -1)


def filters_outside(weight):
    return weight.reshape(-1, 49, 16)[:, :, : 3 * WIN].swapaxes(1, 2).reshape(weight.shape[0], -1)


def lanes(*entries):
    return jnp.broadcast_to(jnp.stack(entries)[:, :, None], (len(entries), entries[0].size, 128))


taps = [(ky, kx) for ky in range(3) for kx in range(3)]
f32, bf16 = jnp.float32, jnp.bfloat16


def dot(left, right, sides="NN", precision=None):
    contract = ((0 if sides[0] == "T" else 1,), (1 if sides[1] == "T" else 0,))
    return lax.dot_general(
        left, right, (contract, ((), ())), preferred_element_type=f32, precision=precision
    )


def split_dot(matrix, values):
    upper = values.astype(bf16)
    lower = (values - upper.astype(f32)).astype(bf16)
    return dot(matrix, upper) + dot(matrix, lower)


def shift_columns(pad_ref, values, width):
    rows = values.shape[0]
    band = (pad_ref.shape[1] - rows) // 2
    column = stack_index(values.shape, 0) % width
    wide = values.astype(f32)
    for kx in range(3):
        moved = wide
        if kx == 0:
            moved = jnp.where(column == 0, 0.0, pltpu.roll(wide, 1, 0))
        if kx == 2:
            moved = jnp.where(column == width - 1, 0.0, pltpu.roll(wide, rows - 1, 0))
        zeros = jnp.zeros((band, values.shape[1]), pad_ref.dtype)
        pad_ref[kx, 0:band] = zeros
        pad_ref[kx, band : band + rows] = moved.astype(pad_ref.dtype)
        pad_ref[kx, band + rows :] = zeros
    return band


def conv_taps(pad_ref, band, first, rows, weight_ref, back=False, precision=None):
    channels = weight_ref.shape[0] // 9
    result = None
    for ky, kx in taps:
        part = pad_ref[kx, pl.ds(first + ky * band, rows)]
        tap = 8 - (3 * ky + kx) if back else 3 * ky + kx
        weight = weight_ref[tap * channels : (tap + 1) * channels, :].astype(pad_ref.dtype)
        term = dot(part, weight, "NT" if back else "NN", precision)
        result = term if result is None else result + term
    return result


def pool_matrix(out_rows, rows, factor, width, value, dtype=bf16):
    out, inner = stack_index((out_rows, rows), 0), stack_index((out_rows, rows), 1)
    band, small = SEG * width, width // factor
    out_band = SEG * small
    hit = (
        (out // out_band == inner // band // factor)
        & (out % out_band // small == inner % band // width)
        & (out % small == inner % width // factor)
    )
    return jnp.where(hit, value, 0.0).astype(dtype)


def spread_matrix(rows, factor, width):
    small = width // factor
    dims = (rows, SEG * small)
    out, inner = stack_index(dims, 0), stack_index(dims, 1)
    image, column = out % (SEG * width) // width, out % width
    hit = (inner // small == image) & (inner % small == column // factor)
    return jnp.where(hit, 1.0, 0.0).astype(bf16)


def as_row(block):
    return jnp.concatenate([block[j : j + 1] for j in range(block.shape[0])], 1)


def as_block(row):
    lanes_of = row.shape[1] // 128
    return jnp.concatenate([row[:, 128 * j : 128 * j + 128] for j in range(lanes_of)], 0)


def put_sums(out_ref, first, second, extra=None):
    block = jnp.concatenate([as_block(first), as_block(second)], 0)
    rows = out_ref.shape[1]
    if extra is not None:
        block = jnp.concatenate([block, extra], 0)
    if block.shape[0] < rows:
        block = jnp.concatenate([block, jnp.zeros((rows - block.shape[0], 128), f32)], 0)
    out_ref[...] = jnp.broadcast_to(block[None], out_ref.shape)


def get_sums(sums_ref, rows):
    block = jnp.sum(sums_ref[...], 0)
    return as_row(block[:rows]), as_row(block[rows : 2 * rows])


def norm_of(sums_ref, rows, count):
    first, second = get_sums(sums_ref, rows)
    mean = first / count
    return mean, lax.rsqrt(second / count - mean * mean + epsilon)


def silu(values):
    return values * jax.nn.sigmoid(values)


def column_sum(values):
    return jnp.sum(values, 0, keepdims=True)


def padded(rows, unit=16):
    return (rows + unit - 1) // unit * unit


def pack_kernel(place_ref, side_ref, one_ref, fine_ref, half_w_ref, quarter_w_ref, expand_ref,
                reduce_ref, two_ref, three_ref, sent_ref, parts_ref, early_ref):
    place, side = place_ref[0], side_ref[0]
    half = one_ref.shape[0] // 2
    part = early_ref.shape[0] // 2
    start = 0
    for part_ref in (fine_ref, half_w_ref, quarter_w_ref):
        early_ref[start : start + part_ref.shape[0]] = part_ref[...]
        start += padded(part_ref.shape[0])
    for block in range(expand_ref.shape[1] // 128):
        lanes_of = slice(128 * block, 128 * block + 128)
        early_ref[start : start + expand_ref.shape[0]] = expand_ref[:, lanes_of]
        start += padded(expand_ref.shape[0])

    def put(start, value):
        shape = (sent_ref.shape[0],) + value.shape
        sent_ref[:, start : start + value.shape[0]] = jnp.broadcast_to(value[None], shape)
        return start + padded(value.shape[0])

    start = 0
    rows = pl.ds(pl.multiple_of(side * half, half), half)
    for block in range(one_ref.shape[1] // 128):
        start = put(start, one_ref[rows, 128 * block : 128 * block + 128])
    start = put(start, early_ref[pl.ds(pl.multiple_of(side * part, part), part)])
    put(start, reduce_ref[...])
    wide = three_ref.shape[1] // 4
    columns = pl.ds(pl.multiple_of(place * 128, 128), 128)
    parts_ref[0 : two_ref.shape[0]] = two_ref[:, columns]
    start = padded(two_ref.shape[0])
    for block in range(wide // 128):
        columns = pl.ds(pl.multiple_of(place * wide + 128 * block, 128), 128)
        parts_ref[start : start + three_ref.shape[0]] = three_ref[:, columns]
        start += padded(three_ref.shape[0])


def own_lanes(place_ref, *refs):
    wide = refs[0].shape[1] // 4
    return [ref[:, pl.ds(pl.multiple_of(place_ref[0] * wide, wide), wide)] for ref in refs]


def first_kernel(side_ref, x_ref, mine_ref, other_ref, stem_ref,
                 full_ref, first_ref, sums_ref):
    side = side_ref[0]
    half = full_ref.shape[2]
    for part in range(full_ref.shape[3] // 128):
        rows, lanes_of = slice(half * part, half * part + half), slice(128 * part, 128 * part + 128)
        full_ref[:, pl.ds(side, 1), :, lanes_of] = mine_ref[:, rows][:, None]
        full_ref[:, pl.ds(1 - side, 1), :, lanes_of] = other_ref[:, rows][:, None]
    weight = full_ref[...].reshape(x_ref.shape[1], -1)
    first = dot(x_ref[...], weight)
    first_ref[...] = first
    put_sums(sums_ref, column_sum(first), column_sum(first * first), stem_row(stem_ref))


def stem_row(*refs):
    stem = sum(ref[...] for ref in refs).reshape(128, 128)
    return dot(jnp.ones((8, 128), f32), stem, "NT", lax.Precision.HIGHEST)


def hidden_kernel(count, mask_ref, sums_ref, first_ref, gain_ref, bias_ref, reduce_ref,
                  hidden_ref, change_ref, norm_ref):
    mean, inverse = norm_of(sums_ref, 4, count)
    norm_ref[...] = jnp.concatenate([mean, inverse], 0)
    level = (first_ref[...] - mean) * inverse * gain_ref[...] + bias_ref[...]
    hidden = silu(level).astype(bf16)
    hidden_ref[...] = hidden
    reduced = dot(hidden, reduce_ref[...])
    reduced = reduced.reshape(-1, SEG, 8, reduced.shape[1])
    steps = [
        mask_ref[0, t].astype(f32) * (reduced[:, t + 1] - reduced[:, t]) for t in range(SEG - 1)
    ]
    steps.append(jnp.zeros_like(steps[0]))
    change_ref[...] = jnp.stack(steps, 1).reshape(change_ref.shape).astype(bf16)


def gate_kernel(place_ref, change_ref, hidden_ref, fine_ref, half_w_ref, quarter_w_ref, expand_ref,
                gated_ref, sigmoid_ref, merged_ref, half_ref, quarter_ref,
                pad_ref, pad_half_ref, pad_quarter_ref):
    place = place_ref[0]
    change = change_ref[...]
    own = gated_ref.shape[0]
    band = shift_columns(pad_ref, change, 8)
    first = pl.multiple_of(place * own, own)
    fine = conv_taps(pad_ref, band, first, own, fine_ref)
    half = dot(pool_matrix(own, 4 * own, 2, 8, 0.25), change).astype(bf16)
    half_ref[...] = half
    band = shift_columns(pad_half_ref, half, 4)
    coarse = conv_taps(pad_half_ref, band, pl.multiple_of(place * 32, 32), 32, half_w_ref)
    quarter = dot(pool_matrix(own // 4, own, 2, 4, 0.25), half)
    quarter_ref[...] = quarter
    band = shift_columns(pad_quarter_ref, quarter, 2)
    coarsest = conv_taps(
        pad_quarter_ref, band, pl.multiple_of(place // 2 * 16, 16), 16, quarter_w_ref,
        precision=lax.Precision.HIGHEST,
    )
    merged = (
        fine
        + split_dot(spread_matrix(own, 2, 8), coarse)
        + split_dot(spread_matrix(own, 4, 8), coarsest)
    ).astype(bf16)
    merged_ref[...] = merged
    sigmoid = jax.nn.sigmoid(dot(merged, expand_ref[...]))
    sigmoid_ref[...] = sigmoid
    gated_ref[...] = (hidden_ref[...].astype(f32) * (1.0 + sigmoid)).astype(bf16)


def second_kernel(two_rows, gated_ref, packed_ref, second_ref, weight_ref, sums_ref, pad_ref):
    for clip in range(packed_ref.shape[0]):
        weight_ref[two_rows * clip : two_rows * clip + two_rows] = packed_ref[clip, :two_rows]
    band = shift_columns(pad_ref, gated_ref[...], 8)
    second = conv_taps(pad_ref, band, 0, second_ref.shape[0], weight_ref)
    second_ref[...] = second
    put_sums(sums_ref, column_sum(second), column_sum(second * second))


def hidden_two_kernel(count, place_ref, sums_ref, second_ref, gain_ref, bias_ref, hidden_ref, norm_ref):
    mean, inverse = norm_of(sums_ref, 1, count)
    norm_ref[...] = jnp.concatenate([mean, inverse], 0)
    gain, bias = own_lanes(place_ref, gain_ref, bias_ref)
    level = (second_ref[...] - mean) * inverse * gain + bias
    hidden_ref[...] = silu(level).astype(bf16)


def third_kernel(two_rows, three_rows, hidden_ref, packed_ref, third_ref, weight_ref, sums_ref):
    start = padded(two_rows)
    for block in range(weight_ref.shape[1] // 128):
        for clip in range(packed_ref.shape[0]):
            weight_ref[
                three_rows * clip : three_rows * clip + three_rows, 128 * block : 128 * block + 128
            ] = packed_ref[clip, start : start + three_rows]
        start += padded(three_rows)
    third = None
    for part in range(hidden_ref.shape[0]):
        term = dot(hidden_ref[part], weight_ref[128 * part : 128 * part + 128, :])
        third = term if third is None else third + term
    third_ref[...] = third
    put_sums(sums_ref, column_sum(third), column_sum(third * third))


def sources(place, size):
    return [place ^ s for s in range(size)]


def output_kernel(count, place_ref, sums_ref, third_ref, gain_ref, bias_ref,
                  x0_ref, x1_ref, x2_ref, x3_ref, c0_ref, c1_ref, c2_ref, c3_ref,
                  low_ref, high_ref, s0_ref, s1_ref, s2_ref, s3_ref, slope_ref, norm_ref,
                  out_sums_ref):
    place = place_ref[0]
    mean, inverse = norm_of(sums_ref, 4, count)
    norm_ref[...] = jnp.concatenate([mean, inverse], 0)
    gain, bias = own_lanes(place_ref, gain_ref, bias_ref)
    own, wide = x0_ref.shape[0], third_ref.shape[1]
    lanes_r = pl.ds(pl.multiple_of(place * wide, wide), wide)
    total_bias, total_gain = jnp.zeros((1, wide), f32), jnp.zeros((1, wide), f32)
    pieces = zip(
        sources(place, 4),
        (x0_ref, x1_ref, x2_ref, x3_ref),
        (c0_ref, c1_ref, c2_ref, c3_ref),
        (s0_ref, s1_ref, s2_ref, s3_ref),
    )
    for source, x_ref, c_ref, send_ref in pieces:
        rows = pl.ds(pl.multiple_of(source * own, own), own)
        normed = (third_ref[rows] - mean) * inverse
        summed = normed * gain + bias + x_ref[:, lanes_r].astype(f32)
        sigmoid = jax.nn.sigmoid(summed)
        send_ref[0] = (summed * sigmoid).astype(bf16)
        slope = c_ref[...].astype(f32) * (sigmoid * (1.0 + summed * (1.0 - sigmoid)))
        slope_ref[rows] = slope
        send_ref[1] = slope.astype(bf16)
        total_bias += column_sum(slope)
        total_gain += column_sum(slope * normed)
    put_sums(out_sums_ref, total_bias, total_gain, stem_row(low_ref, high_ref))


def third_back_kernel(count, place_ref, sums_ref, third_ref, slope_ref, norm_ref, gain_ref, weight_ref,
                      grad_ref, part_ref, vectors_ref):
    total_bias, total_gain = get_sums(sums_ref, 4)
    vectors_ref[...] = jnp.concatenate([as_block(total_bias), as_block(total_gain)], 0)
    mean, inverse = norm_ref[0:1], norm_ref[1:2]
    normed = (third_ref[...] - mean) * inverse
    grad = own_lanes(place_ref, gain_ref)[0] * inverse * (
        slope_ref[...] - total_bias / count - normed * (total_gain / count)
    )
    grad = grad.astype(bf16)
    grad_ref[...] = grad
    back = dot(grad, weight_ref[...], "NT").astype(bf16)
    rest, stem = jnp.sum(sums_ref[:, 8:16], 0), []
    for _ in range(2):
        stem.append(rest.astype(bf16).astype(f32))
        rest = rest - stem[-1]
    order = stack_index((16, 128), 0)
    stem = jnp.where(
        order == 0, stem[0][0:1], jnp.where(order == 1, stem[1][0:1], rest[0:1])
    ).astype(bf16)
    rows = grad.shape[0]
    for part in range(part_ref.shape[0]):
        part_ref[part, :rows] = back[:, 128 * part : 128 * part + 128]
        part_ref[part, rows:] = stem


def second_slope_kernel(place_ref, part_ref, second_ref, norm_ref, gain_ref, bias_ref,
                        grad_ref, stem_ref, sums_ref):
    rows = second_ref.shape[0]
    back = jnp.sum(part_ref[:, :rows].astype(f32), 0)
    stem = jnp.sum(part_ref[:, rows:].astype(f32), 0)
    stem_ref[...] = jnp.broadcast_to(stem[0:1] + stem[1:2] + stem[2:3], stem_ref.shape)
    normed = (second_ref[...] - norm_ref[0:1]) * norm_ref[1:2]
    gain, bias = own_lanes(place_ref, gain_ref, bias_ref)
    grad = back * silu_slope(normed * gain + bias)
    grad_ref[...] = grad
    put_sums(sums_ref, column_sum(grad), column_sum(grad * normed))


def second_back_kernel(count, place_ref, sums_ref, slope_ref, second_ref, norm_ref, gain_ref, weight_ref,
                       grad_ref, part_ref, vectors_ref, pad_ref):
    total_bias, total_gain = get_sums(sums_ref, 1)
    vectors_ref[...] = jnp.concatenate([total_bias, total_gain], 0)
    inverse = norm_ref[1:2]
    normed = (second_ref[...] - norm_ref[0:1]) * inverse
    grad = own_lanes(place_ref, gain_ref)[0] * inverse * (
        slope_ref[...] - total_bias / count - normed * (total_gain / count)
    )
    grad = grad.astype(bf16)
    grad_ref[...] = grad
    band = shift_columns(pad_ref, grad, 8)
    own = part_ref.shape[1]
    for part in range(part_ref.shape[0]):
        back = conv_taps(pad_ref, band, part * own, own, weight_ref, True)
        part_ref[part] = back.astype(bf16)


def wide_grads_kernel(gated_ref, grad_ref, hidden_ref, third_ref, out_ref, pad_ref, all_ref):
    band = shift_columns(pad_ref, gated_ref[...], 8)
    rows, channels = gated_ref.shape
    clips = out_ref.shape[0]
    two_rows = 9 * channels // clips
    for ky, kx in taps:
        tap = 3 * ky + kx
        all_ref[tap * channels : (tap + 1) * channels, :] = dot(
            pad_ref[kx, ky * band : ky * band + rows], grad_ref[...], "TN"
        ).astype(bf16)
    start = 9 * channels
    for part in range(hidden_ref.shape[0]):
        value = dot(hidden_ref[part], third_ref[...], "TN").astype(bf16)
        for block in range(value.shape[1] // 128):
            first = start + channels * block + 128 * part
            all_ref[first : first + 128] = value[:, 128 * block : 128 * block + 128]
    three_rows = channels // clips

    for clip in range(clips):
        out_ref[clip, 0:two_rows] = all_ref[two_rows * clip : two_rows * clip + two_rows]
        at = padded(two_rows)
        for block in range(third_ref.shape[1] // 128):
            first = start + channels * block + three_rows * clip
            out_ref[clip, at : at + three_rows] = all_ref[first : first + three_rows]
            at += padded(three_rows)


def last_kernel(sum_ref, three_ref, two_ref, out_ref):
    rows = sum_ref.shape[0]
    out_ref[0:rows] = sum_ref[...]
    vectors = jnp.concatenate([three_ref[...], two_ref[...], jnp.zeros((6, 128), f32)], 0)
    upper = vectors.astype(bf16)
    out_ref[rows : rows + 16] = upper
    out_ref[rows + 16 : rows + 32] = (vectors - upper.astype(f32)).astype(bf16)


def gate_back_kernel(part_ref, hidden_ref, sigmoid_ref, expand_ref,
                     fine_ref, gate_ref, hidden_grad_ref):
    gated = jnp.sum(part_ref[...].astype(f32), 0)
    sigmoid = sigmoid_ref[...]
    gate = (gated * hidden_ref[...].astype(f32) * sigmoid * (1.0 - sigmoid)).astype(bf16)
    gate_ref[...] = gate
    hidden_grad_ref[...] = gated * (1.0 + sigmoid)
    fine_ref[...] = dot(gate, expand_ref[...], "NT").astype(bf16)


def reduce_back_kernel(place_ref, mask_ref, grad_ref, fine_ref, half_w_ref, quarter_w_ref,
                       reduce_ref, hidden_grad_ref, first_ref, norm_ref, gain_ref, bias_ref,
                       reduced_ref, slope_ref, coarse_ref, coarsest_ref, sums_ref,
                       pad_ref, pad_half_ref, pad_quarter_ref):
    place = place_ref[0]
    own = reduced_ref.shape[0]
    grad_fine = grad_ref[...]
    coarse = dot(pool_matrix(own, 4 * own, 2, 8, 1.0), grad_fine).astype(bf16)
    coarse_ref[...] = coarse
    coarsest = dot(pool_matrix(own // 4, 4 * own, 4, 8, 1.0), grad_fine)
    coarsest_ref[...] = coarsest
    band = shift_columns(pad_quarter_ref, coarsest, 2)
    low = conv_taps(
        pad_quarter_ref, band, pl.multiple_of(place // 2 * 16, 16), 16, quarter_w_ref, True,
        lax.Precision.HIGHEST,
    )
    band = shift_columns(pad_half_ref, coarse, 4)
    middle = conv_taps(pad_half_ref, band, pl.multiple_of(place * 32, 32), 32, half_w_ref, True)
    middle = middle + 0.25 * split_dot(spread_matrix(32, 2, 4), low)
    band = shift_columns(pad_ref, grad_fine, 8)
    change = conv_taps(pad_ref, band, pl.multiple_of(place * own, own), own, fine_ref, True)
    change = change + 0.25 * split_dot(spread_matrix(own, 2, 8), middle)
    change = change.reshape(-1, SEG, 8, change.shape[1])
    carried = [mask_ref[0, t].astype(f32) * change[:, t] for t in range(SEG - 1)]
    zero = jnp.zeros_like(carried[0])
    before, here = [zero] + carried, carried + [zero]
    reduced = jnp.stack([b - h for b, h in zip(before, here)], 1)
    reduced = reduced.reshape(reduced_ref.shape).astype(bf16)
    reduced_ref[...] = reduced
    grad_hidden = hidden_grad_ref[...] + dot(reduced, reduce_ref[...], "NT")
    normed = (first_ref[...] - norm_ref[0:1]) * norm_ref[1:2]
    slope = grad_hidden * silu_slope(normed * gain_ref[...] + bias_ref[...])
    slope_ref[...] = slope
    put_sums(sums_ref, column_sum(slope), column_sum(slope * normed))


def first_back_kernel(count, sums_ref, slope_ref, first_ref, norm_ref, gain_ref,
                      grad_ref, vectors_ref):
    total_bias, total_gain = get_sums(sums_ref, 4)
    vectors_ref[...] = jnp.concatenate([total_bias, total_gain], 0)
    inverse = norm_ref[1:2]
    normed = (first_ref[...] - norm_ref[0:1]) * inverse
    grad = gain_ref[...] * inverse * (
        slope_ref[...] - total_bias / count - normed * (total_gain / count)
    )
    grad_ref[...] = grad.astype(bf16)


def one_grad_kernel(place_ref, grad_ref, x0_ref, x1_ref, x2_ref, x3_ref, out_ref):
    place = place_ref[0]
    lanes_r = pl.ds(pl.multiple_of(place * 128, 128), 128)
    total = None
    for source, x_ref in zip(sources(place, 4), (x0_ref, x1_ref, x2_ref, x3_ref)):
        grad = grad_ref[pl.ds(source, 1), :, lanes_r][0]
        term = dot(x_ref[...], grad, "TN")
        total = term if total is None else total + term
    out_ref[...] = total.astype(bf16)


def small_grads_kernel(place_ref, change_ref, half_ref, quarter_ref, grad_ref, coarse_ref,
                       coarsest_ref, hidden_ref, reduced_ref, merged_ref, gate_ref,
                       stem_low_ref, stem_high_ref, out_ref,
                       pad_ref, pad_half_ref, pad_quarter_ref, grads_ref, shares_ref):
    place = place_ref[0]
    clips, part = out_ref.shape[0], shares_ref.shape[1] // 4
    scales = (
        (change_ref, grad_ref, pad_ref, 8, None),
        (half_ref, coarse_ref, pad_half_ref, 4, None),
        (quarter_ref, coarsest_ref, pad_quarter_ref, 2, lax.Precision.HIGHEST),
    )
    at = 0
    for map_ref, cot_ref, padded_ref, width, precision in scales:
        rows, channels = map_ref.shape
        band = shift_columns(padded_ref, map_ref[...], width)
        for ky, kx in taps:
            tap = 3 * ky + kx
            grads_ref[tap * channels : (tap + 1) * channels, :] = dot(
                padded_ref[kx, ky * band : ky * band + rows], cot_ref[...], "TN", precision
            ).astype(bf16)
        share = 9 * channels // clips
        for clip in range(clips):
            shares_ref[clip, :share] = grads_ref[share * clip : share * clip + share]
        out_ref[:, at : at + part] = shares_ref[:, pl.ds(pl.multiple_of(place * part, part), part)]
        at += part
    value = dot(hidden_ref[...], reduced_ref[...], "TN").astype(bf16)
    expand = dot(merged_ref[...], gate_ref[...], "TN").astype(bf16)
    blocks = [value] + [
        expand[:, first : first + 128] for first in range(0, expand.shape[1], 128)
    ]
    blocks += [
        (stem_low_ref[k] + stem_high_ref[k]).astype(bf16) for k in range(stem_low_ref.shape[0])
    ]
    for block in blocks:
        share = block.shape[0] // clips
        for clip in range(clips):
            out_ref[clip, at : at + share] = block[share * clip : share * clip + share]
        at += padded(share)


def input_grad_kernel(place_ref, grad_ref, weight_ref, r0_ref, r1_ref, r2_ref, r3_ref,
                      input_ref, out_ref):
    place = place_ref[0]
    wide = r0_ref.shape[2]
    for source, r_ref in zip(sources(place, 4), (r0_ref, r1_ref, r2_ref, r3_ref)):
        lanes_r = pl.ds(pl.multiple_of(source * wide, wide), wide)
        weight = weight_ref[pl.ds(pl.multiple_of(source * wide, wide), wide), :]
        value = dot(grad_ref[...], weight, "NT") + r_ref[1].astype(f32)
        shape = (input_ref.shape[1], input_ref.shape[0], input_ref.shape[2], wide)
        value, result = value.reshape(shape), r_ref[0].astype(f32).reshape(shape)
        for row in range(shape[0]):
            input_ref[:, row, :, lanes_r] = value[row]
            out_ref[:, row, :, lanes_r] = result[row].astype(bf16)


def by_source(place, refs):
    pieces = [ref[...].astype(f32) for ref in refs]
    low, high = (place & 1) == 0, (place & 2) == 0
    pairs = []
    for first, second in ((pieces[0], pieces[1]), (pieces[2], pieces[3])):
        pairs.append((jnp.where(low, first, second), jnp.where(low, second, first)))
    near, far = pairs
    return [jnp.where(high, near[k], far[k]) for k in range(2)] + [
        jnp.where(high, far[k], near[k]) for k in range(2)
    ]


def wide_shares_kernel(place_ref, *refs):
    pieces = by_source(place_ref[0], refs[:4])
    two_ref, three_ref, gain_two_ref, bias_two_ref, gain_three_ref, bias_three_ref = refs[4:]
    two_rows, three_rows = two_ref.shape[0], three_ref.shape[0]
    blocks = three_ref.shape[1] // 512
    vectors_at = padded(two_rows) + blocks * padded(three_rows)
    for source, piece in enumerate(pieces):
        lanes_of = slice(128 * source, 128 * source + 128)
        two_ref[:, lanes_of] = piece[:two_rows]
        vectors = piece[vectors_at : vectors_at + 16] + piece[vectors_at + 16 : vectors_at + 32]
        bias_two_ref[:, lanes_of], gain_two_ref[:, lanes_of] = vectors[8:9], vectors[9:10]
        for block in range(blocks):
            start = padded(two_rows) + block * padded(three_rows)
            first = 128 * (blocks * source + block)
            three_ref[:, first : first + 128] = piece[start : start + three_rows]
            bias_three_ref[:, first : first + 128] = vectors[block : block + 1]
            gain_three_ref[:, first : first + 128] = vectors[4 + block : 5 + block]


def one_share_kernel(place_ref, *refs):
    for source, piece in enumerate(by_source(place_ref[0], refs[:4])):
        refs[4][:, 128 * source : 128 * source + 128] = piece


def rest_shares_kernel(tap_rows, place_ref, *refs):
    pieces = by_source(place_ref[0], refs[:4])
    fine_ref, half_w_ref, quarter_w_ref, reduce_ref, expand_ref, stem_ref = refs[4:]
    start = 0
    for out_ref in (fine_ref, half_w_ref, quarter_w_ref):
        rows = [piece[start : start + tap_rows] for piece in pieces]
        out_ref[...] = jnp.concatenate(rows, 0)[: out_ref.shape[0]]
        start += tap_rows
    total = pieces[0] + pieces[1] + pieces[2] + pieces[3]
    for out_ref in (reduce_ref, expand_ref, stem_ref):
        rows = out_ref.shape[0]
        for first in range(0, out_ref.shape[1], 128):
            out_ref[:, first : first + 128] = total[start : start + rows]
            start += padded(rows)


class Fresh:
    def __init__(self, array):
        self.array = array


def call(kernel, scalars, arrays, outs, scratch=(), waits=(), flops=10**9, moved=2 * 10**6):
    used = len(scalars) + len(arrays)

    def body(*refs):
        kernel(*refs[:used], *refs[used + len(waits) :])

    shapes = [(entry.array if isinstance(entry, Fresh) else entry).shape for entry in arrays]
    return pl.pallas_call(
        body,
        grid=(1,),
        in_specs=[pl.BlockSpec(memory_space=pltpu.SMEM)] * len(scalars)
        + [whole(shape) for shape in shapes]
        + [pl.BlockSpec(memory_space=pl.ANY)] * len(waits),
        out_specs=[whole(shape) for shape, _ in outs],
        out_shape=[pltpu.HBM(shape, dtype) for shape, dtype in outs],
        scratch_shapes=[pltpu.VMEM(shape, dtype) for shape, dtype in scratch],
        compiler_params=pltpu.CompilerParams(vmem_limit_bytes=block_limit),
        cost_estimate=pl.CostEstimate(flops=flops, bytes_accessed=moved, transcendentals=0),
    )(
        *scalars,
        *(entry.array if isinstance(entry, Fresh) else in_hbm(entry) for entry in arrays),
        *waits,
    )


def together(*values):
    return lax.optimization_barrier(values)


def exchange(blocks, axis):
    return lax.all_to_all(blocks, axis, 0, 0)


def to_all(part, axis):
    size = lax.axis_size(axis)
    return exchange(jnp.broadcast_to(part[None], (size,) + part.shape), axis)


def swap(piece, axis, step):
    return lax.ppermute(piece, axis, [(i, i ^ step) for i in range(lax.axis_size(axis))])


def lane_blocks(array):
    return [array[:, start : start + 128] for start in range(0, array.shape[1], 128)]


def pick(array, index, axis=0):
    return lax.dynamic_index_in_dim(array, index, axis, keepdims=False)


def per_device(
    frames,
    frame_start,
    boundary_mask,
    stem_weight,
    stem_gain,
    stem_bias,
    block_input,
    w_one,
    w_reduce,
    k_fine,
    k_half,
    k_quarter,
    w_expand,
    w_two,
    w_three,
    gain_one,
    bias_one,
    gain_two,
    bias_two,
    gain_three,
    bias_three,
    stem_cot,
    block_cot,
):
    nc, nr = lax.axis_size("clip"), lax.axis_size("row")
    u32 = jnp.uint32
    place = lax.axis_index("row").astype(u32)
    spots = [place ^ u32(s) for s in range(nr)]
    side = place & u32(1)
    spot = place.astype(jnp.int32).reshape(1)
    both = ("clip", "row")
    images, block_rows, cols, c_in = block_input.shape
    mid, red = gain_one.shape[0], w_reduce.shape[1]
    mid_r, in_r = mid // nr, c_in // nr
    own = images * block_rows * cols
    pixels = own * nr
    count = float(pixels * nc)
    clip_sums = ((nc, 8, 128), f32)
    both_sums = ((nc * nr, 16, 128), f32)

    def in_part(array, index):
        return lax.dynamic_slice_in_dim(array, index * u32(in_r), in_r, array.ndim - 1)

    half = w_one.shape[0] // 2
    expand_rows = padded(w_expand.shape[0])
    early_rows = padded(3 * padded(k_fine.shape[0]) + mid // 128 * expand_rows, 32)
    edges = [4 * padded(half)]
    for rows in (early_rows // 2, w_reduce.shape[0]):
        edges.append(edges[-1] + padded(rows))
    two_rows, three_rows = w_two.shape[0], w_three.shape[0]
    two_end = padded(two_rows)
    part_rows = two_end + in_r // 128 * padded(three_rows)
    sent, parts = call(
        pack_kernel,
        (spot, side.astype(jnp.int32).reshape(1)),
        (w_one, k_fine, k_half, k_quarter, w_expand, w_reduce, w_two, w_three),
        (((nc, edges[-1], 128), bf16), ((part_rows, 128), bf16)),
        [((early_rows, 128), bf16)],
        [entry.reshape(1) for entry in spots],
    )
    taps_own, sent = together(filters_inside(stem_weight), sent)
    stem_taps = to_all(taps_own, "clip").reshape(STEM, -1)
    sent, stem_taps = together(sent, stem_taps)
    mine = exchange(sent, "clip")
    filters = jnp.concatenate(
        [jnp.pad(stem_taps, ((0, 0), (224 * y, 672 - 224 * y))) for y in range(4)], 0
    )

    x_own = block_input.swapaxes(0, 1).reshape(own, c_in)
    cot_own = block_cot.swapaxes(0, 1).reshape(own, c_in)

    local = frames[0]
    rows = local.shape[2]
    above = lax.ppermute(local[:, :, rows - 16 :], "row", [(i, i + 1) for i in range(nr - 1)])
    below = lax.ppermute(local[:, :, :16], "row", [(i + 1, i) for i in range(nr - 1)])
    cot_own, x_own, above, below = together(cot_own, x_own, above, below)
    planes = stem_planes(frame_start[0], local, above, below)
    stem_count = float(SEG * (rows // 2) * (local.shape[3] // 2) * nc * nr)
    cot_pieces = [in_part(cot_own, place)] + [
        swap(in_part(cot_own, spots[s]), "row", s) for s in range(1, nr)
    ]
    x_pieces = [x_own, swap(x_own, "row", 1), swap(x_own, "row", 2)]
    x_pieces.append(swap(x_pieces[2], "row", 1))

    stem_pre, stem_sums = stem_conv(planes, filters, *x_pieces[1:3], *cot_pieces[1:])
    mine, stem_sums = together(mine, stem_sums)
    other = swap(mine, "row", 1)
    packed = lax.all_gather(parts, "clip")
    full_one, first, sums = call(
        first_kernel,
        (side.astype(jnp.int32).reshape(1),),
        (x_own, Fresh(mine), Fresh(other), stem_sums),
        (((nc, 2, half, mid), bf16), ((own, mid), f32), both_sums),
    )
    full_one = full_one.reshape(c_in, mid)
    sums = exchange(sums, both)
    mine, other, first = together(mine, other, first)
    full_reduce = mine[:, edges[1] : edges[1] + w_reduce.shape[0]].reshape(mid, red)
    halves = [entry[:, edges[0] : edges[1]] for entry in (mine, other)]
    quarters = jnp.concatenate(
        [
            jnp.where(side == u32(0), halves[0], halves[1]),
            jnp.where(side == u32(0), halves[1], halves[0]),
        ],
        1,
    )
    early_parts, start = [], 0
    for size in (k_fine.shape[0],) * 3 + (w_expand.shape[0],) * (mid // 128):
        early_parts.append(quarters[:, start : start + size].reshape(-1, 128))
        start += padded(size)
    full_fine, full_half, full_quarter = early_parts[:3]
    full_expand = jnp.concatenate(early_parts[3:], 1)
    stem_totals = jnp.sum(sums[:, 8], 0).reshape(2, STEM)
    stem_mean, stem_inverse = statistics(stem_totals, stem_count)
    stem_vectors = lanes(stem_mean, stem_inverse, stem_gain, stem_bias)
    gain_one, bias_one = gain_one.reshape(1, -1), bias_one.reshape(1, -1)
    hidden_one, change, norm_one = call(
        functools.partial(hidden_kernel, count),
        (boundary_mask,),
        (Fresh(sums), first, gain_one, bias_one, full_reduce),
        (((own, mid), bf16), ((own, red), bf16), ((2, mid), f32)),
    )
    change = lax.all_gather(change, "row").reshape(pixels, red)
    pads = [
        ((3, pixels + 2 * images * cols, red), bf16),
        ((3, pixels // 4 + images * cols, red), bf16),
        ((3, pixels // 16 + images * cols // 2, red), f32),
    ]
    gated, sigmoid, merged, half_map, quarter = call(
        gate_kernel,
        (spot,),
        (Fresh(change), hidden_one, full_fine, full_half, full_quarter, full_expand),
        (
            ((own, mid), bf16),
            ((own, mid), f32),
            ((own, red), bf16),
            ((pixels // 4, red), bf16),
            ((pixels // 16, red), f32),
        ),
        pads,
    )
    gated = lax.all_gather(gated, "row").reshape(pixels, mid)
    second, two_r, sums = call(
        functools.partial(second_kernel, two_rows),
        (),
        (Fresh(gated), packed),
        (((pixels, mid_r), f32), ((9 * mid, mid_r), bf16), clip_sums),
        [((3, pixels + 2 * images * cols, mid), bf16)],
    )
    gain_two, bias_two = gain_two.reshape(1, -1), bias_two.reshape(1, -1)
    outer_low, slope_low = stem_slope(stem_pre, stem_cot, 0, stem_vectors, second)
    hidden_two, norm_two = call(
        functools.partial(hidden_two_kernel, count),
        (spot,),
        (Fresh(exchange(sums, "clip")), second, gain_two, bias_two),
        (((pixels, mid_r), bf16), ((2, mid_r), f32)),
        waits=(slope_low,),
    )
    hidden_two = lax.all_gather(hidden_two, "row")
    third, three_r, sums = call(
        functools.partial(third_kernel, two_rows, three_rows),
        (),
        (Fresh(hidden_two), packed),
        (((pixels, in_r), f32), ((mid, in_r), bf16), clip_sums),
    )
    outer_high, slope_high = stem_slope(stem_pre, stem_cot, 4, stem_vectors, third)
    gain_three, bias_three = gain_three.reshape(1, -1), bias_three.reshape(1, -1)
    *send, slope_three, norm_three, sums = call(
        functools.partial(output_kernel, count),
        (spot,),
        (
            Fresh(exchange(sums, "clip")), third, gain_three, bias_three, *x_pieces, *cot_pieces,
            slope_low, slope_high,
        ),
        (
            *[((2, own, in_r), bf16)] * nr,
            ((pixels, in_r), f32),
            ((2, in_r), f32),
            ((nc, 16, 128), f32),
        ),
    )

    returned = [send[0]] + [swap(send[s], "row", s) for s in range(1, nr)]
    grad_third, parts, vectors_three = call(
        functools.partial(third_back_kernel, count),
        (spot,),
        (
            Fresh(exchange(sums, "clip")), third, slope_three, norm_three, gain_three, three_r,
        ),
        (((pixels, in_r), bf16), ((nr, pixels + 16, mid_r), bf16), ((8, 128), f32)),
        waits=returned[1:],
    )
    slope_two, stem_totals, sums = call(
        second_slope_kernel,
        (spot,),
        (Fresh(exchange(parts, "row")), second, norm_two, gain_two, bias_two),
        (((pixels, mid_r), f32), ((8, 128), f32), clip_sums),
    )
    stem_bias_grad, stem_gain_grad = stem_totals[0].reshape(2, STEM)
    stem_vectors = lanes(
        stem_mean,
        stem_inverse,
        stem_gain * stem_inverse,
        stem_bias_grad / stem_count,
        stem_gain_grad / stem_count,
    )
    stem_low = stem_grad(planes, stem_pre, outer_low, 0, stem_vectors)
    grad_second, parts, vectors_two = call(
        functools.partial(second_back_kernel, count),
        (spot,),
        (
            Fresh(exchange(sums, "clip")), slope_two, second, norm_two, gain_two, two_r,
        ),
        (((pixels, mid_r), bf16), ((nr, own, mid), bf16), ((2, mid_r), f32)),
        [((3, pixels + 2 * images * cols, mid_r), bf16)],
        (stem_low,),
    )
    (wide,) = call(
        wide_grads_kernel,
        (),
        (gated, grad_second, hidden_two, grad_third),
        (((nc, part_rows, 128), bf16),),
        [
            ((3, pixels + 2 * images * cols, mid), bf16),
            ((9 * mid + mid * in_r // 128, 128), bf16),
        ],
    )
    wide_total = lax.psum_scatter(wide, "clip", scatter_dimension=0, tiled=False)
    stem_high = stem_grad(
        planes, stem_pre, outer_high, len(planes) // 2, stem_vectors, grad_second
    )
    grad_fine, grad_gate, grad_hidden = call(
        gate_back_kernel,
        (),
        (Fresh(exchange(parts, "row")), hidden_one, sigmoid, full_expand),
        (((own, red), bf16), ((own, mid), bf16), ((own, mid), f32)),
        waits=(wide, stem_high),
    )
    grad_fine = lax.all_gather(grad_fine, "row").reshape(pixels, red)
    grad_reduced, slope_one, grad_coarse, grad_coarsest, sums = call(
        reduce_back_kernel,
        (spot, boundary_mask),
        (
            Fresh(grad_fine), full_fine, full_half, full_quarter, full_reduce,
            grad_hidden, first, norm_one, gain_one, bias_one,
        ),
        (
            ((own, red), bf16),
            ((own, mid), f32),
            ((pixels // 4, red), bf16),
            ((pixels // 16, red), f32),
            both_sums,
        ),
        pads,
    )
    tap_rows = padded(padded(k_fine.shape[0], 4) // 4)
    rest_rows = 3 * tap_rows + padded(w_reduce.shape[0])
    rest_rows += mid // 128 * padded(w_expand.shape[0]) + 8 * padded(stem_weight.shape[0])
    (rest,) = call(
        small_grads_kernel,
        (spot,),
        (
            change, half_map, quarter, grad_fine, grad_coarse, grad_coarsest,
            hidden_one, grad_reduced, merged, grad_gate, stem_low, stem_high,
        ),
        (((nc, rest_rows, 128), bf16),),
        [*pads, ((9 * red, red), bf16), ((nc, 4 * tap_rows, 128), bf16)],
    )
    sums = exchange(sums, both)
    grad_first, vectors_one = call(
        functools.partial(first_back_kernel, count),
        (),
        (Fresh(sums), slope_one, first, norm_one, gain_one),
        (((own, mid), bf16), ((2, mid), f32)),
        waits=(rest,),
    )
    rest, grad_first = together(rest, grad_first)
    rest_total = jnp.sum(exchange(rest, "clip"), 0, dtype=f32).astype(bf16)
    (one_grad,) = call(
        one_grad_kernel,
        (spot,),
        (Fresh(lax.all_gather(grad_first, "row")), *x_pieces),
        (((c_in, mid_r), bf16),),
    )
    one_rows = c_in // nc
    one_grad, rest_total = together(one_grad, rest_total)
    one_total = exchange(one_grad.reshape(nc, one_rows, 128), "clip")
    one_total = jnp.sum(one_total, 0, dtype=f32).astype(bf16)
    input_grad, block_out = call(
        input_grad_kernel,
        (spot,),
        (grad_first, full_one, *returned),
        ((block_input.shape, f32), (block_input.shape, bf16)),
    )

    (last,) = call(
        last_kernel,
        (),
        (Fresh(wide_total), vectors_three, vectors_two),
        (((part_rows + 32, 128), bf16),),
    )
    def from_row(piece):
        return [piece] + [Fresh(swap(piece, "row", s)) for s in range(1, nr)]

    two_share, three_share, gain_two, bias_two, gain_three, bias_three = call(
        wide_shares_kernel,
        (spot,),
        from_row(last),
        (
            ((two_rows, mid), f32), ((three_rows, c_in), f32),
            ((1, mid), f32), ((1, mid), f32), ((1, c_in), f32), ((1, c_in), f32),
        ),
    )
    rest_shares = call(
        functools.partial(rest_shares_kernel, tap_rows),
        (spot,),
        from_row(rest_total),
        (
            *[(entry.shape, f32) for entry in (k_fine, k_half, k_quarter, w_reduce, w_expand)],
            ((stem_weight.shape[0], 1024), f32),
        ),
    )
    one_total, input_grad, two_share, *rest_shares = together(
        one_total, input_grad, two_share, *rest_shares
    )
    (one_share,) = call(one_share_kernel, (spot,), from_row(one_total), (((one_rows, mid), f32),))
    return (
        block_out,
        input_grad,
        filters_outside(rest_shares[5][:, :784]),
        stem_gain_grad,
        stem_bias_grad,
        one_share,
        rest_shares[3],
        *rest_shares[:3],
        rest_shares[4],
        two_share,
        three_share,
        vectors_one[1],
        vectors_one[0],
        gain_two[0],
        bias_two[0],
        gain_three[0],
        bias_three[0],
    )


def solution(mesh):
    in_specs = (
        P("clip", None, None, "row", None),
        P("clip", None),
        P("clip", None),
        P("clip", None),
        P(),
        P(),
        P("clip", "row", None, None),
        P("clip", None),
        P("clip", None),
        P("clip", None),
        P("clip", None),
        P("clip", None),
        P("clip", None),
        P("clip", None),
        P("clip", None),
        P(),
        P(),
        P(),
        P(),
        P(),
        P(),
        P("clip", None, "row", None),
        P("clip", "row", None, None),
    )
    out_specs = (
        P("clip", "row", None, None),
        P("clip", "row", None, None),
        P("clip", None),
        P(),
        P(),
        P("clip", None),
        P("clip", None),
        P("clip", None),
        P("clip", None),
        P("clip", None),
        P("clip", None),
        P("clip", None),
        P("clip", None),
        P(),
        P(),
        P(),
        P(),
        P(),
        P(),
    )
    return jax.shard_map(
        per_device, mesh=mesh, in_specs=in_specs, out_specs=out_specs, check_vma=False
    )
```

```python
import functools

import jax
import jax.numpy as jnp
from jax import lax
from jax.experimental import pallas as pl
from jax.experimental.pallas import tpu as pltpu
from jax.sharding import PartitionSpec as P

STEM = 64
SEG = 8
WIN = 5


epsilon = 1e-05


def silu_slope(values):
    sigmoid_val = jax.nn.sigmoid(values)
    return sigmoid_val * (1.0 + values * (1.0 - sigmoid_val))


def statistics(totals, count):
    mean = totals[0] / count
    return mean, lax.rsqrt(totals[1] / count - mean * mean + epsilon)


def stack_index(shape, dim):
    return lax.broadcasted_iota(jnp.int32, shape, dim)


def stem_planes_kernel(
    start_ref, local_ref, above_ref, below_ref, planes_ref, pick_ref, shift_ref
):
    pair = pl.program_id(0)

    @pl.when(pair == 0)
    def _():
        dims = (256, 240)
        out, inner = stack_index(dims, 0), stack_index(dims, 1)
        channel, plane = out % 16, inner // 16
        plus = plane == jnp.where(channel < 3, channel + 6, channel)
        minus = (channel >= 3) & (plane == channel - 3)
        value = jnp.where(plus, 1.0, 0.0) - jnp.where(minus, 1.0, 0.0)
        keep = (out // 16 == inner % 16) & (channel < 15)
        pick_ref[...] = jnp.where(keep, value, 0.0).astype(jnp.bfloat16)
        dims = (256, 896)
        source, target = stack_index(dims, 0), stack_index(dims, 1)
        wanted = 2 * (target % 128) + target // 128 - 3
        shift_ref[...] = jnp.where(source == wanted, 1.0, 0.0).astype(jnp.bfloat16)

    for side in range(2):
        first = start_ref[2 * pair + side]
        lanes = slice(128 * side, 128 * side + 128)
        for base in (0, 3):
            parts = []
            for block in range(base, base + 3):
                if block == 0:
                    window = above_ref[pl.ds(first, WIN)]
                elif block == 5:
                    window = below_ref[pl.ds(first, WIN)]
                else:
                    window = local_ref[pl.ds(first, WIN), :, 16 * block - 16 : 16 * block, :]
                part = jnp.dot(
                    pick_ref[...], window.reshape(240, 256), preferred_element_type=jnp.float32
                )
                parts.append(part.astype(jnp.bfloat16))
            stacked = jnp.concatenate(parts, 0)
            low, high = (8, 48) if base == 0 else (0, 40)
            at = 16 * base - 8
            for first_kx in range(0, 7, 2):
                count = min(2, 7 - first_kx)
                shifted = jnp.dot(
                    stacked,
                    shift_ref[:, 128 * first_kx : 128 * (first_kx + count)],
                    preferred_element_type=jnp.float32,
                ).astype(jnp.bfloat16)
                for k in range(count):
                    piece = shifted[:, 128 * k : 128 * k + 128].reshape(48, 16, 128)
                    channels = slice(16 * (first_kx + k), 16 * (first_kx + k) + 16)
                    planes_ref[0, at + low : at + high, channels, lanes] = piece[low:high]


def stem_conv_kernel(planes_ref, weight_ref, pre_ref, sums_ref):
    @pl.when(pl.program_id(0) == 0)
    def _():
        sums_ref[...] = jnp.zeros_like(sums_ref)

    @pl.loop(0, 2)
    def _(part):
        totals = [jnp.zeros((64, 128), jnp.float32)] * 2
        for step in range(4):
            group = 4 * part + step
            patches = planes_ref[0, pl.ds(5 + 8 * group, 13)].reshape(13 * 112, 256)
            out = jnp.dot(weight_ref[...], patches, preferred_element_type=jnp.float32)
            out = out.reshape(4, 64, 256)
            for side in range(2):
                half = out[:, :, 128 * side : 128 * side + 128]
                pre_ref[side, pl.ds(4 * group, 4)] = half
                totals = [totals[0] + jnp.sum(half, 0), totals[1] + jnp.sum(half * half, 0)]
        sums_ref[0] += totals[0]
        sums_ref[1] += totals[1]


def stem_slope_kernel(pre_ref, cot_ref, vectors_ref, outer_ref, sums_ref, swap_ref):
    @pl.when(pl.program_id(0) == 0)
    def _():
        out, inner = stack_index((256, 256), 0), stack_index((256, 256), 1)
        hit = (out // 16 == inner % 16) & (out % 16 == inner // 16)
        swap_ref[...] = jnp.where(hit, 1.0, 0.0).astype(jnp.bfloat16)
        sums_ref[...] = jnp.zeros_like(sums_ref)

    for part in range(4):
        channels = slice(16 * part, 16 * part + 16)
        mean, inverse = vectors_ref[0, channels], vectors_ref[1, channels]
        gain, bias = vectors_ref[2, channels], vectors_ref[3, channels]
        block = jnp.concatenate(
            [cot_ref[0, channels, 16 * k : 16 * k + 16, :].reshape(256, 128) for k in range(2)], 1
        )
        turned = jnp.dot(swap_ref[...], block, preferred_element_type=jnp.float32)
        total_bias, total_gain = jnp.zeros((16, 128)), jnp.zeros((16, 128))
        for k in range(2):
            rows = slice(16 * k, 16 * k + 16)
            cot = turned[:, 128 * k : 128 * k + 128].reshape(16, 16, 128)
            normed = (pre_ref[0, rows, channels, :] - mean) * inverse
            outer = cot * silu_slope(normed * gain + bias)
            outer_ref[0, rows, channels, :] = outer.astype(jnp.bfloat16)
            total_bias += jnp.sum(outer, 0)
            total_gain += jnp.sum(outer * normed, 0)
        sums_ref[0, channels] += total_bias
        sums_ref[1, channels] += total_gain


def stem_grad_kernel(planes_ref, pre_ref, outer_ref, vectors_ref, out_ref, acc_ref):
    pair, last = pl.program_id(0), pl.num_programs(0) - 1

    @pl.when(pair == 0)
    def _():
        acc_ref[...] = jnp.zeros_like(acc_ref)

    @pl.loop(0, 2)
    def _(half):
        total = None
        for step in range(4):
            group = 4 * half + step
            rows = pl.ds(4 * group, 4)
            sides = []
            for side in range(2):
                normed = (pre_ref[side, rows] - vectors_ref[0]) * vectors_ref[1]
                outer = outer_ref[side, rows].astype(jnp.float32)
                grad = vectors_ref[2] * (outer - vectors_ref[3] - normed * vectors_ref[4])
                sides.append(grad.astype(jnp.bfloat16).reshape(256, 128))
            patches = planes_ref[0, pl.ds(5 + 8 * group, 13)].reshape(13 * 112, 256)
            term = lax.dot_general(
                jnp.concatenate(sides, 1),
                patches,
                (((1,), (1,)), ((), ())),
                preferred_element_type=jnp.float32,
            )
            total = term if total is None else total + term
        acc_ref[...] += total

    @pl.when(pair == last)
    def _():
        total = acc_ref[0:64, 0:784]
        for y in range(1, 4):
            total += acc_ref[64 * y : 64 * y + 64, 224 * y : 224 * y + 784]
        total = jnp.concatenate([total, jnp.zeros((64, 240), jnp.float32)], 1)
        for part in range(8):
            out_ref[part] = total[:, 128 * part : 128 * part + 128]


stem_limit = 24 * 1024 * 1024
block_limit = 40 * 1024 * 1024
planes_shape, map_shape = (80, 112, 256), (32, 64, 128)


def whole(shape):
    return pl.BlockSpec(shape, lambda *_: (0,) * len(shape))


def by_step(shape):
    return pl.BlockSpec(shape, lambda i: (i,) + (0,) * (len(shape) - 1))


def in_hbm(array):
    return pltpu.with_memory_space_constraint(array, pltpu.HBM)


def stem_call(kernel, steps, in_specs, out_specs, outs, scratch, flops, moved, args, waits=()):
    flops = 10**6 if len(waits) == 1 and args[-1].shape[0] == 5 else flops
    used = len(args)

    def body(*refs):
        kernel(*refs[:used], *refs[used + len(waits) :])

    return pl.pallas_call(
        body,
        grid=(steps,),
        in_specs=in_specs + [pl.BlockSpec(memory_space=pl.ANY)] * len(waits),
        out_specs=out_specs,
        out_shape=[
            (pltpu.HBM if len(shape) == 4 else jax.ShapeDtypeStruct)(shape, dtype)
            for shape, dtype in outs
        ],
        scratch_shapes=[pltpu.VMEM(shape, dtype) for shape, dtype in scratch],
        compiler_params=pltpu.CompilerParams(vmem_limit_bytes=stem_limit),
        cost_estimate=pl.CostEstimate(flops=flops, bytes_accessed=moved, transcendentals=0),
    )(*(in_hbm(entry) if entry.ndim > 1 else entry for entry in args), *waits)


def stem_planes(starts, local, above, below):
    pairs = starts.shape[0] // 2
    return stem_call(
        stem_planes_kernel,
        pairs,
        [pl.BlockSpec(memory_space=pltpu.SMEM)]
        + [whole(entry.shape) for entry in (local, above, below)],
        [by_step((1,) + planes_shape)],
        [((pairs,) + planes_shape, jnp.bfloat16)],
        [((256, 240), jnp.bfloat16), ((256, 896), jnp.bfloat16)],
        4 * 10**9 * pairs,
        5 * 10**6 * pairs,
        (starts, local, above, below),
    )[0]


def stem_conv(planes, weight, *waits):
    pairs = planes.shape[0]
    return stem_call(
        stem_conv_kernel,
        pairs,
        [
            by_step((1,) + planes_shape),
            whole(weight.shape),
        ],
        [by_step((2,) + map_shape), whole((2, 64, 128))],
        [((2 * pairs,) + map_shape, jnp.float32), ((2, 64, 128), jnp.float32)],
        [],
        4 * 10**9 * pairs,
        7 * 10**6 * pairs,
        (planes, weight),
        waits,
    )


def stem_slope(pre, cot, first, vectors, *waits):
    images = pre.shape[0] // 2
    return stem_call(
        stem_slope_kernel,
        images,
        [
            pl.BlockSpec((1,) + map_shape, lambda i: (i + first, 0, 0, 0)),
            pl.BlockSpec((1, 64, 32, 128), lambda i: (i + first, 0, 0, 0)),
            whole(vectors.shape),
        ],
        [by_step((1,) + map_shape), whole((2, 64, 128))],
        [((images,) + map_shape, jnp.bfloat16), ((2, 64, 128), jnp.float32)],
        [((256, 256), jnp.bfloat16)],
        10**9 * images,
        2 * 10**6 * images,
        (pre, cot, vectors),
        waits,
    )


def stem_grad(planes, pre, outer, first, vectors, *waits):
    pairs = planes.shape[0] // 2

    def later(shape):
        return pl.BlockSpec(shape, lambda i: (i + first, 0, 0, 0))

    return stem_call(
        stem_grad_kernel,
        pairs,
        [
            later((1,) + planes_shape), later((2,) + map_shape), by_step((2,) + map_shape),
            whole(vectors.shape),
        ],
        [whole((8, 64, 128))],
        [((8, 64, 128), jnp.float32)],
        [((256, 13 * 112), jnp.float32)],
        4 * 10**9 * pairs,
        8 * 10**6 * pairs,
        (planes, pre, outer, vectors),
        waits,
    )[0]


def filters_inside(weight):
    taps = weight.reshape(-1, 3 * WIN, 49).swapaxes(1, 2)
    return jnp.pad(taps, ((0, 0), (0, 0), (0, 1))).reshape(weight.shape[0], -1)


def filters_outside(weight):
    return weight.reshape(-1, 49, 16)[:, :, : 3 * WIN].swapaxes(1, 2).reshape(weight.shape[0], -1)


def lanes(*entries):
    return jnp.broadcast_to(jnp.stack(entries)[:, :, None], (len(entries), entries[0].size, 128))


taps = [(ky, kx) for ky in range(3) for kx in range(3)]
f32, bf16 = jnp.float32, jnp.bfloat16


def dot(left, right, sides="NN", precision=None):
    contract = ((0 if sides[0] == "T" else 1,), (1 if sides[1] == "T" else 0,))
    return lax.dot_general(
        left, right, (contract, ((), ())), preferred_element_type=f32, precision=precision
    )


def split_dot(matrix, values):
    upper = values.astype(bf16)
    lower = (values - upper.astype(f32)).astype(bf16)
    return dot(matrix, upper) + dot(matrix, lower)


def shift_columns(pad_ref, values, width):
    rows = values.shape[0]
    band = (pad_ref.shape[1] - rows) // 2
    column = stack_index(values.shape, 0) % width
    wide = values.astype(f32)
    for kx in range(3):
        moved = wide
        if kx == 0:
            moved = jnp.where(column == 0, 0.0, pltpu.roll(wide, 1, 0))
        if kx == 2:
            moved = jnp.where(column == width - 1, 0.0, pltpu.roll(wide, rows - 1, 0))
        zeros = jnp.zeros((band, values.shape[1]), pad_ref.dtype)
        pad_ref[kx, 0:band] = zeros
        pad_ref[kx, band : band + rows] = moved.astype(pad_ref.dtype)
        pad_ref[kx, band + rows :] = zeros
    return band


def conv_taps(pad_ref, band, first, rows, weight_ref, back=False, precision=None):
    channels = weight_ref.shape[0] // 9
    result = None
    for ky, kx in taps:
        part = pad_ref[kx, pl.ds(first + ky * band, rows)]
        tap = 8 - (3 * ky + kx) if back else 3 * ky + kx
        weight = weight_ref[tap * channels : (tap + 1) * channels, :].astype(pad_ref.dtype)
        term = dot(part, weight, "NT" if back else "NN", precision)
        result = term if result is None else result + term
    return result


def pool_matrix(out_rows, rows, factor, width, value, dtype=bf16):
    out, inner = stack_index((out_rows, rows), 0), stack_index((out_rows, rows), 1)
    band, small = SEG * width, width // factor
    out_band = SEG * small
    hit = (
        (out // out_band == inner // band // factor)
        & (out % out_band // small == inner % band // width)
        & (out % small == inner % width // factor)
    )
    return jnp.where(hit, value, 0.0).astype(dtype)


def spread_matrix(rows, factor, width):
    small = width // factor
    dims = (rows, SEG * small)
    out, inner = stack_index(dims, 0), stack_index(dims, 1)
    image, column = out % (SEG * width) // width, out % width
    hit = (inner // small == image) & (inner % small == column // factor)
    return jnp.where(hit, 1.0, 0.0).astype(bf16)


def as_row(block):
    return jnp.concatenate([block[j : j + 1] for j in range(block.shape[0])], 1)


def as_block(row):
    lanes_of = row.shape[1] // 128
    return jnp.concatenate([row[:, 128 * j : 128 * j + 128] for j in range(lanes_of)], 0)


def put_sums(out_ref, first, second, extra=None):
    block = jnp.concatenate([as_block(first), as_block(second)], 0)
    rows = out_ref.shape[1]
    if extra is not None:
        block = jnp.concatenate([block, extra], 0)
    if block.shape[0] < rows:
        block = jnp.concatenate([block, jnp.zeros((rows - block.shape[0], 128), f32)], 0)
    out_ref[...] = jnp.broadcast_to(block[None], out_ref.shape)


def get_sums(sums_ref, rows):
    block = jnp.sum(sums_ref[...], 0)
    return as_row(block[:rows]), as_row(block[rows : 2 * rows])


def norm_of(sums_ref, rows, count):
    first, second = get_sums(sums_ref, rows)
    mean = first / count
    return mean, lax.rsqrt(second / count - mean * mean + epsilon)


def silu(values):
    return values * jax.nn.sigmoid(values)


def column_sum(values):
    return jnp.sum(values, 0, keepdims=True)


def padded(rows, unit=16):
    return (rows + unit - 1) // unit * unit


def pack_kernel(place_ref, side_ref, one_ref, fine_ref, half_w_ref, quarter_w_ref, expand_ref,
                reduce_ref, two_ref, three_ref, sent_ref, parts_ref, early_ref):
    place, side = place_ref[0], side_ref[0]
    half = one_ref.shape[0] // 2
    part = early_ref.shape[0] // 2
    start = 0
    for part_ref in (fine_ref, half_w_ref, quarter_w_ref):
        early_ref[start : start + part_ref.shape[0]] = part_ref[...]
        start += padded(part_ref.shape[0])
    for block in range(expand_ref.shape[1] // 128):
        lanes_of = slice(128 * block, 128 * block + 128)
        early_ref[start : start + expand_ref.shape[0]] = expand_ref[:, lanes_of]
        start += padded(expand_ref.shape[0])

    def put(start, value):
        shape = (sent_ref.shape[0],) + value.shape
        sent_ref[:, start : start + value.shape[0]] = jnp.broadcast_to(value[None], shape)
        return start + padded(value.shape[0])

    start = 0
    rows = pl.ds(pl.multiple_of(side * half, half), half)
    for block in range(one_ref.shape[1] // 128):
        start = put(start, one_ref[rows, 128 * block : 128 * block + 128])
    start = put(start, early_ref[pl.ds(pl.multiple_of(side * part, part), part)])
    put(start, reduce_ref[...])
    wide = three_ref.shape[1] // 4
    columns = pl.ds(pl.multiple_of(place * 128, 128), 128)
    parts_ref[0 : two_ref.shape[0]] = two_ref[:, columns]
    start = padded(two_ref.shape[0])
    for block in range(wide // 128):
        columns = pl.ds(pl.multiple_of(place * wide + 128 * block, 128), 128)
        parts_ref[start : start + three_ref.shape[0]] = three_ref[:, columns]
        start += padded(three_ref.shape[0])


def own_lanes(place_ref, *refs):
    wide = refs[0].shape[1] // 4
    return [ref[:, pl.ds(pl.multiple_of(place_ref[0] * wide, wide), wide)] for ref in refs]


def first_kernel(side_ref, x_ref, mine_ref, other_ref, stem_ref,
                 full_ref, first_ref, sums_ref):
    side = side_ref[0]
    half = full_ref.shape[2]
    for part in range(full_ref.shape[3] // 128):
        rows, lanes_of = slice(half * part, half * part + half), slice(128 * part, 128 * part + 128)
        full_ref[:, pl.ds(side, 1), :, lanes_of] = mine_ref[:, rows][:, None]
        full_ref[:, pl.ds(1 - side, 1), :, lanes_of] = other_ref[:, rows][:, None]
    weight = full_ref[...].reshape(x_ref.shape[1], -1)
    first = dot(x_ref[...], weight)
    first_ref[...] = first
    put_sums(sums_ref, column_sum(first), column_sum(first * first), stem_row(stem_ref))


def stem_row(*refs):
    stem = sum(ref[...] for ref in refs).reshape(128, 128)
    return dot(jnp.ones((8, 128), f32), stem, "NT", lax.Precision.HIGHEST)


def hidden_kernel(count, mask_ref, sums_ref, first_ref, gain_ref, bias_ref, reduce_ref,
                  hidden_ref, change_ref, norm_ref):
    mean, inverse = norm_of(sums_ref, 4, count)
    norm_ref[...] = jnp.concatenate([mean, inverse], 0)
    level = (first_ref[...] - mean) * inverse * gain_ref[...] + bias_ref[...]
    hidden = silu(level).astype(bf16)
    hidden_ref[...] = hidden
    reduced = dot(hidden, reduce_ref[...])
    reduced = reduced.reshape(-1, SEG, 8, reduced.shape[1])
    steps = [
        mask_ref[0, t].astype(f32) * (reduced[:, t + 1] - reduced[:, t]) for t in range(SEG - 1)
    ]
    steps.append(jnp.zeros_like(steps[0]))
    change_ref[...] = jnp.stack(steps, 1).reshape(change_ref.shape).astype(bf16)


def gate_kernel(place_ref, change_ref, hidden_ref, fine_ref, half_w_ref, quarter_w_ref, expand_ref,
                gated_ref, sigmoid_ref, merged_ref, half_ref, quarter_ref,
                pad_ref, pad_half_ref, pad_quarter_ref):
    place = place_ref[0]
    change = change_ref[...]
    own = gated_ref.shape[0]
    band = shift_columns(pad_ref, change, 8)
    first = pl.multiple_of(place * own, own)
    fine = conv_taps(pad_ref, band, first, own, fine_ref)
    half = dot(pool_matrix(own, 4 * own, 2, 8, 0.25), change).astype(bf16)
    half_ref[...] = half
    band = shift_columns(pad_half_ref, half, 4)
    coarse = conv_taps(pad_half_ref, band, pl.multiple_of(place * 32, 32), 32, half_w_ref)
    quarter = dot(pool_matrix(own // 4, own, 2, 4, 0.25), half)
    quarter_ref[...] = quarter
    band = shift_columns(pad_quarter_ref, quarter, 2)
    coarsest = conv_taps(
        pad_quarter_ref, band, pl.multiple_of(place // 2 * 16, 16), 16, quarter_w_ref,
        precision=lax.Precision.HIGHEST,
    )
    merged = (
        fine
        + split_dot(spread_matrix(own, 2, 8), coarse)
        + split_dot(spread_matrix(own, 4, 8), coarsest)
    ).astype(bf16)
    merged_ref[...] = merged
    sigmoid = jax.nn.sigmoid(dot(merged, expand_ref[...]))
    sigmoid_ref[...] = sigmoid
    gated_ref[...] = (hidden_ref[...].astype(f32) * (1.0 + sigmoid)).astype(bf16)


def second_kernel(two_rows, gated_ref, packed_ref, second_ref, weight_ref, sums_ref, pad_ref):
    for clip in range(packed_ref.shape[0]):
        weight_ref[two_rows * clip : two_rows * clip + two_rows] = packed_ref[clip, :two_rows]
    band = shift_columns(pad_ref, gated_ref[...], 8)
    second = conv_taps(pad_ref, band, 0, second_ref.shape[0], weight_ref)
    second_ref[...] = second
    put_sums(sums_ref, column_sum(second), column_sum(second * second))


def hidden_two_kernel(count, place_ref, sums_ref, second_ref, gain_ref, bias_ref, hidden_ref, norm_ref):
    mean, inverse = norm_of(sums_ref, 1, count)
    norm_ref[...] = jnp.concatenate([mean, inverse], 0)
    gain, bias = own_lanes(place_ref, gain_ref, bias_ref)
    level = (second_ref[...] - mean) * inverse * gain + bias
    hidden_ref[...] = silu(level).astype(bf16)


def third_kernel(two_rows, three_rows, hidden_ref, packed_ref, third_ref, weight_ref, sums_ref):
    start = padded(two_rows)
    for block in range(weight_ref.shape[1] // 128):
        for clip in range(packed_ref.shape[0]):
            weight_ref[
                three_rows * clip : three_rows * clip + three_rows, 128 * block : 128 * block + 128
            ] = packed_ref[clip, start : start + three_rows]
        start += padded(three_rows)
    third = None
    for part in range(hidden_ref.shape[0]):
        term = dot(hidden_ref[part], weight_ref[128 * part : 128 * part + 128, :])
        third = term if third is None else third + term
    third_ref[...] = third
    put_sums(sums_ref, column_sum(third), column_sum(third * third))


def sources(place, size):
    return [place ^ s for s in range(size)]


def output_kernel(count, place_ref, sums_ref, third_ref, gain_ref, bias_ref,
                  x0_ref, x1_ref, x2_ref, x3_ref, c0_ref, c1_ref, c2_ref, c3_ref,
                  s0_ref, s1_ref, s2_ref, s3_ref, slope_ref, norm_ref,
                  out_sums_ref):
    place = place_ref[0]
    mean, inverse = norm_of(sums_ref, 4, count)
    norm_ref[...] = jnp.concatenate([mean, inverse], 0)
    gain, bias = own_lanes(place_ref, gain_ref, bias_ref)
    own, wide = x0_ref.shape[0], third_ref.shape[1]
    lanes_r = pl.ds(pl.multiple_of(place * wide, wide), wide)
    total_bias, total_gain = jnp.zeros((1, wide), f32), jnp.zeros((1, wide), f32)
    pieces = zip(
        sources(place, 4),
        (x0_ref, x1_ref, x2_ref, x3_ref),
        (c0_ref, c1_ref, c2_ref, c3_ref),
        (s0_ref, s1_ref, s2_ref, s3_ref),
    )
    for source, x_ref, c_ref, send_ref in pieces:
        rows = pl.ds(pl.multiple_of(source * own, own), own)
        normed = (third_ref[rows] - mean) * inverse
        summed = normed * gain + bias + x_ref[:, lanes_r].astype(f32)
        sigmoid = jax.nn.sigmoid(summed)
        send_ref[0] = (summed * sigmoid).astype(bf16)
        slope = c_ref[...].astype(f32) * (sigmoid * (1.0 + summed * (1.0 - sigmoid)))
        slope_ref[rows] = slope
        send_ref[1] = slope.astype(bf16)
        total_bias += column_sum(slope)
        total_gain += column_sum(slope * normed)
    put_sums(out_sums_ref, total_bias, total_gain)


def third_back_kernel(count, place_ref, sums_ref, third_ref, slope_ref, norm_ref, gain_ref, weight_ref,
                      grad_ref, part_ref, vectors_ref):
    total_bias, total_gain = get_sums(sums_ref, 4)
    vectors_ref[...] = jnp.concatenate([as_block(total_bias), as_block(total_gain)], 0)
    mean, inverse = norm_ref[0:1], norm_ref[1:2]
    normed = (third_ref[...] - mean) * inverse
    grad = own_lanes(place_ref, gain_ref)[0] * inverse * (
        slope_ref[...] - total_bias / count - normed * (total_gain / count)
    )
    grad = grad.astype(bf16)
    grad_ref[...] = grad
    back = dot(grad, weight_ref[...], "NT").astype(bf16)
    for part in range(part_ref.shape[0]):
        part_ref[part] = back[:, 128 * part : 128 * part + 128]


def second_slope_kernel(place_ref, part_ref, second_ref, norm_ref, gain_ref, bias_ref,
                        low_ref, high_ref, grad_ref, sums_ref):
    back = jnp.sum(part_ref[...].astype(f32), 0)
    normed = (second_ref[...] - norm_ref[0:1]) * norm_ref[1:2]
    gain, bias = own_lanes(place_ref, gain_ref, bias_ref)
    grad = back * silu_slope(normed * gain + bias)
    grad_ref[...] = grad
    stem = stem_row(low_ref, high_ref)[0:1]
    put_sums(sums_ref, column_sum(grad), column_sum(grad * normed), stem)


def second_back_kernel(count, place_ref, sums_ref, slope_ref, second_ref, norm_ref, gain_ref, weight_ref,
                       grad_ref, part_ref, vectors_ref, stem_ref, pad_ref):
    total_bias, total_gain = get_sums(sums_ref, 1)
    rest, stem = jnp.sum(sums_ref[...], 0)[2:3], []
    for _ in range(2):
        stem.append(rest.astype(bf16).astype(f32))
        rest = rest - stem[-1]
    order = stack_index((16, 128), 0)
    stem = jnp.where(order == 0, stem[0], jnp.where(order == 1, stem[1], rest))
    stem_ref[...] = jnp.where(order < 3, stem, 0.0).astype(bf16)
    vectors_ref[...] = jnp.concatenate([total_bias, total_gain], 0)
    inverse = norm_ref[1:2]
    normed = (second_ref[...] - norm_ref[0:1]) * inverse
    grad = own_lanes(place_ref, gain_ref)[0] * inverse * (
        slope_ref[...] - total_bias / count - normed * (total_gain / count)
    )
    grad = grad.astype(bf16)
    grad_ref[...] = grad
    band = shift_columns(pad_ref, grad, 8)
    own = part_ref.shape[1]
    for part in range(part_ref.shape[0]):
        back = conv_taps(pad_ref, band, part * own, own, weight_ref, True)
        part_ref[part] = back.astype(bf16)


def wide_grads_kernel(gated_ref, grad_ref, hidden_ref, third_ref, out_ref, pad_ref, all_ref):
    band = shift_columns(pad_ref, gated_ref[...], 8)
    rows, channels = gated_ref.shape
    clips = out_ref.shape[0]
    two_rows = 9 * channels // clips
    for ky, kx in taps:
        tap = 3 * ky + kx
        all_ref[tap * channels : (tap + 1) * channels, :] = dot(
            pad_ref[kx, ky * band : ky * band + rows], grad_ref[...], "TN"
        ).astype(bf16)
    start = 9 * channels
    for part in range(hidden_ref.shape[0]):
        value = dot(hidden_ref[part], third_ref[...], "TN").astype(bf16)
        for block in range(value.shape[1] // 128):
            first = start + channels * block + 128 * part
            all_ref[first : first + 128] = value[:, 128 * block : 128 * block + 128]
    three_rows = channels // clips

    for clip in range(clips):
        out_ref[clip, 0:two_rows] = all_ref[two_rows * clip : two_rows * clip + two_rows]
        at = padded(two_rows)
        for block in range(third_ref.shape[1] // 128):
            first = start + channels * block + three_rows * clip
            out_ref[clip, at : at + three_rows] = all_ref[first : first + three_rows]
            at += padded(three_rows)


def last_kernel(sum_ref, three_ref, two_ref, out_ref):
    rows = sum_ref.shape[0]
    out_ref[0:rows] = sum_ref[...]
    vectors = jnp.concatenate([three_ref[...], two_ref[...], jnp.zeros((6, 128), f32)], 0)
    upper = vectors.astype(bf16)
    out_ref[rows : rows + 16] = upper
    out_ref[rows + 16 : rows + 32] = (vectors - upper.astype(f32)).astype(bf16)


def gate_back_kernel(part_ref, hidden_ref, sigmoid_ref, expand_ref, stem_ref,
                     fine_ref, gate_ref, hidden_grad_ref):
    gated = jnp.sum(part_ref[...].astype(f32), 0)
    sigmoid = sigmoid_ref[...]
    gate = (gated * hidden_ref[...].astype(f32) * sigmoid * (1.0 - sigmoid)).astype(bf16)
    gate_ref[...] = gate
    hidden_grad_ref[...] = gated * (1.0 + sigmoid)
    rows = gate.shape[0]
    fine_ref[:rows] = dot(gate, expand_ref[...], "NT").astype(bf16)
    fine_ref[rows:] = stem_ref[...]


def reduce_back_kernel(place_ref, mask_ref, grad_ref, fine_ref, half_w_ref, quarter_w_ref,
                       reduce_ref, hidden_grad_ref, first_ref, norm_ref, gain_ref, bias_ref,
                       reduced_ref, slope_ref, coarse_ref, coarsest_ref, stem_ref, sums_ref,
                       pad_ref, pad_half_ref, pad_quarter_ref):
    place = place_ref[0]
    own = reduced_ref.shape[0]
    grad_fine = grad_ref[:, :own].reshape(4 * own, grad_ref.shape[2])
    stem = jnp.sum(grad_ref[:, own:].astype(f32), 0)
    stem_ref[...] = jnp.broadcast_to(stem[0:1] + stem[1:2] + stem[2:3], stem_ref.shape)
    coarse = dot(pool_matrix(own, 4 * own, 2, 8, 1.0), grad_fine).astype(bf16)
    coarse_ref[...] = coarse
    coarsest = dot(pool_matrix(own // 4, 4 * own, 4, 8, 1.0), grad_fine)
    coarsest_ref[...] = coarsest
    band = shift_columns(pad_quarter_ref, coarsest, 2)
    low = conv_taps(
        pad_quarter_ref, band, pl.multiple_of(place // 2 * 16, 16), 16, quarter_w_ref, True,
        lax.Precision.HIGHEST,
    )
    band = shift_columns(pad_half_ref, coarse, 4)
    middle = conv_taps(pad_half_ref, band, pl.multiple_of(place * 32, 32), 32, half_w_ref, True)
    middle = middle + 0.25 * split_dot(spread_matrix(32, 2, 4), low)
    band = shift_columns(pad_ref, grad_fine, 8)
    change = conv_taps(pad_ref, band, pl.multiple_of(place * own, own), own, fine_ref, True)
    change = change + 0.25 * split_dot(spread_matrix(own, 2, 8), middle)
    change = change.reshape(-1, SEG, 8, change.shape[1])
    carried = [mask_ref[0, t].astype(f32) * change[:, t] for t in range(SEG - 1)]
    zero = jnp.zeros_like(carried[0])
    before, here = [zero] + carried, carried + [zero]
    reduced = jnp.stack([b - h for b, h in zip(before, here)], 1)
    reduced = reduced.reshape(reduced_ref.shape).astype(bf16)
    reduced_ref[...] = reduced
    grad_hidden = hidden_grad_ref[...] + dot(reduced, reduce_ref[...], "NT")
    normed = (first_ref[...] - norm_ref[0:1]) * norm_ref[1:2]
    slope = grad_hidden * silu_slope(normed * gain_ref[...] + bias_ref[...])
    slope_ref[...] = slope
    put_sums(sums_ref, column_sum(slope), column_sum(slope * normed))


def first_back_kernel(count, sums_ref, slope_ref, first_ref, norm_ref, gain_ref,
                      grad_ref, vectors_ref):
    total_bias, total_gain = get_sums(sums_ref, 4)
    vectors_ref[...] = jnp.concatenate([total_bias, total_gain], 0)
    inverse = norm_ref[1:2]
    normed = (first_ref[...] - norm_ref[0:1]) * inverse
    grad = gain_ref[...] * inverse * (
        slope_ref[...] - total_bias / count - normed * (total_gain / count)
    )
    grad_ref[...] = grad.astype(bf16)


def one_grad_kernel(place_ref, grad_ref, x0_ref, x1_ref, x2_ref, x3_ref, out_ref):
    place = place_ref[0]
    lanes_r = pl.ds(pl.multiple_of(place * 128, 128), 128)
    total = None
    for source, x_ref in zip(sources(place, 4), (x0_ref, x1_ref, x2_ref, x3_ref)):
        grad = grad_ref[pl.ds(source, 1), :, lanes_r][0]
        term = dot(x_ref[...], grad, "TN")
        total = term if total is None else total + term
    out_ref[...] = total.astype(bf16)


def small_grads_kernel(place_ref, change_ref, half_ref, quarter_ref, grad_ref, coarse_ref,
                       coarsest_ref, hidden_ref, reduced_ref, merged_ref, gate_ref,
                       out_ref,
                       pad_ref, pad_half_ref, pad_quarter_ref, grads_ref, shares_ref):
    place = place_ref[0]
    clips, part = out_ref.shape[0], shares_ref.shape[1] // 4
    own = hidden_ref.shape[0]
    grad_fine = grad_ref[:, :own].reshape(4 * own, grad_ref.shape[2])
    scales = (
        (change_ref, grad_fine, pad_ref, 8, None),
        (half_ref, coarse_ref[...], pad_half_ref, 4, None),
        (quarter_ref, coarsest_ref[...], pad_quarter_ref, 2, lax.Precision.HIGHEST),
    )
    at = 0
    for map_ref, cotangent, padded_ref, width, precision in scales:
        rows, channels = map_ref.shape
        band = shift_columns(padded_ref, map_ref[...], width)
        for ky, kx in taps:
            tap = 3 * ky + kx
            grads_ref[tap * channels : (tap + 1) * channels, :] = dot(
                padded_ref[kx, ky * band : ky * band + rows], cotangent, "TN", precision
            ).astype(bf16)
        share = 9 * channels // clips
        for clip in range(clips):
            shares_ref[clip, :share] = grads_ref[share * clip : share * clip + share]
        out_ref[:, at : at + part] = shares_ref[:, pl.ds(pl.multiple_of(place * part, part), part)]
        at += part
    value = dot(hidden_ref[...], reduced_ref[...], "TN").astype(bf16)
    expand = dot(merged_ref[...], gate_ref[...], "TN").astype(bf16)
    blocks = [value] + [
        expand[:, first : first + 128] for first in range(0, expand.shape[1], 128)
    ]
    for block in blocks:
        share = block.shape[0] // clips
        for clip in range(clips):
            out_ref[clip, at : at + share] = block[share * clip : share * clip + share]
        at += padded(share)


def join_kernel(grad_ref, low_ref, high_ref, out_ref):
    clips, rows = out_ref.shape[0], grad_ref.shape[0] // out_ref.shape[0]
    stem = low_ref[...] + high_ref[...]
    share = stem.shape[1] // clips
    for clip in range(clips):
        out_ref[clip, :rows] = grad_ref[rows * clip : rows * clip + rows]
        pieces = [stem[k, share * clip : share * clip + share] for k in range(stem.shape[0])]
        value = jnp.concatenate(pieces, 0).astype(bf16)
        out_ref[clip, rows : rows + value.shape[0]] = value


def input_grad_kernel(place_ref, grad_ref, weight_ref, r0_ref, r1_ref, r2_ref, r3_ref,
                      input_ref, out_ref):
    place = place_ref[0]
    wide = r0_ref.shape[2]
    for source, r_ref in zip(sources(place, 4), (r0_ref, r1_ref, r2_ref, r3_ref)):
        lanes_r = pl.ds(pl.multiple_of(source * wide, wide), wide)
        weight = weight_ref[pl.ds(pl.multiple_of(source * wide, wide), wide), :]
        value = dot(grad_ref[...], weight, "NT") + r_ref[1].astype(f32)
        shape = (input_ref.shape[1], input_ref.shape[0], input_ref.shape[2], wide)
        value, result = value.reshape(shape), r_ref[0].astype(f32).reshape(shape)
        for row in range(shape[0]):
            input_ref[:, row, :, lanes_r] = value[row]
            out_ref[:, row, :, lanes_r] = result[row].astype(bf16)


def by_source(place, refs):
    pieces = [ref[...].astype(f32) for ref in refs]
    low, high = (place & 1) == 0, (place & 2) == 0
    pairs = []
    for first, second in ((pieces[0], pieces[1]), (pieces[2], pieces[3])):
        pairs.append((jnp.where(low, first, second), jnp.where(low, second, first)))
    near, far = pairs
    return [jnp.where(high, near[k], far[k]) for k in range(2)] + [
        jnp.where(high, far[k], near[k]) for k in range(2)
    ]


def wide_shares_kernel(place_ref, *refs):
    pieces = by_source(place_ref[0], refs[:4])
    two_ref, three_ref, gain_two_ref, bias_two_ref, gain_three_ref, bias_three_ref = refs[4:]
    two_rows, three_rows = two_ref.shape[0], three_ref.shape[0]
    blocks = three_ref.shape[1] // 512
    vectors_at = padded(two_rows) + blocks * padded(three_rows)
    for source, piece in enumerate(pieces):
        lanes_of = slice(128 * source, 128 * source + 128)
        two_ref[:, lanes_of] = piece[:two_rows]
        vectors = piece[vectors_at : vectors_at + 16] + piece[vectors_at + 16 : vectors_at + 32]
        bias_two_ref[:, lanes_of], gain_two_ref[:, lanes_of] = vectors[8:9], vectors[9:10]
        for block in range(blocks):
            start = padded(two_rows) + block * padded(three_rows)
            first = 128 * (blocks * source + block)
            three_ref[:, first : first + 128] = piece[start : start + three_rows]
            bias_three_ref[:, first : first + 128] = vectors[block : block + 1]
            gain_three_ref[:, first : first + 128] = vectors[4 + block : 5 + block]


def one_share_kernel(place_ref, *refs):
    pieces = by_source(place_ref[0], refs[:4])
    one_ref, stem_ref = refs[4:]
    at, share = one_ref.shape[0], stem_ref.shape[0]
    for source, piece in enumerate(pieces):
        one_ref[:, 128 * source : 128 * source + 128] = piece[:at]
    total = pieces[0] + pieces[1] + pieces[2] + pieces[3]
    for block in range(stem_ref.shape[1] // 128):
        first = at + share * block
        stem_ref[:, 128 * block : 128 * block + 128] = total[first : first + share]


def rest_shares_kernel(tap_rows, place_ref, *refs):
    pieces = by_source(place_ref[0], refs[:4])
    fine_ref, half_w_ref, quarter_w_ref, reduce_ref, expand_ref = refs[4:]
    start = 0
    for out_ref in (fine_ref, half_w_ref, quarter_w_ref):
        rows = [piece[start : start + tap_rows] for piece in pieces]
        out_ref[...] = jnp.concatenate(rows, 0)[: out_ref.shape[0]]
        start += tap_rows
    total = pieces[0] + pieces[1] + pieces[2] + pieces[3]
    for out_ref in (reduce_ref, expand_ref):
        rows = out_ref.shape[0]
        for first in range(0, out_ref.shape[1], 128):
            out_ref[:, first : first + 128] = total[start : start + rows]
            start += padded(rows)


class Fresh:
    def __init__(self, array):
        self.array = array


def call(kernel, scalars, arrays, outs, scratch=(), waits=(), flops=10**9, moved=2 * 10**6):
    used = len(scalars) + len(arrays)

    def body(*refs):
        kernel(*refs[:used], *refs[used + len(waits) :])

    shapes = [(entry.array if isinstance(entry, Fresh) else entry).shape for entry in arrays]
    return pl.pallas_call(
        body,
        grid=(1,),
        in_specs=[pl.BlockSpec(memory_space=pltpu.SMEM)] * len(scalars)
        + [whole(shape) for shape in shapes]
        + [pl.BlockSpec(memory_space=pl.ANY)] * len(waits),
        out_specs=[whole(shape) for shape, _ in outs],
        out_shape=[pltpu.HBM(shape, dtype) for shape, dtype in outs],
        scratch_shapes=[pltpu.VMEM(shape, dtype) for shape, dtype in scratch],
        compiler_params=pltpu.CompilerParams(vmem_limit_bytes=block_limit),
        cost_estimate=pl.CostEstimate(flops=flops, bytes_accessed=moved, transcendentals=0),
    )(
        *scalars,
        *(entry.array if isinstance(entry, Fresh) else in_hbm(entry) for entry in arrays),
        *waits,
    )


def together(*values):
    return lax.optimization_barrier(values)


def exchange(blocks, axis):
    return lax.all_to_all(blocks, axis, 0, 0)


def to_all(part, axis):
    size = lax.axis_size(axis)
    return exchange(jnp.broadcast_to(part[None], (size,) + part.shape), axis)


def swap(piece, axis, step):
    return lax.ppermute(piece, axis, [(i, i ^ step) for i in range(lax.axis_size(axis))])


def lane_blocks(array):
    return [array[:, start : start + 128] for start in range(0, array.shape[1], 128)]


def pick(array, index, axis=0):
    return lax.dynamic_index_in_dim(array, index, axis, keepdims=False)


def per_device(
    frames,
    frame_start,
    boundary_mask,
    stem_weight,
    stem_gain,
    stem_bias,
    block_input,
    w_one,
    w_reduce,
    k_fine,
    k_half,
    k_quarter,
    w_expand,
    w_two,
    w_three,
    gain_one,
    bias_one,
    gain_two,
    bias_two,
    gain_three,
    bias_three,
    stem_cot,
    block_cot,
):
    nc, nr = lax.axis_size("clip"), lax.axis_size("row")
    u32 = jnp.uint32
    place = lax.axis_index("row").astype(u32)
    spots = [place ^ u32(s) for s in range(nr)]
    side = place & u32(1)
    spot = place.astype(jnp.int32).reshape(1)
    both = ("clip", "row")
    images, block_rows, cols, c_in = block_input.shape
    mid, red = gain_one.shape[0], w_reduce.shape[1]
    mid_r, in_r = mid // nr, c_in // nr
    own = images * block_rows * cols
    pixels = own * nr
    count = float(pixels * nc)
    clip_sums = ((nc, 8, 128), f32)
    both_sums = ((nc * nr, 16, 128), f32)

    def in_part(array, index):
        return lax.dynamic_slice_in_dim(array, index * u32(in_r), in_r, array.ndim - 1)

    half = w_one.shape[0] // 2
    expand_rows = padded(w_expand.shape[0])
    early_rows = padded(3 * padded(k_fine.shape[0]) + mid // 128 * expand_rows, 32)
    edges = [4 * padded(half)]
    for rows in (early_rows // 2, w_reduce.shape[0]):
        edges.append(edges[-1] + padded(rows))
    two_rows, three_rows = w_two.shape[0], w_three.shape[0]
    two_end = padded(two_rows)
    part_rows = two_end + in_r // 128 * padded(three_rows)
    sent, parts = call(
        pack_kernel,
        (spot, side.astype(jnp.int32).reshape(1)),
        (w_one, k_fine, k_half, k_quarter, w_expand, w_reduce, w_two, w_three),
        (((nc, edges[-1], 128), bf16), ((part_rows, 128), bf16)),
        [((early_rows, 128), bf16)],
        [entry.reshape(1) for entry in spots],
    )
    taps_own, sent = together(filters_inside(stem_weight), sent)
    stem_taps = to_all(taps_own, "clip").reshape(STEM, -1)
    sent, stem_taps = together(sent, stem_taps)
    mine = exchange(sent, "clip")
    filters = jnp.concatenate(
        [jnp.pad(stem_taps, ((0, 0), (224 * y, 672 - 224 * y))) for y in range(4)], 0
    )

    x_own = block_input.swapaxes(0, 1).reshape(own, c_in)
    cot_own = block_cot.swapaxes(0, 1).reshape(own, c_in)

    local = frames[0]
    rows = local.shape[2]
    above = lax.ppermute(local[:, :, rows - 16 :], "row", [(i, i + 1) for i in range(nr - 1)])
    below = lax.ppermute(local[:, :, :16], "row", [(i + 1, i) for i in range(nr - 1)])
    cot_own, x_own, above, below = together(cot_own, x_own, above, below)
    planes = stem_planes(frame_start[0], local, above, below)
    stem_count = float(SEG * (rows // 2) * (local.shape[3] // 2) * nc * nr)
    cot_pieces = [in_part(cot_own, place)] + [
        swap(in_part(cot_own, spots[s]), "row", s) for s in range(1, nr)
    ]
    x_pieces = [x_own, swap(x_own, "row", 1), swap(x_own, "row", 2)]
    x_pieces.append(swap(x_pieces[2], "row", 1))

    stem_pre, stem_sums = stem_conv(planes, filters, *x_pieces[1:3], *cot_pieces[1:])
    mine, stem_sums = together(mine, stem_sums)
    other = swap(mine, "row", 1)
    packed = lax.all_gather(parts, "clip")
    full_one, first, sums = call(
        first_kernel,
        (side.astype(jnp.int32).reshape(1),),
        (x_own, Fresh(mine), Fresh(other), stem_sums),
        (((nc, 2, half, mid), bf16), ((own, mid), f32), both_sums),
    )
    full_one = full_one.reshape(c_in, mid)
    sums = exchange(sums, both)
    mine, other, first = together(mine, other, first)
    full_reduce = mine[:, edges[1] : edges[1] + w_reduce.shape[0]].reshape(mid, red)
    halves = [entry[:, edges[0] : edges[1]] for entry in (mine, other)]
    quarters = jnp.concatenate(
        [
            jnp.where(side == u32(0), halves[0], halves[1]),
            jnp.where(side == u32(0), halves[1], halves[0]),
        ],
        1,
    )
    early_parts, start = [], 0
    for size in (k_fine.shape[0],) * 3 + (w_expand.shape[0],) * (mid // 128):
        early_parts.append(quarters[:, start : start + size].reshape(-1, 128))
        start += padded(size)
    full_fine, full_half, full_quarter = early_parts[:3]
    full_expand = jnp.concatenate(early_parts[3:], 1)
    stem_totals = jnp.sum(sums[:, 8], 0).reshape(2, STEM)
    stem_mean, stem_inverse = statistics(stem_totals, stem_count)
    stem_vectors = lanes(stem_mean, stem_inverse, stem_gain, stem_bias)
    gain_one, bias_one = gain_one.reshape(1, -1), bias_one.reshape(1, -1)
    hidden_one, change, norm_one = call(
        functools.partial(hidden_kernel, count),
        (boundary_mask,),
        (Fresh(sums), first, gain_one, bias_one, full_reduce),
        (((own, mid), bf16), ((own, red), bf16), ((2, mid), f32)),
    )
    change = lax.all_gather(change, "row").reshape(pixels, red)
    pads = [
        ((3, pixels + 2 * images * cols, red), bf16),
        ((3, pixels // 4 + images * cols, red), bf16),
        ((3, pixels // 16 + images * cols // 2, red), f32),
    ]
    gated, sigmoid, merged, half_map, quarter = call(
        gate_kernel,
        (spot,),
        (Fresh(change), hidden_one, full_fine, full_half, full_quarter, full_expand),
        (
            ((own, mid), bf16),
            ((own, mid), f32),
            ((own, red), bf16),
            ((pixels // 4, red), bf16),
            ((pixels // 16, red), f32),
        ),
        pads,
    )
    gated = lax.all_gather(gated, "row").reshape(pixels, mid)
    second, two_r, sums = call(
        functools.partial(second_kernel, two_rows),
        (),
        (Fresh(gated), packed),
        (((pixels, mid_r), f32), ((9 * mid, mid_r), bf16), clip_sums),
        [((3, pixels + 2 * images * cols, mid), bf16)],
    )
    gain_two, bias_two = gain_two.reshape(1, -1), bias_two.reshape(1, -1)
    outer_low, slope_low = stem_slope(stem_pre, stem_cot, 0, stem_vectors, second)
    hidden_two, norm_two = call(
        functools.partial(hidden_two_kernel, count),
        (spot,),
        (Fresh(exchange(sums, "clip")), second, gain_two, bias_two),
        (((pixels, mid_r), bf16), ((2, mid_r), f32)),
        waits=(slope_low,),
    )
    hidden_two = lax.all_gather(hidden_two, "row")
    third, three_r, sums = call(
        functools.partial(third_kernel, two_rows, three_rows),
        (),
        (Fresh(hidden_two), packed),
        (((pixels, in_r), f32), ((mid, in_r), bf16), clip_sums),
    )
    gain_three, bias_three = gain_three.reshape(1, -1), bias_three.reshape(1, -1)
    *send, slope_three, norm_three, sums = call(
        functools.partial(output_kernel, count),
        (spot,),
        (
            Fresh(exchange(sums, "clip")), third, gain_three, bias_three, *x_pieces, *cot_pieces,
        ),
        (
            *[((2, own, in_r), bf16)] * nr,
            ((pixels, in_r), f32),
            ((2, in_r), f32),
            clip_sums,
        ),
    )

    outer_high, slope_high = stem_slope(stem_pre, stem_cot, SEG // 2, stem_vectors, slope_three)
    grad_third, parts, vectors_three = call(
        functools.partial(third_back_kernel, count),
        (spot,),
        (
            Fresh(exchange(sums, "clip")), third, slope_three, norm_three, gain_three, three_r,
        ),
        (((pixels, in_r), bf16), ((nr, pixels, mid_r), bf16), ((8, 128), f32)),
        waits=(slope_high,),
    )
    slope_two, sums = call(
        second_slope_kernel,
        (spot,),
        (
            Fresh(exchange(parts, "row")), second, norm_two, gain_two, bias_two,
            slope_low, slope_high,
        ),
        (((pixels, mid_r), f32), clip_sums),
    )
    slope_two, *send = together(slope_two, *send)
    returned = [send[0]] + [swap(send[s], "row", s) for s in range(1, nr)]
    grad_second, parts, vectors_two, stem_part = call(
        functools.partial(second_back_kernel, count),
        (spot,),
        (
            Fresh(exchange(sums, "clip")), slope_two, second, norm_two, gain_two, two_r,
        ),
        (
            ((pixels, mid_r), bf16), ((nr, own, mid), bf16), ((2, mid_r), f32),
            ((16, 128), bf16),
        ),
        [((3, pixels + 2 * images * cols, mid_r), bf16)],
        returned[1:],
    )
    (wide,) = call(
        wide_grads_kernel,
        (),
        (gated, grad_second, hidden_two, grad_third),
        (((nc, part_rows, 128), bf16),),
        [
            ((3, pixels + 2 * images * cols, mid), bf16),
            ((9 * mid + mid * in_r // 128, 128), bf16),
        ],
    )
    wide_total = lax.psum_scatter(wide, "clip", scatter_dimension=0, tiled=False)
    grad_fine, grad_gate, grad_hidden = call(
        gate_back_kernel,
        (),
        (Fresh(exchange(parts, "row")), hidden_one, sigmoid, full_expand, stem_part),
        (((own + 16, red), bf16), ((own, mid), bf16), ((own, mid), f32)),
        waits=(wide,),
    )
    grad_fine = lax.all_gather(grad_fine, "row")
    grad_reduced, slope_one, grad_coarse, grad_coarsest, stem_totals, sums = call(
        reduce_back_kernel,
        (spot, boundary_mask),
        (
            Fresh(grad_fine), full_fine, full_half, full_quarter, full_reduce,
            grad_hidden, first, norm_one, gain_one, bias_one,
        ),
        (
            ((own, red), bf16),
            ((own, mid), f32),
            ((pixels // 4, red), bf16),
            ((pixels // 16, red), f32),
            ((8, 128), f32),
            both_sums,
        ),
        pads,
    )
    stem_bias_grad, stem_gain_grad = stem_totals[0].reshape(2, STEM)
    stem_vectors = lanes(
        stem_mean,
        stem_inverse,
        stem_gain * stem_inverse,
        stem_bias_grad / stem_count,
        stem_gain_grad / stem_count,
    )
    stem_low = stem_grad(planes, stem_pre, outer_low, 0, stem_vectors, slope_one)
    tap_rows = padded(padded(k_fine.shape[0], 4) // 4)
    rest_rows = 3 * tap_rows + padded(w_reduce.shape[0])
    rest_rows += mid // 128 * padded(w_expand.shape[0])
    (rest,) = call(
        small_grads_kernel,
        (spot,),
        (
            change, half_map, quarter, grad_fine, grad_coarse, grad_coarsest,
            hidden_one, grad_reduced, merged, grad_gate,
        ),
        (((nc, rest_rows, 128), bf16),),
        [*pads, ((9 * red, red), bf16), ((nc, 4 * tap_rows, 128), bf16)],
    )
    sums = exchange(sums, both)
    grad_first, vectors_one = call(
        functools.partial(first_back_kernel, count),
        (),
        (Fresh(sums), slope_one, first, norm_one, gain_one),
        (((own, mid), bf16), ((2, mid), f32)),
        waits=(rest, stem_low),
    )
    rest, grad_first = together(rest, grad_first)
    rest_total = jnp.sum(exchange(rest, "clip"), 0, dtype=f32).astype(bf16)
    (one_grad,) = call(
        one_grad_kernel,
        (spot,),
        (Fresh(lax.all_gather(grad_first, "row")), *x_pieces),
        (((c_in, mid_r), bf16),),
    )
    stem_high = stem_grad(planes, stem_pre, outer_high, len(planes) // 2, stem_vectors, one_grad)
    one_rows, stem_rows = c_in // nc, padded(8 * stem_weight.shape[0])
    (one_grad,) = call(
        join_kernel,
        (),
        (one_grad, stem_low, stem_high),
        (((nc, one_rows + stem_rows, 128), bf16),),
    )
    one_grad, rest_total = together(one_grad, rest_total)
    one_total = jnp.sum(exchange(one_grad, "clip"), 0, dtype=f32).astype(bf16)
    input_grad, block_out = call(
        input_grad_kernel,
        (spot,),
        (grad_first, full_one, *returned),
        ((block_input.shape, f32), (block_input.shape, bf16)),
    )

    (last,) = call(
        last_kernel,
        (),
        (Fresh(wide_total), vectors_three, vectors_two),
        (((part_rows + 32, 128), bf16),),
    )
    def from_row(piece):
        return [piece] + [Fresh(swap(piece, "row", s)) for s in range(1, nr)]

    wide_pieces = [last] + [swap(last, "row", s) for s in range(1, nr)]
    rest_shares = call(
        functools.partial(rest_shares_kernel, tap_rows),
        (spot,),
        from_row(rest_total),
        (
            *[(entry.shape, f32) for entry in (k_fine, k_half, k_quarter, w_reduce, w_expand)],
        ),
    )
    one_total, input_grad, *wide_pieces = together(one_total, input_grad, *wide_pieces)
    two_share, three_share, gain_two, bias_two, gain_three, bias_three = call(
        wide_shares_kernel,
        (spot,),
        [wide_pieces[0], *[Fresh(piece) for piece in wide_pieces[1:]]],
        (
            ((two_rows, mid), f32), ((three_rows, c_in), f32),
            ((1, mid), f32), ((1, mid), f32), ((1, c_in), f32), ((1, c_in), f32),
        ),
    )
    one_share, stem_share = call(
        one_share_kernel,
        (spot,),
        from_row(one_total),
        (((one_rows, mid), f32), ((stem_weight.shape[0], 1024), f32)),
    )
    return (
        block_out,
        input_grad,
        filters_outside(stem_share[:, :784]),
        stem_gain_grad,
        stem_bias_grad,
        one_share,
        rest_shares[3],
        *rest_shares[:3],
        rest_shares[4],
        two_share,
        three_share,
        vectors_one[1],
        vectors_one[0],
        gain_two[0],
        bias_two[0],
        gain_three[0],
        bias_three[0],
    )


def solution(mesh):
    in_specs = (
        P("clip", None, None, "row", None),
        P("clip", None),
        P("clip", None),
        P("clip", None),
        P(),
        P(),
        P("clip", "row", None, None),
        P("clip", None),
        P("clip", None),
        P("clip", None),
        P("clip", None),
        P("clip", None),
        P("clip", None),
        P("clip", None),
        P("clip", None),
        P(),
        P(),
        P(),
        P(),
        P(),
        P(),
        P("clip", None, "row", None),
        P("clip", "row", None, None),
    )
    out_specs = (
        P("clip", "row", None, None),
        P("clip", "row", None, None),
        P("clip", None),
        P(),
        P(),
        P("clip", None),
        P("clip", None),
        P("clip", None),
        P("clip", None),
        P("clip", None),
        P("clip", None),
        P("clip", None),
        P("clip", None),
        P(),
        P(),
        P(),
        P(),
        P(),
        P(),
    )
    return jax.shard_map(
        per_device, mesh=mesh, in_specs=in_specs, out_specs=out_specs, check_vma=False
    )
```

```python
import functools

import jax
import jax.numpy as jnp
from jax import lax
from jax.experimental import pallas as pl
from jax.experimental.pallas import tpu as pltpu
from jax.sharding import PartitionSpec as P

STEM = 64
SEG = 8
WIN = 5


epsilon = 1e-05


def silu_slope(values):
    sigmoid_val = jax.nn.sigmoid(values)
    return sigmoid_val * (1.0 + values * (1.0 - sigmoid_val))


def statistics(totals, count):
    mean = totals[0] / count
    return mean, lax.rsqrt(totals[1] / count - mean * mean + epsilon)


def stack_index(shape, dim):
    return lax.broadcasted_iota(jnp.int32, shape, dim)


def stem_planes_kernel(
    start_ref, local_ref, above_ref, below_ref, planes_ref, pick_ref, shift_ref
):
    pair = pl.program_id(0)

    @pl.when(pair == 0)
    def _():
        dims = (256, 240)
        out, inner = stack_index(dims, 0), stack_index(dims, 1)
        channel, plane = out % 16, inner // 16
        plus = plane == jnp.where(channel < 3, channel + 6, channel)
        minus = (channel >= 3) & (plane == channel - 3)
        value = jnp.where(plus, 1.0, 0.0) - jnp.where(minus, 1.0, 0.0)
        keep = (out // 16 == inner % 16) & (channel < 15)
        pick_ref[...] = jnp.where(keep, value, 0.0).astype(jnp.bfloat16)
        dims = (256, 896)
        source, target = stack_index(dims, 0), stack_index(dims, 1)
        wanted = 2 * (target % 128) + target // 128 - 3
        shift_ref[...] = jnp.where(source == wanted, 1.0, 0.0).astype(jnp.bfloat16)

    for side in range(2):
        first = start_ref[2 * pair + side]
        lanes = slice(128 * side, 128 * side + 128)
        for base in (0, 3):
            parts = []
            for block in range(base, base + 3):
                if block == 0:
                    window = above_ref[pl.ds(first, WIN)]
                elif block == 5:
                    window = below_ref[pl.ds(first, WIN)]
                else:
                    window = local_ref[pl.ds(first, WIN), :, 16 * block - 16 : 16 * block, :]
                part = jnp.dot(
                    pick_ref[...], window.reshape(240, 256), preferred_element_type=jnp.float32
                )
                parts.append(part.astype(jnp.bfloat16))
            stacked = jnp.concatenate(parts, 0)
            low, high = (8, 48) if base == 0 else (0, 40)
            at = 16 * base - 8
            for first_kx in range(0, 7, 2):
                count = min(2, 7 - first_kx)
                shifted = jnp.dot(
                    stacked,
                    shift_ref[:, 128 * first_kx : 128 * (first_kx + count)],
                    preferred_element_type=jnp.float32,
                ).astype(jnp.bfloat16)
                for k in range(count):
                    piece = shifted[:, 128 * k : 128 * k + 128].reshape(48, 16, 128)
                    channels = slice(16 * (first_kx + k), 16 * (first_kx + k) + 16)
                    planes_ref[0, at + low : at + high, channels, lanes] = piece[low:high]


def stem_conv_kernel(planes_ref, weight_ref, pre_ref, sums_ref):
    @pl.when(pl.program_id(0) == 0)
    def _():
        sums_ref[...] = jnp.zeros_like(sums_ref)

    @pl.loop(0, 2)
    def _(part):
        totals = [jnp.zeros((64, 128), jnp.float32)] * 2
        for step in range(4):
            group = 4 * part + step
            patches = planes_ref[0, pl.ds(5 + 8 * group, 13)].reshape(13 * 112, 256)
            out = jnp.dot(weight_ref[...], patches, preferred_element_type=jnp.float32)
            out = out.reshape(4, 64, 256)
            for side in range(2):
                half = out[:, :, 128 * side : 128 * side + 128]
                pre_ref[side, pl.ds(4 * group, 4)] = half
                totals = [totals[0] + jnp.sum(half, 0), totals[1] + jnp.sum(half * half, 0)]
        sums_ref[0] += totals[0]
        sums_ref[1] += totals[1]


def stem_slope_kernel(pre_ref, cot_ref, vectors_ref, outer_ref, sums_ref, swap_ref):
    @pl.when(pl.program_id(0) == 0)
    def _():
        out, inner = stack_index((256, 256), 0), stack_index((256, 256), 1)
        hit = (out // 16 == inner % 16) & (out % 16 == inner // 16)
        swap_ref[...] = jnp.where(hit, 1.0, 0.0).astype(jnp.bfloat16)
        sums_ref[...] = jnp.zeros_like(sums_ref)

    for part in range(4):
        channels = slice(16 * part, 16 * part + 16)
        mean, inverse = vectors_ref[0, channels], vectors_ref[1, channels]
        gain, bias = vectors_ref[2, channels], vectors_ref[3, channels]
        block = jnp.concatenate(
            [cot_ref[0, channels, 16 * k : 16 * k + 16, :].reshape(256, 128) for k in range(2)], 1
        )
        turned = jnp.dot(swap_ref[...], block, preferred_element_type=jnp.float32)
        total_bias, total_gain = jnp.zeros((16, 128)), jnp.zeros((16, 128))
        for k in range(2):
            rows = slice(16 * k, 16 * k + 16)
            cot = turned[:, 128 * k : 128 * k + 128].reshape(16, 16, 128)
            normed = (pre_ref[0, rows, channels, :] - mean) * inverse
            outer = cot * silu_slope(normed * gain + bias)
            outer_ref[0, rows, channels, :] = outer.astype(jnp.bfloat16)
            total_bias += jnp.sum(outer, 0)
            total_gain += jnp.sum(outer * normed, 0)
        sums_ref[0, channels] += total_bias
        sums_ref[1, channels] += total_gain


def stem_grad_kernel(planes_ref, pre_ref, outer_ref, vectors_ref, out_ref, acc_ref):
    pair, last = pl.program_id(0), pl.num_programs(0) - 1

    @pl.when(pair == 0)
    def _():
        acc_ref[...] = jnp.zeros_like(acc_ref)

    @pl.loop(0, 2)
    def _(half):
        total = None
        for step in range(4):
            group = 4 * half + step
            rows = pl.ds(4 * group, 4)
            sides = []
            for side in range(2):
                normed = (pre_ref[side, rows] - vectors_ref[0]) * vectors_ref[1]
                outer = outer_ref[side, rows].astype(jnp.float32)
                grad = vectors_ref[2] * (outer - vectors_ref[3] - normed * vectors_ref[4])
                sides.append(grad.astype(jnp.bfloat16).reshape(256, 128))
            patches = planes_ref[0, pl.ds(5 + 8 * group, 13)].reshape(13 * 112, 256)
            term = lax.dot_general(
                jnp.concatenate(sides, 1),
                patches,
                (((1,), (1,)), ((), ())),
                preferred_element_type=jnp.float32,
            )
            total = term if total is None else total + term
        acc_ref[...] += total

    @pl.when(pair == last)
    def _():
        total = acc_ref[0:64, 0:784]
        for y in range(1, 4):
            total += acc_ref[64 * y : 64 * y + 64, 224 * y : 224 * y + 784]
        total = jnp.concatenate([total, jnp.zeros((64, 240), jnp.float32)], 1)
        for part in range(8):
            out_ref[part] = total[:, 128 * part : 128 * part + 128]


stem_limit = 24 * 1024 * 1024
block_limit = 40 * 1024 * 1024
planes_shape, map_shape = (80, 112, 256), (32, 64, 128)


def whole(shape):
    return pl.BlockSpec(shape, lambda *_: (0,) * len(shape))


def by_step(shape):
    return pl.BlockSpec(shape, lambda i: (i,) + (0,) * (len(shape) - 1))


def in_hbm(array):
    return pltpu.with_memory_space_constraint(array, pltpu.HBM)


def stem_call(kernel, steps, in_specs, out_specs, outs, scratch, flops, moved, args, waits=()):
    flops = 10**6 if len(waits) == 1 and args[-1].shape[0] == 5 else flops
    used = len(args)

    def body(*refs):
        kernel(*refs[:used], *refs[used + len(waits) :])

    return pl.pallas_call(
        body,
        grid=(steps,),
        in_specs=in_specs + [pl.BlockSpec(memory_space=pl.ANY)] * len(waits),
        out_specs=out_specs,
        out_shape=[
            (pltpu.HBM if len(shape) == 4 else jax.ShapeDtypeStruct)(shape, dtype)
            for shape, dtype in outs
        ],
        scratch_shapes=[pltpu.VMEM(shape, dtype) for shape, dtype in scratch],
        compiler_params=pltpu.CompilerParams(vmem_limit_bytes=stem_limit),
        cost_estimate=pl.CostEstimate(flops=flops, bytes_accessed=moved, transcendentals=0),
    )(*(in_hbm(entry) if entry.ndim > 1 else entry for entry in args), *waits)


def stem_planes(starts, local, above, below):
    pairs = starts.shape[0] // 2
    return stem_call(
        stem_planes_kernel,
        pairs,
        [pl.BlockSpec(memory_space=pltpu.SMEM)]
        + [whole(entry.shape) for entry in (local, above, below)],
        [by_step((1,) + planes_shape)],
        [((pairs,) + planes_shape, jnp.bfloat16)],
        [((256, 240), jnp.bfloat16), ((256, 896), jnp.bfloat16)],
        4 * 10**9 * pairs,
        5 * 10**6 * pairs,
        (starts, local, above, below),
    )[0]


def stem_conv(planes, weight, *waits):
    pairs = planes.shape[0]
    return stem_call(
        stem_conv_kernel,
        pairs,
        [
            by_step((1,) + planes_shape),
            whole(weight.shape),
        ],
        [by_step((2,) + map_shape), whole((2, 64, 128))],
        [((2 * pairs,) + map_shape, jnp.float32), ((2, 64, 128), jnp.float32)],
        [],
        4 * 10**9 * pairs,
        7 * 10**6 * pairs,
        (planes, weight),
        waits,
    )


def stem_slope(pre, cot, first, vectors, *waits):
    images = pre.shape[0] // 2
    return stem_call(
        stem_slope_kernel,
        images,
        [
            pl.BlockSpec((1,) + map_shape, lambda i: (i + first, 0, 0, 0)),
            pl.BlockSpec((1, 64, 32, 128), lambda i: (i + first, 0, 0, 0)),
            whole(vectors.shape),
        ],
        [by_step((1,) + map_shape), whole((2, 64, 128))],
        [((images,) + map_shape, jnp.bfloat16), ((2, 64, 128), jnp.float32)],
        [((256, 256), jnp.bfloat16)],
        10**9 * images,
        2 * 10**6 * images,
        (pre, cot, vectors),
        waits,
    )


def stem_grad(planes, pre, outer, first, vectors, *waits):
    pairs = planes.shape[0] // 2

    def later(shape):
        return pl.BlockSpec(shape, lambda i: (i + first, 0, 0, 0))

    return stem_call(
        stem_grad_kernel,
        pairs,
        [
            later((1,) + planes_shape), later((2,) + map_shape), by_step((2,) + map_shape),
            whole(vectors.shape),
        ],
        [whole((8, 64, 128))],
        [((8, 64, 128), jnp.float32)],
        [((256, 13 * 112), jnp.float32)],
        4 * 10**9 * pairs,
        8 * 10**6 * pairs,
        (planes, pre, outer, vectors),
        waits,
    )[0]


def filters_inside(weight):
    taps = weight.reshape(-1, 3 * WIN, 49).swapaxes(1, 2)
    return jnp.pad(taps, ((0, 0), (0, 0), (0, 1))).reshape(weight.shape[0], -1)


def filters_outside(weight):
    return weight.reshape(-1, 49, 16)[:, :, : 3 * WIN].swapaxes(1, 2).reshape(weight.shape[0], -1)


def lanes(*entries):
    return jnp.broadcast_to(jnp.stack(entries)[:, :, None], (len(entries), entries[0].size, 128))


taps = [(ky, kx) for ky in range(3) for kx in range(3)]
f32, bf16 = jnp.float32, jnp.bfloat16


def dot(left, right, sides="NN", precision=None):
    contract = ((0 if sides[0] == "T" else 1,), (1 if sides[1] == "T" else 0,))
    return lax.dot_general(
        left, right, (contract, ((), ())), preferred_element_type=f32, precision=precision
    )


def split_dot(matrix, values):
    upper = values.astype(bf16)
    lower = (values - upper.astype(f32)).astype(bf16)
    return dot(matrix, upper) + dot(matrix, lower)


def shift_columns(pad_ref, values, width):
    rows = values.shape[0]
    band = (pad_ref.shape[1] - rows) // 2
    column = stack_index(values.shape, 0) % width
    wide = values.astype(f32)
    for kx in range(3):
        moved = wide
        if kx == 0:
            moved = jnp.where(column == 0, 0.0, pltpu.roll(wide, 1, 0))
        if kx == 2:
            moved = jnp.where(column == width - 1, 0.0, pltpu.roll(wide, rows - 1, 0))
        zeros = jnp.zeros((band, values.shape[1]), pad_ref.dtype)
        pad_ref[kx, 0:band] = zeros
        pad_ref[kx, band : band + rows] = moved.astype(pad_ref.dtype)
        pad_ref[kx, band + rows :] = zeros
    return band


def conv_taps(pad_ref, band, first, rows, weight_ref, back=False, precision=None):
    channels = weight_ref.shape[0] // 9
    result = None
    for ky, kx in taps:
        part = pad_ref[kx, pl.ds(first + ky * band, rows)]
        tap = 8 - (3 * ky + kx) if back else 3 * ky + kx
        weight = weight_ref[tap * channels : (tap + 1) * channels, :].astype(pad_ref.dtype)
        term = dot(part, weight, "NT" if back else "NN", precision)
        result = term if result is None else result + term
    return result


def pool_matrix(out_rows, rows, factor, width, value, dtype=bf16):
    out, inner = stack_index((out_rows, rows), 0), stack_index((out_rows, rows), 1)
    band, small = SEG * width, width // factor
    out_band = SEG * small
    hit = (
        (out // out_band == inner // band // factor)
        & (out % out_band // small == inner % band // width)
        & (out % small == inner % width // factor)
    )
    return jnp.where(hit, value, 0.0).astype(dtype)


def spread_matrix(rows, factor, width):
    small = width // factor
    dims = (rows, SEG * small)
    out, inner = stack_index(dims, 0), stack_index(dims, 1)
    image, column = out % (SEG * width) // width, out % width
    hit = (inner // small == image) & (inner % small == column // factor)
    return jnp.where(hit, 1.0, 0.0).astype(bf16)


def as_row(block):
    return jnp.concatenate([block[j : j + 1] for j in range(block.shape[0])], 1)


def as_block(row):
    lanes_of = row.shape[1] // 128
    return jnp.concatenate([row[:, 128 * j : 128 * j + 128] for j in range(lanes_of)], 0)


def put_sums(out_ref, first, second, extra=None):
    block = jnp.concatenate([as_block(first), as_block(second)], 0)
    rows = out_ref.shape[1]
    if extra is not None:
        block = jnp.concatenate([block, extra], 0)
    if block.shape[0] < rows:
        block = jnp.concatenate([block, jnp.zeros((rows - block.shape[0], 128), f32)], 0)
    out_ref[...] = jnp.broadcast_to(block[None], out_ref.shape)


def get_sums(sums_ref, rows):
    block = jnp.sum(sums_ref[...], 0)
    return as_row(block[:rows]), as_row(block[rows : 2 * rows])


def norm_of(sums_ref, rows, count):
    first, second = get_sums(sums_ref, rows)
    mean = first / count
    return mean, lax.rsqrt(second / count - mean * mean + epsilon)


def silu(values):
    return values * jax.nn.sigmoid(values)


def column_sum(values):
    return jnp.sum(values, 0, keepdims=True)


def padded(rows, unit=16):
    return (rows + unit - 1) // unit * unit


def pack_kernel(place_ref, side_ref, one_ref, fine_ref, half_w_ref, quarter_w_ref, expand_ref,
                reduce_ref, two_ref, three_ref, sent_ref, parts_ref, early_ref):
    place, side = place_ref[0], side_ref[0]
    half = one_ref.shape[0] // 2
    part = early_ref.shape[0] // 2
    start = 0
    for part_ref in (fine_ref, half_w_ref, quarter_w_ref, reduce_ref):
        early_ref[start : start + part_ref.shape[0]] = part_ref[...]
        start += padded(part_ref.shape[0])
    for block in range(expand_ref.shape[1] // 128):
        lanes_of = slice(128 * block, 128 * block + 128)
        early_ref[start : start + expand_ref.shape[0]] = expand_ref[:, lanes_of]
        start += padded(expand_ref.shape[0])

    def put(start, value):
        shape = (sent_ref.shape[0],) + value.shape
        sent_ref[:, start : start + value.shape[0]] = jnp.broadcast_to(value[None], shape)
        return start + padded(value.shape[0])

    start = 0
    rows = pl.ds(pl.multiple_of(side * half, half), half)
    for block in range(one_ref.shape[1] // 128):
        start = put(start, one_ref[rows, 128 * block : 128 * block + 128])
    put(start, early_ref[pl.ds(pl.multiple_of(side * part, part), part)])
    wide = three_ref.shape[1] // 4
    columns = pl.ds(pl.multiple_of(place * 128, 128), 128)
    parts_ref[0 : two_ref.shape[0]] = two_ref[:, columns]
    start = padded(two_ref.shape[0])
    for block in range(wide // 128):
        columns = pl.ds(pl.multiple_of(place * wide + 128 * block, 128), 128)
        parts_ref[start : start + three_ref.shape[0]] = three_ref[:, columns]
        start += padded(three_ref.shape[0])


def own_lanes(place_ref, *refs):
    wide = refs[0].shape[1] // 4
    return [ref[:, pl.ds(pl.multiple_of(place_ref[0] * wide, wide), wide)] for ref in refs]


def first_kernel(side_ref, x_ref, mine_ref, other_ref, stem_ref,
                 full_ref, first_ref, sums_ref):
    side = side_ref[0]
    half = full_ref.shape[2]
    for part in range(full_ref.shape[3] // 128):
        rows, lanes_of = slice(half * part, half * part + half), slice(128 * part, 128 * part + 128)
        full_ref[:, pl.ds(side, 1), :, lanes_of] = mine_ref[:, rows][:, None]
        full_ref[:, pl.ds(1 - side, 1), :, lanes_of] = other_ref[:, rows][:, None]
    weight = full_ref[...].reshape(x_ref.shape[1], -1)
    first = dot(x_ref[...], weight)
    first_ref[...] = first
    put_sums(sums_ref, column_sum(first), column_sum(first * first), stem_row(stem_ref))


def stem_row(*refs):
    stem = sum(ref[...] for ref in refs).reshape(128, 128)
    return dot(jnp.ones((8, 128), f32), stem, "NT", lax.Precision.HIGHEST)


def hidden_kernel(count, mask_ref, sums_ref, first_ref, gain_ref, bias_ref, reduce_ref,
                  hidden_ref, change_ref, norm_ref):
    mean, inverse = norm_of(sums_ref, 4, count)
    norm_ref[...] = jnp.concatenate([mean, inverse], 0)
    level = (first_ref[...] - mean) * inverse * gain_ref[...] + bias_ref[...]
    hidden = silu(level).astype(bf16)
    hidden_ref[...] = hidden
    reduced = dot(hidden, reduce_ref[...])
    reduced = reduced.reshape(-1, SEG, 8, reduced.shape[1])
    steps = [
        mask_ref[0, t].astype(f32) * (reduced[:, t + 1] - reduced[:, t]) for t in range(SEG - 1)
    ]
    steps.append(jnp.zeros_like(steps[0]))
    change_ref[...] = jnp.stack(steps, 1).reshape(change_ref.shape).astype(bf16)


def gate_kernel(place_ref, change_ref, hidden_ref, fine_ref, half_w_ref, quarter_w_ref, expand_ref,
                gated_ref, sigmoid_ref, merged_ref, half_ref, quarter_ref,
                pad_ref, pad_half_ref, pad_quarter_ref):
    place = place_ref[0]
    change = change_ref[...]
    own = gated_ref.shape[0]
    band = shift_columns(pad_ref, change, 8)
    first = pl.multiple_of(place * own, own)
    fine = conv_taps(pad_ref, band, first, own, fine_ref)
    half = dot(pool_matrix(own, 4 * own, 2, 8, 0.25), change).astype(bf16)
    half_ref[...] = half
    band = shift_columns(pad_half_ref, half, 4)
    coarse = conv_taps(pad_half_ref, band, pl.multiple_of(place * 32, 32), 32, half_w_ref)
    quarter = dot(pool_matrix(own // 4, own, 2, 4, 0.25), half)
    quarter_ref[...] = quarter
    band = shift_columns(pad_quarter_ref, quarter, 2)
    coarsest = conv_taps(
        pad_quarter_ref, band, pl.multiple_of(place // 2 * 16, 16), 16, quarter_w_ref,
        precision=lax.Precision.HIGHEST,
    )
    merged = (
        fine
        + split_dot(spread_matrix(own, 2, 8), coarse)
        + split_dot(spread_matrix(own, 4, 8), coarsest)
    ).astype(bf16)
    merged_ref[...] = merged
    sigmoid = jax.nn.sigmoid(dot(merged, expand_ref[...]))
    sigmoid_ref[...] = sigmoid
    gated_ref[...] = (hidden_ref[...].astype(f32) * (1.0 + sigmoid)).astype(bf16)


def second_kernel(two_rows, gated_ref, packed_ref, second_ref, weight_ref, sums_ref, pad_ref):
    for clip in range(packed_ref.shape[0]):
        weight_ref[two_rows * clip : two_rows * clip + two_rows] = packed_ref[clip, :two_rows]
    band = shift_columns(pad_ref, gated_ref[...], 8)
    second = conv_taps(pad_ref, band, 0, second_ref.shape[0], weight_ref)
    second_ref[...] = second
    put_sums(sums_ref, column_sum(second), column_sum(second * second))


def hidden_two_kernel(count, place_ref, sums_ref, second_ref, gain_ref, bias_ref, hidden_ref, norm_ref):
    mean, inverse = norm_of(sums_ref, 1, count)
    norm_ref[...] = jnp.concatenate([mean, inverse], 0)
    gain, bias = own_lanes(place_ref, gain_ref, bias_ref)
    level = (second_ref[...] - mean) * inverse * gain + bias
    hidden_ref[...] = silu(level).astype(bf16)


def third_kernel(two_rows, three_rows, hidden_ref, packed_ref, third_ref, weight_ref, sums_ref):
    start = padded(two_rows)
    for block in range(weight_ref.shape[1] // 128):
        for clip in range(packed_ref.shape[0]):
            weight_ref[
                three_rows * clip : three_rows * clip + three_rows, 128 * block : 128 * block + 128
            ] = packed_ref[clip, start : start + three_rows]
        start += padded(three_rows)
    third = None
    for part in range(hidden_ref.shape[0]):
        term = dot(hidden_ref[part], weight_ref[128 * part : 128 * part + 128, :])
        third = term if third is None else third + term
    third_ref[...] = third
    put_sums(sums_ref, column_sum(third), column_sum(third * third))


def sources(place, size):
    return [place ^ s for s in range(size)]


def output_kernel(count, place_ref, sums_ref, third_ref, gain_ref, bias_ref,
                  x0_ref, x1_ref, x2_ref, x3_ref, c0_ref, c1_ref, c2_ref, c3_ref,
                  s0_ref, s1_ref, s2_ref, s3_ref, slope_ref, norm_ref,
                  out_sums_ref):
    place = place_ref[0]
    mean, inverse = norm_of(sums_ref, 4, count)
    norm_ref[...] = jnp.concatenate([mean, inverse], 0)
    gain, bias = own_lanes(place_ref, gain_ref, bias_ref)
    own, wide = x0_ref.shape[0], third_ref.shape[1]
    lanes_r = pl.ds(pl.multiple_of(place * wide, wide), wide)
    total_bias, total_gain = jnp.zeros((1, wide), f32), jnp.zeros((1, wide), f32)
    pieces = zip(
        sources(place, 4),
        (x0_ref, x1_ref, x2_ref, x3_ref),
        (c0_ref, c1_ref, c2_ref, c3_ref),
        (s0_ref, s1_ref, s2_ref, s3_ref),
    )
    for source, x_ref, c_ref, send_ref in pieces:
        rows = pl.ds(pl.multiple_of(source * own, own), own)
        normed = (third_ref[rows] - mean) * inverse
        summed = normed * gain + bias + x_ref[:, lanes_r].astype(f32)
        sigmoid = jax.nn.sigmoid(summed)
        send_ref[0] = (summed * sigmoid).astype(bf16)
        slope = c_ref[...].astype(f32) * (sigmoid * (1.0 + summed * (1.0 - sigmoid)))
        slope_ref[rows] = slope
        send_ref[1] = slope.astype(bf16)
        total_bias += column_sum(slope)
        total_gain += column_sum(slope * normed)
    put_sums(out_sums_ref, total_bias, total_gain)


def third_back_kernel(count, place_ref, sums_ref, third_ref, slope_ref, norm_ref, gain_ref, weight_ref,
                      grad_ref, part_ref, vectors_ref):
    total_bias, total_gain = get_sums(sums_ref, 4)
    vectors_ref[...] = jnp.concatenate([as_block(total_bias), as_block(total_gain)], 0)
    mean, inverse = norm_ref[0:1], norm_ref[1:2]
    normed = (third_ref[...] - mean) * inverse
    grad = own_lanes(place_ref, gain_ref)[0] * inverse * (
        slope_ref[...] - total_bias / count - normed * (total_gain / count)
    )
    grad = grad.astype(bf16)
    grad_ref[...] = grad
    back = dot(grad, weight_ref[...], "NT").astype(bf16)
    for part in range(part_ref.shape[0]):
        part_ref[part] = back[:, 128 * part : 128 * part + 128]


def second_slope_kernel(place_ref, part_ref, second_ref, norm_ref, gain_ref, bias_ref,
                        low_ref, high_ref, grad_ref, sums_ref):
    back = jnp.sum(part_ref[...].astype(f32), 0)
    normed = (second_ref[...] - norm_ref[0:1]) * norm_ref[1:2]
    gain, bias = own_lanes(place_ref, gain_ref, bias_ref)
    grad = back * silu_slope(normed * gain + bias)
    grad_ref[...] = grad
    stem = stem_row(low_ref, high_ref)[0:1]
    put_sums(sums_ref, column_sum(grad), column_sum(grad * normed), stem)


def second_back_kernel(count, place_ref, sums_ref, slope_ref, second_ref, norm_ref, gain_ref, weight_ref,
                       grad_ref, part_ref, vectors_ref, stem_ref, pad_ref):
    total_bias, total_gain = get_sums(sums_ref, 1)
    rest, stem = jnp.sum(sums_ref[...], 0)[2:3], []
    for _ in range(2):
        stem.append(rest.astype(bf16).astype(f32))
        rest = rest - stem[-1]
    order = stack_index((16, 128), 0)
    stem = jnp.where(order == 0, stem[0], jnp.where(order == 1, stem[1], rest))
    stem_ref[...] = jnp.where(order < 3, stem, 0.0).astype(bf16)
    vectors_ref[...] = jnp.concatenate([total_bias, total_gain], 0)
    inverse = norm_ref[1:2]
    normed = (second_ref[...] - norm_ref[0:1]) * inverse
    grad = own_lanes(place_ref, gain_ref)[0] * inverse * (
        slope_ref[...] - total_bias / count - normed * (total_gain / count)
    )
    grad = grad.astype(bf16)
    grad_ref[...] = grad
    band = shift_columns(pad_ref, grad, 8)
    own = part_ref.shape[1]
    for part in range(part_ref.shape[0]):
        back = conv_taps(pad_ref, band, part * own, own, weight_ref, True)
        part_ref[part] = back.astype(bf16)


def wide_grads_kernel(gated_ref, grad_ref, hidden_ref, third_ref, out_ref, pad_ref, all_ref):
    band = shift_columns(pad_ref, gated_ref[...], 8)
    rows, channels = gated_ref.shape
    clips = out_ref.shape[0]
    two_rows = 9 * channels // clips
    for ky, kx in taps:
        tap = 3 * ky + kx
        all_ref[tap * channels : (tap + 1) * channels, :] = dot(
            pad_ref[kx, ky * band : ky * band + rows], grad_ref[...], "TN"
        ).astype(bf16)
    start = 9 * channels
    for part in range(hidden_ref.shape[0]):
        value = dot(hidden_ref[part], third_ref[...], "TN").astype(bf16)
        for block in range(value.shape[1] // 128):
            first = start + channels * block + 128 * part
            all_ref[first : first + 128] = value[:, 128 * block : 128 * block + 128]
    three_rows = channels // clips

    for clip in range(clips):
        out_ref[clip, 0:two_rows] = all_ref[two_rows * clip : two_rows * clip + two_rows]
        at = padded(two_rows)
        for block in range(third_ref.shape[1] // 128):
            first = start + channels * block + three_rows * clip
            out_ref[clip, at : at + three_rows] = all_ref[first : first + three_rows]
            at += padded(three_rows)


def last_kernel(sum_ref, three_ref, two_ref, out_ref):
    rows = sum_ref.shape[0]
    out_ref[0:rows] = sum_ref[...]
    vectors = jnp.concatenate([three_ref[...], two_ref[...], jnp.zeros((6, 128), f32)], 0)
    upper = vectors.astype(bf16)
    out_ref[rows : rows + 16] = upper
    out_ref[rows + 16 : rows + 32] = (vectors - upper.astype(f32)).astype(bf16)


def gate_back_kernel(part_ref, hidden_ref, sigmoid_ref, expand_ref, stem_ref,
                     fine_ref, gate_ref, hidden_grad_ref):
    gated = jnp.sum(part_ref[...].astype(f32), 0)
    sigmoid = sigmoid_ref[...]
    gate = (gated * hidden_ref[...].astype(f32) * sigmoid * (1.0 - sigmoid)).astype(bf16)
    gate_ref[...] = gate
    hidden_grad_ref[...] = gated * (1.0 + sigmoid)
    rows = gate.shape[0]
    fine_ref[:rows] = dot(gate, expand_ref[...], "NT").astype(bf16)
    fine_ref[rows:] = stem_ref[...]


def reduce_back_kernel(place_ref, mask_ref, grad_ref, fine_ref, half_w_ref, quarter_w_ref,
                       reduce_ref, hidden_grad_ref, first_ref, norm_ref, gain_ref, bias_ref,
                       reduced_ref, slope_ref, coarse_ref, coarsest_ref, stem_ref, sums_ref,
                       pad_ref, pad_half_ref, pad_quarter_ref):
    place = place_ref[0]
    own = reduced_ref.shape[0]
    grad_fine = grad_ref[:, :own].reshape(4 * own, grad_ref.shape[2])
    stem = jnp.sum(grad_ref[:, own:].astype(f32), 0)
    stem_ref[...] = jnp.broadcast_to(stem[0:1] + stem[1:2] + stem[2:3], stem_ref.shape)
    coarse = dot(pool_matrix(own, 4 * own, 2, 8, 1.0), grad_fine).astype(bf16)
    coarse_ref[...] = coarse
    coarsest = dot(pool_matrix(own // 4, 4 * own, 4, 8, 1.0), grad_fine)
    coarsest_ref[...] = coarsest
    band = shift_columns(pad_quarter_ref, coarsest, 2)
    low = conv_taps(
        pad_quarter_ref, band, pl.multiple_of(place // 2 * 16, 16), 16, quarter_w_ref, True,
        lax.Precision.HIGHEST,
    )
    band = shift_columns(pad_half_ref, coarse, 4)
    middle = conv_taps(pad_half_ref, band, pl.multiple_of(place * 32, 32), 32, half_w_ref, True)
    middle = middle + 0.25 * split_dot(spread_matrix(32, 2, 4), low)
    band = shift_columns(pad_ref, grad_fine, 8)
    change = conv_taps(pad_ref, band, pl.multiple_of(place * own, own), own, fine_ref, True)
    change = change + 0.25 * split_dot(spread_matrix(own, 2, 8), middle)
    change = change.reshape(-1, SEG, 8, change.shape[1])
    carried = [mask_ref[0, t].astype(f32) * change[:, t] for t in range(SEG - 1)]
    zero = jnp.zeros_like(carried[0])
    before, here = [zero] + carried, carried + [zero]
    reduced = jnp.stack([b - h for b, h in zip(before, here)], 1)
    reduced = reduced.reshape(reduced_ref.shape).astype(bf16)
    reduced_ref[...] = reduced
    grad_hidden = hidden_grad_ref[...] + dot(reduced, reduce_ref[...], "NT")
    normed = (first_ref[...] - norm_ref[0:1]) * norm_ref[1:2]
    slope = grad_hidden * silu_slope(normed * gain_ref[...] + bias_ref[...])
    slope_ref[...] = slope
    put_sums(sums_ref, column_sum(slope), column_sum(slope * normed))


def first_back_kernel(count, sums_ref, slope_ref, first_ref, norm_ref, gain_ref,
                      grad_ref, vectors_ref):
    total_bias, total_gain = get_sums(sums_ref, 4)
    vectors_ref[...] = jnp.concatenate([total_bias, total_gain], 0)
    inverse = norm_ref[1:2]
    normed = (first_ref[...] - norm_ref[0:1]) * inverse
    grad = gain_ref[...] * inverse * (
        slope_ref[...] - total_bias / count - normed * (total_gain / count)
    )
    grad_ref[...] = grad.astype(bf16)


def one_grad_kernel(place_ref, grad_ref, x0_ref, x1_ref, x2_ref, x3_ref, out_ref):
    place = place_ref[0]
    lanes_r = pl.ds(pl.multiple_of(place * 128, 128), 128)
    total = None
    for source, x_ref in zip(sources(place, 4), (x0_ref, x1_ref, x2_ref, x3_ref)):
        grad = grad_ref[pl.ds(source, 1), :, lanes_r][0]
        term = dot(x_ref[...], grad, "TN")
        total = term if total is None else total + term
    out_ref[...] = total.astype(bf16)


def small_grads_kernel(place_ref, change_ref, half_ref, quarter_ref, grad_ref, coarse_ref,
                       coarsest_ref, hidden_ref, reduced_ref, merged_ref, gate_ref,
                       out_ref,
                       pad_ref, pad_half_ref, pad_quarter_ref, grads_ref, shares_ref):
    place = place_ref[0]
    clips, part = out_ref.shape[0], shares_ref.shape[1] // 4
    own = hidden_ref.shape[0]
    grad_fine = grad_ref[:, :own].reshape(4 * own, grad_ref.shape[2])
    scales = (
        (change_ref, grad_fine, pad_ref, 8, None),
        (half_ref, coarse_ref[...], pad_half_ref, 4, None),
        (quarter_ref, coarsest_ref[...], pad_quarter_ref, 2, lax.Precision.HIGHEST),
    )
    at = 0
    for map_ref, cotangent, padded_ref, width, precision in scales:
        rows, channels = map_ref.shape
        band = shift_columns(padded_ref, map_ref[...], width)
        for ky, kx in taps:
            tap = 3 * ky + kx
            grads_ref[tap * channels : (tap + 1) * channels, :] = dot(
                padded_ref[kx, ky * band : ky * band + rows], cotangent, "TN", precision
            ).astype(bf16)
        share = 9 * channels // clips
        for clip in range(clips):
            shares_ref[clip, :share] = grads_ref[share * clip : share * clip + share]
        out_ref[:, at : at + part] = shares_ref[:, pl.ds(pl.multiple_of(place * part, part), part)]
        at += part
    value = dot(hidden_ref[...], reduced_ref[...], "TN").astype(bf16)
    expand = dot(merged_ref[...], gate_ref[...], "TN").astype(bf16)
    blocks = [value] + [
        expand[:, first : first + 128] for first in range(0, expand.shape[1], 128)
    ]
    for block in blocks:
        share = block.shape[0] // clips
        for clip in range(clips):
            out_ref[clip, at : at + share] = block[share * clip : share * clip + share]
        at += padded(share)


def join_kernel(grad_ref, low_ref, high_ref, out_ref):
    clips, rows = out_ref.shape[0], grad_ref.shape[0] // out_ref.shape[0]
    stem = low_ref[...] + high_ref[...]
    share = stem.shape[1] // clips
    for clip in range(clips):
        out_ref[clip, :rows] = grad_ref[rows * clip : rows * clip + rows]
        pieces = [stem[k, share * clip : share * clip + share] for k in range(stem.shape[0])]
        value = jnp.concatenate(pieces, 0).astype(bf16)
        out_ref[clip, rows : rows + value.shape[0]] = value


def input_grad_kernel(place_ref, grad_ref, weight_ref, r0_ref, r1_ref, r2_ref, r3_ref,
                      input_ref, out_ref):
    place = place_ref[0]
    wide = r0_ref.shape[2]
    for source, r_ref in zip(sources(place, 4), (r0_ref, r1_ref, r2_ref, r3_ref)):
        lanes_r = pl.ds(pl.multiple_of(source * wide, wide), wide)
        weight = weight_ref[pl.ds(pl.multiple_of(source * wide, wide), wide), :]
        value = dot(grad_ref[...], weight, "NT") + r_ref[1].astype(f32)
        shape = (input_ref.shape[1], input_ref.shape[0], input_ref.shape[2], wide)
        value, result = value.reshape(shape), r_ref[0].astype(f32).reshape(shape)
        for row in range(shape[0]):
            input_ref[:, row, :, lanes_r] = value[row]
            out_ref[:, row, :, lanes_r] = result[row].astype(bf16)


def by_source(place, refs):
    pieces = [ref[...].astype(f32) for ref in refs]
    low, high = (place & 1) == 0, (place & 2) == 0
    pairs = []
    for first, second in ((pieces[0], pieces[1]), (pieces[2], pieces[3])):
        pairs.append((jnp.where(low, first, second), jnp.where(low, second, first)))
    near, far = pairs
    return [jnp.where(high, near[k], far[k]) for k in range(2)] + [
        jnp.where(high, far[k], near[k]) for k in range(2)
    ]


def wide_shares_kernel(place_ref, *refs):
    pieces = by_source(place_ref[0], refs[:4])
    two_ref, three_ref, gain_two_ref, bias_two_ref, gain_three_ref, bias_three_ref = refs[4:]
    two_rows, three_rows = two_ref.shape[0], three_ref.shape[0]
    blocks = three_ref.shape[1] // 512
    vectors_at = padded(two_rows) + blocks * padded(three_rows)
    for source, piece in enumerate(pieces):
        lanes_of = slice(128 * source, 128 * source + 128)
        two_ref[:, lanes_of] = piece[:two_rows]
        vectors = piece[vectors_at : vectors_at + 16] + piece[vectors_at + 16 : vectors_at + 32]
        bias_two_ref[:, lanes_of], gain_two_ref[:, lanes_of] = vectors[8:9], vectors[9:10]
        for block in range(blocks):
            start = padded(two_rows) + block * padded(three_rows)
            first = 128 * (blocks * source + block)
            three_ref[:, first : first + 128] = piece[start : start + three_rows]
            bias_three_ref[:, first : first + 128] = vectors[block : block + 1]
            gain_three_ref[:, first : first + 128] = vectors[4 + block : 5 + block]


def one_share_kernel(place_ref, *refs):
    pieces = by_source(place_ref[0], refs[:4])
    one_ref, stem_ref = refs[4:]
    at, share = one_ref.shape[0], stem_ref.shape[0]
    for source, piece in enumerate(pieces):
        one_ref[:, 128 * source : 128 * source + 128] = piece[:at]
    total = pieces[0] + pieces[1] + pieces[2] + pieces[3]
    for block in range(stem_ref.shape[1] // 128):
        first = at + share * block
        stem_ref[:, 128 * block : 128 * block + 128] = total[first : first + share]


def rest_shares_kernel(tap_rows, place_ref, *refs):
    pieces = by_source(place_ref[0], refs[:4])
    fine_ref, half_w_ref, quarter_w_ref, reduce_ref, expand_ref = refs[4:]
    start = 0
    for out_ref in (fine_ref, half_w_ref, quarter_w_ref):
        rows = [piece[start : start + tap_rows] for piece in pieces]
        out_ref[...] = jnp.concatenate(rows, 0)[: out_ref.shape[0]]
        start += tap_rows
    total = pieces[0] + pieces[1] + pieces[2] + pieces[3]
    for out_ref in (reduce_ref, expand_ref):
        rows = out_ref.shape[0]
        for first in range(0, out_ref.shape[1], 128):
            out_ref[:, first : first + 128] = total[start : start + rows]
            start += padded(rows)


class Fresh:
    def __init__(self, array):
        self.array = array


def call(kernel, scalars, arrays, outs, scratch=(), waits=(), flops=10**9, moved=2 * 10**6):
    used = len(scalars) + len(arrays)

    def body(*refs):
        kernel(*refs[:used], *refs[used + len(waits) :])

    shapes = [(entry.array if isinstance(entry, Fresh) else entry).shape for entry in arrays]
    return pl.pallas_call(
        body,
        grid=(1,),
        in_specs=[pl.BlockSpec(memory_space=pltpu.SMEM)] * len(scalars)
        + [whole(shape) for shape in shapes]
        + [pl.BlockSpec(memory_space=pl.ANY)] * len(waits),
        out_specs=[whole(shape) for shape, _ in outs],
        out_shape=[pltpu.HBM(shape, dtype) for shape, dtype in outs],
        scratch_shapes=[pltpu.VMEM(shape, dtype) for shape, dtype in scratch],
        compiler_params=pltpu.CompilerParams(vmem_limit_bytes=block_limit),
        cost_estimate=pl.CostEstimate(flops=flops, bytes_accessed=moved, transcendentals=0),
    )(
        *scalars,
        *(entry.array if isinstance(entry, Fresh) else in_hbm(entry) for entry in arrays),
        *waits,
    )


def together(*values):
    return lax.optimization_barrier(values)


def exchange(blocks, axis):
    return lax.all_to_all(blocks, axis, 0, 0)


def to_all(part, axis):
    size = lax.axis_size(axis)
    return exchange(jnp.broadcast_to(part[None], (size,) + part.shape), axis)


def swap(piece, axis, step):
    return lax.ppermute(piece, axis, [(i, i ^ step) for i in range(lax.axis_size(axis))])


def lane_blocks(array):
    return [array[:, start : start + 128] for start in range(0, array.shape[1], 128)]


def pick(array, index, axis=0):
    return lax.dynamic_index_in_dim(array, index, axis, keepdims=False)


def per_device(
    frames,
    frame_start,
    boundary_mask,
    stem_weight,
    stem_gain,
    stem_bias,
    block_input,
    w_one,
    w_reduce,
    k_fine,
    k_half,
    k_quarter,
    w_expand,
    w_two,
    w_three,
    gain_one,
    bias_one,
    gain_two,
    bias_two,
    gain_three,
    bias_three,
    stem_cot,
    block_cot,
):
    nc, nr = lax.axis_size("clip"), lax.axis_size("row")
    u32 = jnp.uint32
    place = lax.axis_index("row").astype(u32)
    spots = [place ^ u32(s) for s in range(nr)]
    side = place & u32(1)
    spot = place.astype(jnp.int32).reshape(1)
    both = ("clip", "row")
    images, block_rows, cols, c_in = block_input.shape
    mid, red = gain_one.shape[0], w_reduce.shape[1]
    mid_r, in_r = mid // nr, c_in // nr
    own = images * block_rows * cols
    pixels = own * nr
    count = float(pixels * nc)
    clip_sums = ((nc, 8, 128), f32)
    both_sums = ((nc * nr, 16, 128), f32)

    def in_part(array, index):
        return lax.dynamic_slice_in_dim(array, index * u32(in_r), in_r, array.ndim - 1)

    half = w_one.shape[0] // 2
    expand_rows = padded(w_expand.shape[0])
    early_rows = padded(
        3 * padded(k_fine.shape[0]) + padded(w_reduce.shape[0]) + mid // 128 * expand_rows, 32
    )
    edges = [4 * padded(half)]
    edges.append(edges[0] + early_rows // 2)
    two_rows, three_rows = w_two.shape[0], w_three.shape[0]
    two_end = padded(two_rows)
    part_rows = two_end + in_r // 128 * padded(three_rows)
    sent, parts = call(
        pack_kernel,
        (spot, side.astype(jnp.int32).reshape(1)),
        (w_one, k_fine, k_half, k_quarter, w_expand, w_reduce, w_two, w_three),
        (((nc, edges[-1], 128), bf16), ((part_rows, 128), bf16)),
        [((early_rows, 128), bf16)],
        [entry.reshape(1) for entry in spots],
    )
    taps_own, sent = together(filters_inside(stem_weight), sent)
    stem_taps = to_all(taps_own, "clip").reshape(STEM, -1)
    sent, stem_taps = together(sent, stem_taps)
    mine = exchange(sent, "clip")
    filters = jnp.concatenate(
        [jnp.pad(stem_taps, ((0, 0), (224 * y, 672 - 224 * y))) for y in range(4)], 0
    )

    x_own = block_input.swapaxes(0, 1).reshape(own, c_in)
    cot_own = block_cot.swapaxes(0, 1).reshape(own, c_in)

    local = frames[0]
    rows = local.shape[2]
    above = lax.ppermute(local[:, :, rows - 16 :], "row", [(i, i + 1) for i in range(nr - 1)])
    below = lax.ppermute(local[:, :, :16], "row", [(i + 1, i) for i in range(nr - 1)])
    cot_own, x_own, above, below = together(cot_own, x_own, above, below)
    planes = stem_planes(frame_start[0], local, above, below)
    stem_count = float(SEG * (rows // 2) * (local.shape[3] // 2) * nc * nr)
    cot_pieces = [in_part(cot_own, place)] + [
        swap(in_part(cot_own, spots[s]), "row", s) for s in range(1, nr)
    ]
    x_pieces = [x_own, swap(x_own, "row", 1), swap(x_own, "row", 2)]
    x_pieces.append(swap(x_pieces[2], "row", 1))

    stem_pre, stem_sums = stem_conv(planes, filters, *x_pieces[1:3], *cot_pieces[1:])
    mine, stem_sums = together(mine, stem_sums)
    other = swap(mine, "row", 1)
    packed = lax.all_gather(parts, "clip")
    full_one, first, sums = call(
        first_kernel,
        (side.astype(jnp.int32).reshape(1),),
        (x_own, Fresh(mine), Fresh(other), stem_sums),
        (((nc, 2, half, mid), bf16), ((own, mid), f32), both_sums),
    )
    full_one = full_one.reshape(c_in, mid)
    sums = exchange(sums, both)
    mine, other, first = together(mine, other, first)
    halves = [entry[:, edges[0] : edges[1]] for entry in (mine, other)]
    quarters = jnp.concatenate(
        [
            jnp.where(side == u32(0), halves[0], halves[1]),
            jnp.where(side == u32(0), halves[1], halves[0]),
        ],
        1,
    )
    early_parts, start = [], 0
    sizes = (k_fine.shape[0],) * 3 + (w_reduce.shape[0],) + (w_expand.shape[0],) * (mid // 128)
    for size in sizes:
        early_parts.append(quarters[:, start : start + size].reshape(-1, 128))
        start += padded(size)
    full_fine, full_half, full_quarter, full_reduce = early_parts[:4]
    full_expand = jnp.concatenate(early_parts[4:], 1)
    stem_totals = jnp.sum(sums[:, 8], 0).reshape(2, STEM)
    stem_mean, stem_inverse = statistics(stem_totals, stem_count)
    stem_vectors = lanes(stem_mean, stem_inverse, stem_gain, stem_bias)
    gain_one, bias_one = gain_one.reshape(1, -1), bias_one.reshape(1, -1)
    hidden_one, change, norm_one = call(
        functools.partial(hidden_kernel, count),
        (boundary_mask,),
        (Fresh(sums), first, gain_one, bias_one, full_reduce),
        (((own, mid), bf16), ((own, red), bf16), ((2, mid), f32)),
    )
    change = lax.all_gather(change, "row").reshape(pixels, red)
    pads = [
        ((3, pixels + 2 * images * cols, red), bf16),
        ((3, pixels // 4 + images * cols, red), bf16),
        ((3, pixels // 16 + images * cols // 2, red), f32),
    ]
    gated, sigmoid, merged, half_map, quarter = call(
        gate_kernel,
        (spot,),
        (Fresh(change), hidden_one, full_fine, full_half, full_quarter, full_expand),
        (
            ((own, mid), bf16),
            ((own, mid), f32),
            ((own, red), bf16),
            ((pixels // 4, red), bf16),
            ((pixels // 16, red), f32),
        ),
        pads,
    )
    gated = lax.all_gather(gated, "row").reshape(pixels, mid)
    second, two_r, sums = call(
        functools.partial(second_kernel, two_rows),
        (),
        (Fresh(gated), packed),
        (((pixels, mid_r), f32), ((9 * mid, mid_r), bf16), clip_sums),
        [((3, pixels + 2 * images * cols, mid), bf16)],
    )
    gain_two, bias_two = gain_two.reshape(1, -1), bias_two.reshape(1, -1)
    outer_low, slope_low = stem_slope(stem_pre, stem_cot, 0, stem_vectors, second)
    hidden_two, norm_two = call(
        functools.partial(hidden_two_kernel, count),
        (spot,),
        (Fresh(exchange(sums, "clip")), second, gain_two, bias_two),
        (((pixels, mid_r), bf16), ((2, mid_r), f32)),
        waits=(slope_low,),
    )
    hidden_two = lax.all_gather(hidden_two, "row")
    third, three_r, sums = call(
        functools.partial(third_kernel, two_rows, three_rows),
        (),
        (Fresh(hidden_two), packed),
        (((pixels, in_r), f32), ((mid, in_r), bf16), clip_sums),
    )
    gain_three, bias_three = gain_three.reshape(1, -1), bias_three.reshape(1, -1)
    *send, slope_three, norm_three, sums = call(
        functools.partial(output_kernel, count),
        (spot,),
        (
            Fresh(exchange(sums, "clip")), third, gain_three, bias_three, *x_pieces, *cot_pieces,
        ),
        (
            *[((2, own, in_r), bf16)] * nr,
            ((pixels, in_r), f32),
            ((2, in_r), f32),
            clip_sums,
        ),
    )

    outer_high, slope_high = stem_slope(stem_pre, stem_cot, SEG // 2, stem_vectors, slope_three)
    grad_third, parts, vectors_three = call(
        functools.partial(third_back_kernel, count),
        (spot,),
        (
            Fresh(exchange(sums, "clip")), third, slope_three, norm_three, gain_three, three_r,
        ),
        (((pixels, in_r), bf16), ((nr, pixels, mid_r), bf16), ((8, 128), f32)),
        waits=(slope_high,),
    )
    slope_two, sums = call(
        second_slope_kernel,
        (spot,),
        (
            Fresh(exchange(parts, "row")), second, norm_two, gain_two, bias_two,
            slope_low, slope_high,
        ),
        (((pixels, mid_r), f32), clip_sums),
    )
    slope_two, *send = together(slope_two, *send)
    returned = [send[0]] + [swap(send[s], "row", s) for s in range(1, nr)]
    grad_second, parts, vectors_two, stem_part = call(
        functools.partial(second_back_kernel, count),
        (spot,),
        (
            Fresh(exchange(sums, "clip")), slope_two, second, norm_two, gain_two, two_r,
        ),
        (
            ((pixels, mid_r), bf16), ((nr, own, mid), bf16), ((2, mid_r), f32),
            ((16, 128), bf16),
        ),
        [((3, pixels + 2 * images * cols, mid_r), bf16)],
        returned[1:],
    )
    (wide,) = call(
        wide_grads_kernel,
        (),
        (gated, grad_second, hidden_two, grad_third),
        (((nc, part_rows, 128), bf16),),
        [
            ((3, pixels + 2 * images * cols, mid), bf16),
            ((9 * mid + mid * in_r // 128, 128), bf16),
        ],
    )
    wide_total = lax.psum_scatter(wide, "clip", scatter_dimension=0, tiled=False)
    grad_fine, grad_gate, grad_hidden = call(
        gate_back_kernel,
        (),
        (Fresh(exchange(parts, "row")), hidden_one, sigmoid, full_expand, stem_part),
        (((own + 16, red), bf16), ((own, mid), bf16), ((own, mid), f32)),
        waits=(wide,),
    )
    grad_fine = lax.all_gather(grad_fine, "row")
    grad_reduced, slope_one, grad_coarse, grad_coarsest, stem_totals, sums = call(
        reduce_back_kernel,
        (spot, boundary_mask),
        (
            Fresh(grad_fine), full_fine, full_half, full_quarter, full_reduce,
            grad_hidden, first, norm_one, gain_one, bias_one,
        ),
        (
            ((own, red), bf16),
            ((own, mid), f32),
            ((pixels // 4, red), bf16),
            ((pixels // 16, red), f32),
            ((8, 128), f32),
            both_sums,
        ),
        pads,
    )
    stem_bias_grad, stem_gain_grad = stem_totals[0].reshape(2, STEM)
    stem_vectors = lanes(
        stem_mean,
        stem_inverse,
        stem_gain * stem_inverse,
        stem_bias_grad / stem_count,
        stem_gain_grad / stem_count,
    )
    stem_low = stem_grad(planes, stem_pre, outer_low, 0, stem_vectors, slope_one)
    tap_rows = padded(padded(k_fine.shape[0], 4) // 4)
    rest_rows = 3 * tap_rows + padded(w_reduce.shape[0])
    rest_rows += mid // 128 * padded(w_expand.shape[0])
    (rest,) = call(
        small_grads_kernel,
        (spot,),
        (
            change, half_map, quarter, grad_fine, grad_coarse, grad_coarsest,
            hidden_one, grad_reduced, merged, grad_gate,
        ),
        (((nc, rest_rows, 128), bf16),),
        [*pads, ((9 * red, red), bf16), ((nc, 4 * tap_rows, 128), bf16)],
    )
    sums = exchange(sums, both)
    grad_first, vectors_one = call(
        functools.partial(first_back_kernel, count),
        (),
        (Fresh(sums), slope_one, first, norm_one, gain_one),
        (((own, mid), bf16), ((2, mid), f32)),
        waits=(rest, stem_low),
    )
    rest, grad_first = together(rest, grad_first)
    rest_total = jnp.sum(exchange(rest, "clip"), 0, dtype=f32).astype(bf16)
    (one_grad,) = call(
        one_grad_kernel,
        (spot,),
        (Fresh(lax.all_gather(grad_first, "row")), *x_pieces),
        (((c_in, mid_r), bf16),),
    )
    stem_high = stem_grad(planes, stem_pre, outer_high, len(planes) // 2, stem_vectors, one_grad)
    one_rows, stem_rows = c_in // nc, padded(8 * stem_weight.shape[0])
    (one_grad,) = call(
        join_kernel,
        (),
        (one_grad, stem_low, stem_high),
        (((nc, one_rows + stem_rows, 128), bf16),),
    )
    one_grad, rest_total = together(one_grad, rest_total)
    one_total = jnp.sum(exchange(one_grad, "clip"), 0, dtype=f32).astype(bf16)
    input_grad, block_out = call(
        input_grad_kernel,
        (spot,),
        (grad_first, full_one, *returned),
        ((block_input.shape, f32), (block_input.shape, bf16)),
    )

    (last,) = call(
        last_kernel,
        (),
        (Fresh(wide_total), vectors_three, vectors_two),
        (((part_rows + 32, 128), bf16),),
    )
    def from_row(piece):
        return [piece] + [Fresh(swap(piece, "row", s)) for s in range(1, nr)]

    wide_pieces = [last] + [swap(last, "row", s) for s in range(1, nr)]
    rest_shares = call(
        functools.partial(rest_shares_kernel, tap_rows),
        (spot,),
        from_row(rest_total),
        (
            *[(entry.shape, f32) for entry in (k_fine, k_half, k_quarter, w_reduce, w_expand)],
        ),
    )
    one_total, input_grad, *wide_pieces = together(one_total, input_grad, *wide_pieces)
    two_share, three_share, gain_two, bias_two, gain_three, bias_three = call(
        wide_shares_kernel,
        (spot,),
        [wide_pieces[0], *[Fresh(piece) for piece in wide_pieces[1:]]],
        (
            ((two_rows, mid), f32), ((three_rows, c_in), f32),
            ((1, mid), f32), ((1, mid), f32), ((1, c_in), f32), ((1, c_in), f32),
        ),
    )
    one_share, stem_share = call(
        one_share_kernel,
        (spot,),
        from_row(one_total),
        (((one_rows, mid), f32), ((stem_weight.shape[0], 1024), f32)),
    )
    return (
        block_out,
        input_grad,
        filters_outside(stem_share[:, :784]),
        stem_gain_grad,
        stem_bias_grad,
        one_share,
        rest_shares[3],
        *rest_shares[:3],
        rest_shares[4],
        two_share,
        three_share,
        vectors_one[1],
        vectors_one[0],
        gain_two[0],
        bias_two[0],
        gain_three[0],
        bias_three[0],
    )


def solution(mesh):
    in_specs = (
        P("clip", None, None, "row", None),
        P("clip", None),
        P("clip", None),
        P("clip", None),
        P(),
        P(),
        P("clip", "row", None, None),
        P("clip", None),
        P("clip", None),
        P("clip", None),
        P("clip", None),
        P("clip", None),
        P("clip", None),
        P("clip", None),
        P("clip", None),
        P(),
        P(),
        P(),
        P(),
        P(),
        P(),
        P("clip", None, "row", None),
        P("clip", "row", None, None),
    )
    out_specs = (
        P("clip", "row", None, None),
        P("clip", "row", None, None),
        P("clip", None),
        P(),
        P(),
        P("clip", None),
        P("clip", None),
        P("clip", None),
        P("clip", None),
        P("clip", None),
        P("clip", None),
        P("clip", None),
        P("clip", None),
        P(),
        P(),
        P(),
        P(),
        P(),
        P(),
    )
    return jax.shard_map(
        per_device, mesh=mesh, in_specs=in_specs, out_specs=out_specs, check_vma=False
    )
```
